128 devices in a mesh: fsdp: 16 (over z_hi, y, core), seq: 8 (over z_lo, x).
Axes of the slice: x: 4, y: 4, z: 4 (z_hi: 2, z_lo: 2; z = z_hi * 2 + z_lo), core: 2. Of those that a mesh axis runs over, the one named last changes fastest.
Arguments:
- tokens: bfloat16 [32768, 768], P(('fsdp', 'seq')), may hold values from -6 to 6
- lengths: int32 [16, 3], P('fsdp'), may hold values from 1 to 13, 16 in all within a row
- block_table: int32 [16, 16], P('fsdp'), may hold values from 0 to 15, each once within a row
- qkv_weight: bfloat16 [768, 2304], P(('fsdp', 'seq')), may hold values from -0.21875 to 0.21875
- query_bias: bfloat16 [768], P(('fsdp', 'seq')), may hold values from -3 to 3
- value_bias: bfloat16 [768], P(('fsdp', 'seq')), may hold values from -0.1796875 to 0.1796875
- out_weight: bfloat16 [768, 768], P(('fsdp', 'seq')), may hold values from -3 to 3
- out_bias: bfloat16 [768], P(('fsdp', 'seq')), may hold values from -2 to 2
- first_gain: bfloat16 [768], P(('fsdp', 'seq')), may hold values from 0.5 to 1.5
- first_shift: bfloat16 [768], P(('fsdp', 'seq')), may hold values from -2 to 2
- up_weight: bfloat16 [768, 3072], P(('fsdp', 'seq')), may hold values from -0.21875 to 0.21875
- up_bias: bfloat16 [3072], P(('fsdp', 'seq')), may hold values from -2 to 2
- down_weight: bfloat16 [3072, 768], P(('fsdp', 'seq')), may hold values from -0.109375 to 0.109375
- down_bias: bfloat16 [768], P(('fsdp', 'seq')), may hold values from -2 to 2
- second_gain: bfloat16 [768], P(('fsdp', 'seq')), may hold values from 0.5 to 1.5
- second_shift: bfloat16 [768], P(('fsdp', 'seq')), may hold values from -2 to 2
- cotangent: bfloat16 [32768, 768], P(('fsdp', 'seq')), may hold values from -6 to 6
Outputs:
- layer_out: bfloat16 [32768, 768], P(('fsdp', 'seq'))
- tokens_grad: float32 [32768, 768], P(('fsdp', 'seq'))
- qkv_weight_grad: float32 [768, 2304], P(('fsdp', 'seq'))
- query_bias_grad: float32 [768], P(('fsdp', 'seq'))
- value_bias_grad: float32 [768], P(('fsdp', 'seq'))
- out_weight_grad: float32 [768, 768], P(('fsdp', 'seq'))
- out_bias_grad: float32 [768], P(('fsdp', 'seq'))
- first_gain_grad: float32 [768], P(('fsdp', 'seq'))
- first_shift_grad: float32 [768], P(('fsdp', 'seq'))
- up_weight_grad: float32 [768, 3072], P(('fsdp', 'seq'))
- up_bias_grad: float32 [3072], P(('fsdp', 'seq'))
- down_weight_grad: float32 [3072, 768], P(('fsdp', 'seq'))
- down_bias_grad: float32 [768], P(('fsdp', 'seq'))
- second_gain_grad: float32 [768], P(('fsdp', 'seq'))
- second_shift_grad: float32 [768], P(('fsdp', 'seq'))
The draws below stay inside these ranges and needn't reach their ends.
Inputs may be any that keep to these rules, and one draw needn't show every extreme that they name: `lengths`: each row sums to 16, and one entry of it is exactly 13. `block_table`: each row is a permutation of 0 to 15.
All inputs are finite; a program needn't handle non-finite values.
Results may differ from the reference program's by a relative error of at most 0.023.
Values may be sent and summed in bfloat16 or wider, within the bound.
A program may use at most 128 MiB of HBM per device.

```python
import math
import jax
import jax.numpy as jnp
import numpy as np
from jax import lax

D = 768
H = 12
HD = 64
FF = 3072
BLK = 128
SEQS = 3
NB = 16
GROUPS = 16
GT = 2048
TOKENS = 32768


def shard_levels(own_key, extent, pieces, least, top_value):
    level, own = 1.0, jax.random.fold_in(own_key, 6)
    for axis_at, blocks in pieces:
        draws = jnp.exp(jax.random.uniform(jax.random.fold_in(own, axis_at), (blocks,), jnp.float32, least / len(pieces), top_value / len(pieces)))
        level = level * jnp.repeat(draws, extent[axis_at] // blocks).reshape([-1 if axis == axis_at else 1 for axis in range(len(extent))])
    return level


def length_profile(count, total, most, lean):
    portions = [(1 << 20) // math.isqrt(rank ** lean) + 1 for rank in range(2, count + 1)]
    surplus, counts = total - most - (count - 1), [1] * (count - 1)
    while surplus > 0:
        free = [i for i in range(count - 1) if counts[i] < most]
        whole, budget = sum([portions[i] for i in free]), surplus
        for i in free:
            extra = min(most - counts[i], max(1, budget * portions[i] // whole), surplus)
            counts[i] = counts[i] + extra
            surplus = surplus - extra
    return np.array([most] + counts)


def uneven(stream_key, count, total, bound, skew):
    if count == 2:
        one = jax.random.randint(stream_key, (), max(1, total - bound), min(bound, total - 1) + 1)
        return jnp.stack([one, total - one])
    sizes = jnp.asarray(length_profile(count, total, bound, skew), jnp.int32)
    pairs = (count - 1) // 2
    source_of, sink = sizes[1:1 + 2 * pairs:2], sizes[2:2 + 2 * pairs:2]
    margin = jnp.minimum(source_of - 1, bound - sink)
    shifted = jax.random.randint(jax.random.fold_in(stream_key, 1), (pairs,), 0, 1 << 20) % (margin + 1)
    sizes = sizes.at[1:1 + 2 * pairs:2].set(source_of - shifted).at[2:2 + 2 * pairs:2].set(sink + shifted)
    return sizes[jax.random.permutation(jax.random.fold_in(stream_key, 2), count)]


def gaussian(key, extent, scale, most, pieces=(), kind=jnp.bfloat16):
    values = scale * jax.random.normal(key, extent, jnp.float32)
    if pieces:
        values = values * shard_levels(key, extent, pieces, -0.22, 0.18)
    return jnp.clip(values, -most, most).astype(kind)


def setup_inputs(seed: int = 0) -> dict:
    streams_of = jax.random.split(jax.random.key(seed), 18)
    return {
        "tokens": gaussian(streams_of[0], (TOKENS, D), 1.0, 6.0, ((0, 128),)),
        "lengths": jax.vmap(lambda own: uneven(own, SEQS, NB, NB - 3, 1))(jax.random.split(streams_of[1], GROUPS)).reshape((GROUPS, SEQS)).astype(jnp.int32),
        "block_table": jax.vmap(lambda own: jax.random.permutation(own, NB))(jax.random.split(streams_of[2], GROUPS)).reshape((GROUPS, NB)).astype(jnp.int32),
        "qkv_weight": gaussian(streams_of[3], (D, 3 * D), D ** -0.5, 0.21875, ((0, 128),)),
        "query_bias": gaussian(streams_of[4], (D,), 0.5, 3.0, ((0, 128),)),
        "value_bias": gaussian(streams_of[5], (D,), 0.03, 0.1796875, ((0, 128),)),
        "out_weight": gaussian(streams_of[6], (D, D), 4 ** -0.5, 3.0, ((0, 128),)),
        "out_bias": gaussian(streams_of[7], (D,), 0.3, 2.0, ((0, 128),)),
        "first_gain": jnp.clip(1.0 + 0.1 * jax.random.normal(streams_of[8], (D,), jnp.float32), 0.5, 1.5).astype(jnp.bfloat16),
        "first_shift": gaussian(streams_of[9], (D,), 0.3, 2.0, ((0, 128),)),
        "up_weight": gaussian(streams_of[10], (D, FF), D ** -0.5, 0.21875, ((0, 128),)),
        "up_bias": gaussian(streams_of[11], (FF,), 0.3, 2.0, ((0, 128),)),
        "down_weight": gaussian(streams_of[12], (FF, D), FF ** -0.5, 0.109375, ((0, 128),)),
        "down_bias": gaussian(streams_of[13], (D,), 0.3, 2.0, ((0, 128),)),
        "second_gain": jnp.clip(1.0 + 0.1 * jax.random.normal(streams_of[14], (D,), jnp.float32), 0.5, 1.5).astype(jnp.bfloat16),
        "second_shift": gaussian(streams_of[15], (D,), 0.3, 2.0, ((0, 128),)),
        "cotangent": gaussian(streams_of[16], (TOKENS, D), 1.0, 6.0, ((0, 128),)),
    }


EPS = 1e-12

@jax.custom_vjp
def low(v):
    return lax.optimization_barrier(v.astype(jnp.bfloat16)).astype(jnp.float32)

@jax.custom_vjp
def low_back(v):
    return v

def low_keep(v):
    return (low(v), None)

def low_pass(kept, grad):
    return (grad,)

def back_keep(v):
    return (v, None)

def back_low(kept, grad):
    return (low(grad),)
low.defvjp(low_keep, low_pass)
low_back.defvjp(back_keep, back_low)

def rounded_both(v):
    return low(low_back(v))

def matmul(a, b):
    return jnp.dot(a, b, precision=lax.Precision.HIGHEST)

def layer_norm(z, gain, shift):
    centered = z - lax.optimization_barrier(jnp.mean(z, axis=-1, keepdims=True))
    factor = lax.rsqrt(lax.optimization_barrier(jnp.mean(centered * centered, axis=-1, keepdims=True)) + EPS)
    return centered * factor * gain + shift

def segment_ids(lengths, block_table):
    ends = jnp.cumsum(lengths, axis=1)
    block_seg = lax.optimization_barrier(jnp.sum((block_table[:, :, None] >= ends[:, None, :]).astype(jnp.int32), axis=2))
    return jnp.repeat(block_seg, BLK, axis=1).astype(jnp.int32)

def head_attend(q_head, k_head, v_head, allowed):
    scale = 1.0 / math.sqrt(HD)
    scores = low_back(matmul(q_head, k_head.T) * scale)
    scores = jnp.where(allowed, scores, -1e+30)
    probs = jax.nn.softmax(scores, axis=-1)
    return matmul(low(probs), v_head)

def group_attend(parts):
    query, key, value, seg = parts
    allowed = seg[:, None] == seg[None, :]

    def split(m):
        return m.reshape(GT, H, HD).transpose(1, 0, 2)
    step = jax.checkpoint(lambda t: head_attend(t[0], t[1], t[2], allowed))
    out = lax.map(step, (split(query), split(key), split(value)))
    return out.transpose(1, 0, 2).reshape(GT, D)

def forward(seg, inputs, qkv_weight, query_bias, value_bias, out_weight, out_bias, first_gain, first_shift, up_weight, up_bias, down_weight, down_bias, second_gain, second_shift):
    qkv = matmul(inputs, qkv_weight)
    query = rounded_both(qkv[:, :D] + query_bias)
    key = rounded_both(qkv[:, D:2 * D])
    value = rounded_both(qkv[:, 2 * D:] + value_bias)

    def grouped(m):
        return m.reshape(GROUPS, GT, D)
    attended = lax.map(group_attend, (grouped(query), grouped(key), grouped(value), seg))
    attended = rounded_both(attended.reshape(TOKENS, D))
    branch = low_back(matmul(attended, out_weight) + out_bias)
    hidden1 = layer_norm(inputs + branch, first_gain, first_shift)
    upper = low_back(matmul(low(hidden1), up_weight) + up_bias)
    activ = low(jax.nn.gelu(upper))
    feed = low_back(matmul(activ, down_weight) + down_bias)
    return layer_norm(hidden1 + feed, second_gain, second_shift)

def reference(tokens, lengths, block_table, qkv_weight, query_bias, value_bias, out_weight, out_bias, first_gain, first_shift, up_weight, up_bias, down_weight, down_bias, second_gain, second_shift, cotangent):
    seg = segment_ids(lengths, block_table)
    values = [tokens, qkv_weight, query_bias, value_bias, out_weight, out_bias, first_gain, first_shift, up_weight, up_bias, down_weight, down_bias, second_gain, second_shift]
    values = [v.astype(jnp.float32) for v in values]
    result, pullback = jax.vjp(lambda *v: forward(seg, *v), *values)
    grads = pullback(cotangent.astype(jnp.float32))
    return (result.astype(jnp.bfloat16), grads[0], grads[1], grads[2], grads[3], grads[4], grads[5], grads[6], grads[7], grads[8], grads[9], grads[10], grads[11], grads[12], grads[13])
```

```python
import functools

import jax
import jax.numpy as jnp
from jax import lax
from jax.experimental import pallas as pl
from jax.experimental.pallas import tpu as pltpu
from jax.sharding import PartitionSpec as P

MESH = pl.DeviceIdType.MESH
BF, F32 = jnp.bfloat16, jnp.float32
EPS = 1e-12
D, FF, T = 768, 3072, 256
NA, NB, NC = 2432, 3968, 896
WIDE = ((24, NA), (24, NB), (96, NC))
TALL = ((16, NA), (16, NB), (32, NC))
ROWS = (6, 6, 24)
ROUTES = (
    ("yz", (((0, 0, NA),), ((2, 0, 640),))),
    ("zy", (((2, 640, 256), (1, 0, 1408)), ((1, 1408, 2560),))),
)
CHUNKS = (((0, 0, NA), (2, 0, 640)), ((2, 640, 256), (1, 0, NB)))
BOTH = (0, 1)


def coords():
    f, s = lax.axis_index("fsdp"), lax.axis_index("seq")
    return s % 4, (f // 2) % 4, (f // 8) * 2 + s // 4, f % 2


def ident(x, y, z, core):
    return {"fsdp": (z // 2) * 8 + y * 2 + core, "seq": (z % 2) * 4 + x}


def block_of(y, z, core):
    return (z // 2) * 16 + y * 4 + core * 2 + z % 2


def greet(partners):
    barrier = pltpu.get_barrier_semaphore()
    for who in partners:
        pl.semaphore_signal(barrier, inc=1, device_id=who, device_id_type=MESH)
    pl.semaphore_wait(barrier, len(partners))


def remote(src, dst, send, recv, who):
    return pltpu.make_async_remote_copy(
        src, dst, send, recv, device_id=who, device_id_type=MESH
    )


def dot(a, b):
    return jnp.dot(a, b, preferred_element_type=F32)


def dot_t(a, b):
    return lax.dot_general(a, b, (((1,), (1,)), ((), ())), preferred_element_type=F32)


def dot_rows(a, b):
    return lax.dot_general(a, b, (((0,), (0,)), ((), ())), preferred_element_type=F32)


def picker(shape, rows, at, transposed):
    i = lax.broadcasted_iota(jnp.int32, shape, 0)
    j = lax.broadcasted_iota(jnp.int32, shape, 1)
    if transposed:
        i, j = j, i
    return jnp.where((i == at * rows + j) & (j < rows), 1.0, 0.0).astype(BF)


def neighbours(x, y, z, core):
    peers = [ident((x + d) % 4, y, z, core) for d in (1, 2, 3)]
    rings = {
        "y": [ident(x, (y + d) % 4, z, core) for d in (1, 3)],
        "z": [ident(x, y, (z + d) % 4, core) for d in (1, 3)],
    }
    return peers, rings, ident(x, y, z, 1 - core)


def across(x, y, z, core):
    other = z + 1 - 2 * (z % 2)
    return [ident((x + d) % 4, y, other, core) for d in range(4)]


def gather_kernel(
    s0, s1, s2, tokens, w0, w1, w2, q_out, kv_out,
    x0, x1, x2, own0, own1, own2, land, q_land, kv_land, q_slab, kv_slab,
    x_send, x_recv, put_sem, send, recv, core_send, core_recv, q_send, q_recv, kv_send, kv_recv,
):
    x, y, z, core = coords()
    slabs, arrived, own = (s0, s1, s2), (x0, x1, x2), (own0, own1, own2)
    wide = (land, w1, w2)
    peers, rings, sibling = neighbours(x, y, z, core)
    others = across(x, y, z, core)
    greet(peers + rings["y"] + rings["z"] + [sibling] + others)
    x_copies = []
    for d in (1, 3, 2):
        for k in range(3):
            c = remote(slabs[k], arrived[k].at[d - 1], x_send.at[d - 1, k], x_recv.at[d - 1, k], peers[d - 1])
            c.start()
            x_copies.append(c)
    for c in x_copies:
        c.wait_recv()
    for k, rows in enumerate(ROWS):
        shape = (4 * rows, TALL[k][0])
        total = jnp.zeros(WIDE[k], F32)
        for d in range(4):
            slab = slabs[k][...] if d == 0 else arrived[k][d - 1]
            total += dot(picker(shape, rows, (x + 4 - d) % 4, False), slab)
        own[k][...] = total.astype(BF)

    me = block_of(y, z, core)
    puts = [pltpu.make_async_copy(own[k], wide[k].at[me], put_sem.at[k]) for k in range(3)]
    for c in puts:
        c.start()
    started, shared = [], []

    def place(route, a, b, c):
        dy, dz = (a, b) if ROUTES[route][0] == "yz" else (b, a)
        return block_of((y + dy) % 4, (z + dz) % 4, c)

    def source(k, route, a, b):
        return own[k] if a == 0 and b == 0 else wide[k].at[place(route, a, b, core)]

    def push(route, i, a, b, who, sem):
        at = place(route, a, b, core)
        for j, (k, first, cols) in enumerate(ROUTES[route][1][i]):
            view = pl.ds(first, cols)
            c = remote(source(k, route, a, b).at[:, view], wide[k].at[at, :, view], send.at[sem + j], recv.at[sem + j], who)
            c.start()
            started.append(c)

    def arrive(route, i, a, b, sem):
        for j, (k, first, cols) in enumerate(ROUTES[route][1][i]):
            view = wide[k].at[place(route, a, b, core), :, pl.ds(first, cols)]
            remote(view, view, send.at[sem + j], recv.at[sem + j], sibling).wait_recv()

    def share(route, a, b):
        at = place(route, a, b, core)
        for k, first, cols in CHUNKS[route]:
            n, view = len(shared), pl.ds(first, cols)
            c = remote(source(k, route, a, b).at[:, view], wide[k].at[at, :, view], core_send.at[n], core_recv.at[n], sibling)
            c.start()
            shared.append((c, route, a, b, k, view))

    def slot(route, group, kind, i):
        return (route * 5 + group) * 9 + kind * 3 + (len(ROUTES[route][1][0]) if i else 0)

    def axis(route, group):
        return rings[ROUTES[route][0][0 if group == 0 else 1]]

    def begin(route, group, a, b):
        for turn in BOTH:
            for i in BOTH:
                push(route, i, a, b, axis(route, group)[turn], slot(route, group, turn, i))

    def onward(route, group, turn, a, b):
        for i in BOTH:
            arrive(route, i, a, b, slot(route, group, turn, i))
        push(route, turn, a, b, axis(route, group)[turn], slot(route, group, 2, turn))

    def finish(route, group, a, b):
        for i in BOTH:
            arrive(route, i, a, b, slot(route, group, 2, i))

    for r in BOTH:
        begin(r, 0, 0, 0)
    for r in BOTH:
        begin(r, 1, 0, 0)
    for r in BOTH:
        share(r, 0, 0)
    for turn, a in ((0, 3), (1, 1)):
        for r in BOTH:
            onward(r, 0, turn, a, 0)
            begin(r, 1 + a, a, 0)
            share(r, a, 0)
    for turn, b in ((0, 3), (1, 1)):
        for r in BOTH:
            onward(r, 1, turn, 0, b)
            share(r, 0, b)
    for r in BOTH:
        finish(r, 0, 2, 0)
        begin(r, 3, 2, 0)
        share(r, 2, 0)
    for a in (3, 1):
        for turn, b in ((0, 3), (1, 1)):
            for r in BOTH:
                onward(r, 1 + a, turn, a, b)
                share(r, a, b)
    for r in BOTH:
        finish(r, 1, 0, 2)
        share(r, 0, 2)
    for turn, b in ((0, 3), (1, 1)):
        for r in BOTH:
            onward(r, 3, turn, 2, b)
            share(r, 2, b)
    for a in (3, 1, 2):
        for r in BOTH:
            finish(r, 1 + a, a, 2)
            share(r, a, 2)
    for n, (c, route, a, b, k, view) in enumerate(shared):
        got = wide[k].at[place(route, a, b, 1 - core), :, view]
        remote(got, got, core_send.at[n], core_recv.at[n], sibling).wait_recv()
        c.wait_send()
    for c in x_copies + started:
        c.wait_send()
    for c in puts:
        c.wait()

    keep = pltpu.make_async_copy(land, w0, put_sem.at[0])
    keep.start()
    weight = land[...].reshape(D, NA)
    biases = weight[:, 3 * D :].astype(F32).T
    qkv = dot(tokens[...], weight[:, : 3 * D])
    query = (qkv[:, :D] + biases[0:1]).astype(BF).astype(F32) * 0.125
    key = qkv[:, D : 2 * D]
    value = qkv[:, 2 * D :] + biases[1:2]
    for g in range(4):
        at = g * 192
        q_slab[g] = jnp.concatenate(
            [query[:, at : at + 192], jnp.zeros((T, 64), F32)], axis=1
        ).astype(BF)
        kv_slab[g] = jnp.concatenate(
            [key[:, at : at + 128], value[:, at : at + 128], key[:, at + 128 : at + 192], value[:, at + 128 : at + 192]], axis=1
        ).astype(BF)
    mine = (z % 2) * 4 + x
    copies = []
    for d in range(4):
        to = (x + d) % 4
        c = remote(kv_slab.at[to], kv_land.at[mine], kv_send.at[4 + d], kv_recv.at[4 + d], others[d])
        c.start()
        copies.append((c, kv_land.at[(1 - z % 2) * 4 + (x + 4 - d) % 4], kv_send.at[4 + d], kv_recv.at[4 + d]))
    for d in (2, 1, 3):
        to, fro = (x + d) % 4, (x + 4 - d) % 4
        for slab, landing, place_to, place_from, ss, rr in (
            (kv_slab, kv_land, mine, (z % 2) * 4 + fro, kv_send, kv_recv),
            (q_slab, q_land, x, fro, q_send, q_recv),
        ):
            c = remote(slab.at[to], landing.at[place_to], ss.at[d], rr.at[d], peers[d - 1])
            c.start()
            copies.append((c, landing.at[place_from], ss.at[d], rr.at[d]))
    kv_land[mine] = kv_slab[x]
    q_land[x] = q_slab[x]
    for c, got, ss, rr in copies:
        remote(got, got, ss, rr, sibling).wait_recv()
    for c, got, ss, rr in copies:
        c.wait_send()
    outs = [pltpu.make_async_copy(q_land, q_out, put_sem.at[1]), pltpu.make_async_copy(kv_land, kv_out, put_sem.at[2])]
    for c in outs:
        c.start()
    for c in outs + [keep]:
        c.wait()


ANY = pl.BlockSpec(memory_space=pl.ANY)
VM = pl.BlockSpec(memory_space=pltpu.VMEM)
DMA = pltpu.SemaphoreType.DMA


def struct(shape, kind):
    return jax.ShapeDtypeStruct(shape, kind)


def gather_weights(s0, s1, s2, tokens):
    return pl.pallas_call(
        gather_kernel,
        out_shape=tuple(struct((32,) + w, BF) for w in WIDE) + (struct((4, T, 256), BF), struct((8, T, 384), BF)),
        in_specs=[VM] * 4,
        out_specs=(ANY,) * 5,
        scratch_shapes=[pltpu.VMEM((3,) + t, BF) for t in TALL]
        + [pltpu.VMEM(w, BF) for w in WIDE]
        + [pltpu.VMEM((32,) + WIDE[0], BF), pltpu.VMEM((4, T, 256), BF), pltpu.VMEM((8, T, 384), BF)]
        + [pltpu.VMEM((4, T, 256), BF), pltpu.VMEM((4, T, 384), BF)]
        + [DMA((3, 3)), DMA((3, 3)), DMA((3,)), DMA((90,)), DMA((90,)), DMA((64,)), DMA((64,))]
        + [DMA((4,)), DMA((4,)), DMA((8,)), DMA((8,))],
        compiler_params=pltpu.CompilerParams(collective_id=0, has_side_effects=True, vmem_limit_bytes=48 << 20),
        name="gather_weights",
    )(s0, s1, s2, tokens)


def head_lanes(tile, h):
    lane = lax.broadcasted_iota(jnp.int32, (1, 128), 1)
    return (lane < 64) if h % 2 == 0 else (lane >= 64)


def attend_kernel(q_ref, kv_ref, qseg, kseg, o_ref, lse_ref):
    allowed = qseg[:, :1] == kseg[0:1, :]
    outs, logs = [], []
    for h in range(3):
        tile = h // 2
        lanes = head_lanes(tile, h)
        q = q_ref[:, tile * 128 : tile * 128 + 128]
        q = jnp.where(lanes, q.astype(F32), 0.0).astype(BF)
        k = kv_ref[:, 0:128] if tile == 0 else kv_ref[:, 256:384]
        v = kv_ref[:, 128:256] if tile == 0 else kv_ref[:, 256:384]
        s = jnp.where(allowed, dot_t(q, k), -1e30)
        top = jnp.max(s, axis=1, keepdims=True)
        e = jnp.exp(s - top)
        total = jnp.sum(e, axis=1, keepdims=True)
        outs.append(dot(e.astype(BF), v) / total)
        logs.append(top + jnp.log(total))
    first = head_lanes(0, 0)
    o_ref[:, 0:128] = jnp.where(first, outs[0], outs[1]).astype(BF)
    o_ref[:, 128:256] = jnp.where(first, 0.0, outs[2]).astype(BF)
    lane = lax.broadcasted_iota(jnp.int32, (1, 128), 1)
    lse_ref[...] = jnp.where(lane == 0, logs[0], jnp.where(lane == 1, logs[1], logs[2]))


def attend(q, kv, qseg, kseg):
    step = 256
    return pl.pallas_call(
        attend_kernel,
        grid=(1024 // step,),
        out_shape=(struct((1024, 256), BF), struct((1024, 128), F32)),
        in_specs=[
            pl.BlockSpec((step, 256), lambda i: (i, 0)),
            pl.BlockSpec((2048, 384), lambda i: (0, 0)),
            pl.BlockSpec((step, 128), lambda i: (i, 0)),
            pl.BlockSpec((8, 2048), lambda i: (0, 0)),
        ],
        out_specs=(pl.BlockSpec((step, 256), lambda i: (i, 0)), pl.BlockSpec((step, 128), lambda i: (i, 0))),
        compiler_params=pltpu.CompilerParams(vmem_limit_bytes=48 << 20),
        name="attend",
    )(q, kv, qseg, kseg)


def attend_back_kernel(q_ref, kv_ref, do_ref, o_ref, lse_ref, qseg, kseg, dq_ref, dkv_ref, total):
    step = pl.program_id(0)

    @pl.when(step == 0)
    def _():
        total[...] = jnp.zeros_like(total)

    allowed = kseg[:, :1] == qseg[0:1, :]
    logs = lse_ref[...].T
    first = head_lanes(0, 0)
    grads = []
    for h in range(3):
        tile = h // 2
        lanes = head_lanes(tile, h)
        out_lanes = lanes if h < 2 else jnp.logical_not(lanes)
        cols = slice(tile * 128, tile * 128 + 128)
        q = jnp.where(lanes, q_ref[:, cols].astype(F32), 0.0).astype(BF)
        do = jnp.where(out_lanes, do_ref[:, cols].astype(F32), 0.0)
        inner = jnp.sum(do * o_ref[:, cols].astype(F32), axis=1, keepdims=True)
        inner = jnp.broadcast_to(inner, (inner.shape[0], 128)).T[0:1]
        do = do.astype(BF)
        k = kv_ref[:, 0:128] if tile == 0 else kv_ref[:, 256:384]
        v = kv_ref[:, 128:256] if tile == 0 else kv_ref[:, 256:384]
        s = dot_t(k, q)
        p = jnp.where(allowed, jnp.exp(s - logs[h : h + 1]), 0.0)
        ds = (p * (dot_t(v, do) - inner)).astype(BF)
        dk, dv = dot(ds, q), dot(p.astype(BF), do)
        if tile == 0:
            total[:, 0:128] += dk
            total[:, 128:256] += dv
        else:
            total[:, 256:384] += dk + dv
        grads.append(dot_rows(ds, k) * 0.125)
    dq_ref[:, 0:128] = jnp.where(first, grads[0], grads[1]).astype(BF)
    dq_ref[:, 128:256] = jnp.where(first, grads[2], 0.0).astype(BF)

    @pl.when(step == pl.num_programs(0) - 1)
    def _():
        dkv_ref[...] = total[...].astype(BF)


def attend_back(q, kv, do, o, lse, qseg, kseg):
    step = 256
    rows = lambda i: (i, 0)
    return pl.pallas_call(
        attend_back_kernel,
        grid=(1024 // step,),
        out_shape=(struct((1024, 256), BF), struct((2048, 384), BF)),
        in_specs=[
            pl.BlockSpec((step, 256), rows),
            pl.BlockSpec((2048, 384), lambda i: (0, 0)),
            pl.BlockSpec((step, 256), rows),
            pl.BlockSpec((step, 256), rows),
            pl.BlockSpec((step, 128), rows),
            pl.BlockSpec((8, step), lambda i: (0, i)),
            pl.BlockSpec((2048, 128), lambda i: (0, 0)),
        ],
        out_specs=(pl.BlockSpec((step, 256), rows), pl.BlockSpec((2048, 384), lambda i: (0, 0))),
        scratch_shapes=[pltpu.VMEM((2048, 384), F32)],
        compiler_params=pltpu.CompilerParams(vmem_limit_bytes=56 << 20),
        name="attend_back",
    )(q, kv, do, o, lse, qseg, kseg)


def normalize(v):
    centered = v - jnp.mean(v, axis=-1, keepdims=True)
    factor = lax.rsqrt(jnp.mean(centered * centered, axis=-1, keepdims=True) + EPS)
    return centered * factor, factor


def norm_back(grad, normed, factor, gain):
    scaled = grad * gain
    inner = jnp.mean(scaled * normed, axis=-1, keepdims=True)
    return factor * (scaled - jnp.mean(scaled, axis=-1, keepdims=True) - normed * inner)


def middle_kernel(
    o_ref, tokens, cotangent, w1, w2, result, dz1_ref, do_out, g1, g2,
    land, do_slab, wb, wc, ext, act, slope, load, o_send, o_recv, d_send, d_recv,
):
    x, y, z, core = coords()
    peers, _, sibling = neighbours(x, y, z, core)
    loads = [pltpu.make_async_copy(w1, wb, load.at[0]), pltpu.make_async_copy(w2, wc, load.at[1])]
    for c in loads:
        c.start()
    greet(peers)

    def swap(slab, landing, ss, rr):
        copies = []
        for d in (2, 1, 3):
            c = remote(slab.at[(x + d) % 4], landing.at[x], ss.at[d - 1], rr.at[d - 1], peers[d - 1])
            c.start()
            copies.append((c, landing.at[(x + 4 - d) % 4], ss.at[d - 1], rr.at[d - 1]))
        landing[x] = slab[x]
        return copies

    copies = swap(o_ref, land, o_send, o_recv)
    for c in loads:
        c.wait()
    vectors = wb[:, :, 3840:].reshape(D, 128).astype(F32).T
    out_bias, gain_one, shift_one, down_bias, gain_two, shift_two = (vectors[i : i + 1] for i in range(6))
    for g in range(4):
        part = wb[g * 8 : g * 8 + 8, :, 0:D].reshape(192, D)
        ext[g, 0:128] = part[0:128]
        ext[g, 128:192] = jnp.zeros((64, D), BF)
        ext[g, 192:256] = part[128:192]
    for c, got, ss, rr in copies:
        remote(got, got, ss, rr, sibling).wait_recv()
        c.wait_send()
    branch = dot(land[0], ext[0])
    for g in range(1, 4):
        branch += dot(land[g], ext[g])
    normed_one, factor_one = normalize(tokens[...].astype(F32) + (branch + out_bias))
    hidden = normed_one * gain_one + shift_one
    low = hidden.astype(BF)
    feed = jnp.zeros((T, D), F32)
    for n in range(4):
        up = wb[:, :, D + n * D : 2 * D + n * D].reshape(D, D)
        down = wc[n * 8 : n * 8 + 8].reshape(D, NC)
        upper = dot(low, up) + down[:, D:].astype(F32).T[0:1]
        square = upper * upper
        t = jnp.tanh(0.7978845608028654 * (upper + 0.044715 * (square * upper)))
        half = 0.5 * (1.0 + t)
        slope[n] = half + 0.5 * upper * (1.0 - t * t) * (0.7978845608028654 * (1.0 + 3.0 * 0.044715 * square))
        act[n] = (upper * half).astype(BF)
        feed += dot(act[n], down[:, :D])
    normed_two, factor_two = normalize(hidden + (feed + down_bias))
    result[...] = (normed_two * gain_two + shift_two).astype(BF)
    grad = cotangent[...].astype(F32)
    dz2 = norm_back(grad, normed_two, factor_two, gain_two)

    def columns(v):
        return jnp.sum(v, axis=0, keepdims=True)

    gain_two_grad, shift_two_grad = columns(grad * normed_two), columns(grad)
    dfeed = dz2.astype(BF)
    down_bias_grad = columns(dfeed.astype(F32))
    dhidden = dz2

    def as_columns(rows):
        wide = [jnp.zeros((128 - len(rows), D), F32)]
        return jnp.concatenate(rows + wide, axis=0).T.astype(BF)

    for n in range(4):
        up = wb[:, :, D + n * D : 2 * D + n * D].reshape(D, D)
        down = wc[n * 8 : n * 8 + 8, :, :D].reshape(D, D)
        dupper = dot_t(dfeed, down) * slope[n]
        low_dupper = dupper.astype(BF)
        g2[n * 8 : n * 8 + 8, :, :D] = dot_rows(act[n], dfeed).astype(BF).reshape(8, 96, D)
        g2[n * 8 : n * 8 + 8, :, D:] = as_columns([columns(low_dupper.astype(F32))]).reshape(8, 96, 128)
        g1[:, :, D + n * D : 2 * D + n * D] = dot_rows(low, low_dupper).astype(BF).reshape(32, 24, D)
        dhidden += dot_t(low_dupper, up)
    dz1 = norm_back(dhidden, normed_one, factor_one, gain_one)
    dz1_ref[...] = dz1
    dbranch = dz1.astype(BF)
    for g in range(4):
        do_slab[g] = dot_t(dbranch, ext[g]).astype(BF)
    copies = swap(do_slab, do_out, d_send, d_recv)
    for g in range(4):
        part = dot_rows(land[g], dbranch).astype(BF)
        g1[g * 8 : g * 8 + 8, :, 0:D] = jnp.concatenate([part[0:128], part[192:256]], axis=0).reshape(8, 24, D)
    g1[:, :, 3840:] = as_columns(
        [columns(dbranch.astype(F32)), columns(dhidden * normed_one), columns(dhidden),
         down_bias_grad, gain_two_grad, shift_two_grad]
    ).reshape(32, 24, 128)
    for c, got, ss, rr in copies:
        remote(got, got, ss, rr, sibling).wait_recv()
        c.wait_send()


def middle(o, tokens, cotangent, w1, w2):
    return pl.pallas_call(
        middle_kernel,
        out_shape=(
            struct((T, D), BF), struct((T, D), F32), struct((4, T, 256), BF),
            struct((32,) + WIDE[1], BF), struct((32,) + WIDE[2], BF),
        ),
        in_specs=[VM, VM, VM, ANY, ANY],
        out_specs=(VM,) * 5,
        scratch_shapes=[
            pltpu.VMEM((4, T, 256), BF), pltpu.VMEM((4, T, 256), BF),
            pltpu.VMEM((32,) + WIDE[1], BF), pltpu.VMEM((32,) + WIDE[2], BF),
            pltpu.VMEM((4, 256, D), BF), pltpu.VMEM((4, T, D), BF), pltpu.VMEM((4, T, D), F32),
            DMA((2,)), DMA((3,)), DMA((3,)), DMA((3,)), DMA((3,)),
        ],
        compiler_params=pltpu.CompilerParams(collective_id=1, has_side_effects=True, vmem_limit_bytes=60 << 20),
        name="middle",
    )(o, tokens, cotangent, w1, w2)


def scatter_kernel(
    dq_ref, dkv_ref, tokens, dz1, w0, g1, g2, dx_ref, o0, o1, o2,
    wa, g0, a0, a1, a2, c0, c1, c2, b0, b1, b2, xs0, xs1, xs2, xr0, xr1, xr2, q_land, kv_land,
    load_sem, core_send, core_recv, send, recv, x_send, x_recv, q_send, q_recv, kv_send, kv_recv, w_sem,
):
    x, y, z, core = coords()
    grads, outs, acc, fro, buf = (g0, g1, g2), (o0, o1, o2), (a0, a1, a2), (c0, c1, c2), (b0, b1, b2)
    out_slabs, in_slabs = (xs0, xs1, xs2), (xr0, xr1, xr2)
    peers, rings, sibling = neighbours(x, y, z, core)
    others = across(x, y, z, core)
    fetch = pltpu.make_async_copy(w0, wa, w_sem.at[0])
    fetch.start()
    greet(peers + rings["y"] + rings["z"] + [sibling] + others)

    mine = (z % 2) * 4 + x
    copies = []
    for d in range(4):
        to = (1 - z % 2) * 4 + (x + d) % 4
        c = remote(dkv_ref.at[to], kv_land.at[mine], kv_send.at[4 + d], kv_recv.at[4 + d], others[d])
        c.start()
        copies.append((c, kv_land.at[(1 - z % 2) * 4 + (x + 4 - d) % 4], kv_send.at[4 + d], kv_recv.at[4 + d]))
    for d in (2, 1, 3):
        to, came = (x + d) % 4, (x + 4 - d) % 4
        c = remote(dkv_ref.at[(z % 2) * 4 + to], kv_land.at[mine], kv_send.at[d], kv_recv.at[d], peers[d - 1])
        c.start()
        copies.append((c, kv_land.at[(z % 2) * 4 + came], kv_send.at[d], kv_recv.at[d]))
        c = remote(dq_ref.at[to], q_land.at[x], q_send.at[d], q_recv.at[d], peers[d - 1])
        c.start()
        copies.append((c, q_land.at[came], q_send.at[d], q_recv.at[d]))
    kv_land[mine] = dkv_ref[mine]
    q_land[x] = dq_ref[x]

    def spot(route, a, b):
        dy, dz = (a, b) if ROUTES[route][0] == "yz" else (b, a)
        return dy, dz, dy * 4 + dz

    swaps, loads = {}, {}

    def begin_swaps(arrays):
        for b in (2, 1, 3, 0):
            for a in (2, 1, 3, 0):
                for r in BOTH:
                    dy, dz, at = spot(r, a, b)
                    here = block_of((y + dy) % 4, (z + dz) % 4, core)
                    there = block_of((y + dy) % 4, (z + dz) % 4, 1 - core)
                    for j, (k, first, cols) in enumerate(CHUNKS[r]):
                        if k not in arrays:
                            continue
                        n, view = (r * 16 + a * 4 + b) * 2 + j, pl.ds(first, cols)
                        swaps[n] = remote(
                            grads[k].at[there, :, view], fro[k].at[at, :, view], core_send.at[n], core_recv.at[n], sibling
                        )
                        loads[n] = pltpu.make_async_copy(grads[k].at[here, :, view], acc[k].at[at, :, view], load_sem.at[n])
                        swaps[n].start()
                        loads[n].start()

    begin_swaps((1, 2))
    fetch.wait()
    for c, got, ss, rr in copies:
        remote(got, got, ss, rr, sibling).wait_recv()
    dq = jnp.concatenate([q_land[g][:, 0:192].astype(F32) for g in range(4)], axis=1)
    both = [(kv_land[g].astype(F32) + kv_land[4 + g].astype(F32)) for g in range(4)]
    dk = jnp.concatenate([p for b in both for p in (b[:, 0:128], b[:, 256:320])], axis=1)
    dv = jnp.concatenate([p for b in both for p in (b[:, 128:256], b[:, 320:384])], axis=1)
    dqkv = jnp.concatenate([dq, dk, dv], axis=1).astype(BF)
    g0[:, :, : 3 * D] = dot_rows(tokens[...], dqkv).astype(BF).reshape(32, 24, 3 * D)
    bias = jnp.sum(dqkv.astype(F32), axis=0, keepdims=True)
    bias = jnp.concatenate([bias[:, :D], bias[:, 2 * D :], jnp.zeros((126, D), F32)], axis=0)
    g0[:, :, 3 * D :] = bias.T.astype(BF).reshape(32, 24, 128)
    begin_swaps((0,))
    dx_ref[...] = dz1[...] + dot_t(dqkv, wa[...].reshape(D, NA)[:, : 3 * D])

    def fold(r, a, b):
        _, _, at = spot(r, a, b)
        for j, (k, first, cols) in enumerate(CHUNKS[r]):
            n = (r * 16 + a * 4 + b) * 2 + j
            loads[n].wait()
            swaps[n].wait_recv()
            view = (at, slice(None), pl.ds(first, cols))
            acc[k][view] = acc[k][view] + fro[k][view]

    started = []

    def slot(r, group, kind, i):
        return (r * 5 + group) * 9 + kind * 3 + (len(ROUTES[r][1][0]) if i else 0)

    def axis(r, group):
        return rings[ROUTES[r][0][0 if group == 0 else 1]]

    def at_of(r, group, step):
        return spot(r, *((step, 0) if group == 0 else (group - 1, step)))[2]

    def push(r, group, kind, i, step, who):
        for j, (k, first, cols) in enumerate(ROUTES[r][1][i]):
            n, view = slot(r, group, kind, i) + j, pl.ds(first, cols)
            c = remote(
                acc[k].at[at_of(r, group, step), :, view], buf[k].at[group * 3 + kind, :, view], send.at[n], recv.at[n], who
            )
            c.start()
            started.append(c)

    def add(r, group, kind, i, step):
        for j, (k, first, cols) in enumerate(ROUTES[r][1][i]):
            n, view = slot(r, group, kind, i) + j, pl.ds(first, cols)
            got = buf[k].at[group * 3 + kind, :, view]
            remote(got, got, send.at[n], recv.at[n], sibling).wait_recv()
            at = (at_of(r, group, step), slice(None), view)
            acc[k][at] = acc[k][at] + buf[k][group * 3 + kind, :, view]

    def first_step(r, group):
        right, left = axis(r, group)
        push(r, group, 0, 0, 2, right)
        push(r, group, 0, 1, 2, left)

    def second_step(r, group):
        right, left = axis(r, group)
        add(r, group, 0, 0, 1)
        push(r, group, 1, 0, 1, right)
        push(r, group, 1, 1, 1, right)
        add(r, group, 0, 1, 3)
        push(r, group, 2, 0, 3, left)
        push(r, group, 2, 1, 3, left)

    def third_step(r, group):
        for kind in (1, 2):
            for i in BOTH:
                add(r, group, kind, i, 0)

    turns = (2, 1, 3, 0)
    for a in turns:
        for r in BOTH:
            fold(r, a, 2)
            first_step(r, 1 + a)
    for a in turns:
        for r in BOTH:
            fold(r, a, 1)
            fold(r, a, 3)
            second_step(r, 1 + a)
    for a in turns:
        for r in BOTH:
            fold(r, a, 0)
            third_step(r, 1 + a)
            if a == 2:
                first_step(r, 0)
            if a == 3:
                second_step(r, 0)
    for r in BOTH:
        third_step(r, 0)

    x_copies = []
    for d in (2, 1, 3):
        for k, rows in enumerate(ROWS):
            pick = picker((TALL[k][0], 4 * rows), rows, (x + d) % 4, True)
            out_slabs[k][d - 1] = dot(pick, acc[k][0]).astype(BF)
            c = remote(out_slabs[k].at[d - 1], in_slabs[k].at[d - 1], x_send.at[d - 1, k], x_recv.at[d - 1, k], peers[d - 1])
            c.start()
            x_copies.append(c)
    for k, rows in enumerate(ROWS):
        outs[k][...] = dot(picker((TALL[k][0], 4 * rows), rows, x, True), acc[k][0])
    for c in x_copies:
        c.wait_recv()
    for k in range(3):
        outs[k][...] += in_slabs[k][0].astype(F32) + in_slabs[k][1].astype(F32) + in_slabs[k][2].astype(F32)
    for c in x_copies + started + list(swaps.values()) + [c for c, _, _, _ in copies]:
        c.wait_send()


def scatter_grads(dq, dkv, tokens, dz1, w0, g1, g2):
    return pl.pallas_call(
        scatter_kernel,
        out_shape=(struct((T, D), F32),) + tuple(struct(t, F32) for t in TALL),
        in_specs=[VM, VM, VM, VM, ANY, ANY, ANY],
        out_specs=(VM,) * 4,
        scratch_shapes=[pltpu.VMEM((32,) + WIDE[0], BF)] * 2
        + [pltpu.VMEM((16,) + w, BF) for w in WIDE] * 2
        + [pltpu.VMEM((15,) + w, BF) for w in WIDE]
        + [pltpu.VMEM((3,) + t, BF) for t in TALL] * 2
        + [pltpu.VMEM((4, T, 256), BF), pltpu.VMEM((8, T, 384), BF)]
        + [DMA((64,)), DMA((64,)), DMA((64,)), DMA((90,)), DMA((90,)), DMA((3, 3)), DMA((3, 3))]
        + [DMA((4,)), DMA((4,)), DMA((8,)), DMA((8,)), DMA((1,))],
        compiler_params=pltpu.CompilerParams(collective_id=2, has_side_effects=True, vmem_limit_bytes=62 << 20),
        name="scatter_grads",
    )(dq, dkv, tokens, dz1, w0, g1, g2)


def shards(
    tokens, lengths, block_table, qkv_weight, query_bias, value_bias, out_weight, out_bias, first_gain, first_shift,
    up_weight, up_bias, down_weight, down_bias, second_gain, second_shift, cotangent,
):
    def pack(arrays, shape):
        wide = jnp.concatenate([a if a.ndim == 2 else a[:, None] for a in arrays], axis=1)
        return jnp.pad(wide, ((0, shape[0] - wide.shape[0]), (0, shape[1] - wide.shape[1])))

    slabs = (
        pack((qkv_weight, query_bias, value_bias), TALL[0]),
        pack((out_weight, up_weight, out_bias, first_gain, first_shift, down_bias, second_gain, second_shift), TALL[1]),
        pack((down_weight, up_bias), TALL[2]),
    )
    ends = jnp.cumsum(lengths[0])
    block_seg = jnp.sum((block_table[0][:, None] >= ends[None, :]).astype(jnp.int32), axis=1)
    seg = jnp.repeat(block_seg, 128)
    half = lax.dynamic_slice_in_dim(seg, (lax.axis_index("seq") // 4) * 1024, 1024)
    w0, w1, w2, q, kv = gather_weights(*slabs, tokens)
    q, kv = q.reshape(1024, 256), kv.reshape(2048, 384)
    o, lse = attend(q, kv, jnp.broadcast_to(half[:, None], (1024, 128)), jnp.broadcast_to(seg[None, :], (8, 2048)))
    result, dz1, do, g1, g2 = middle(o.reshape(4, T, 256), tokens, cotangent, w1, w2)
    dq, dkv = attend_back(
        q, kv, do.reshape(1024, 256), o, lse,
        jnp.broadcast_to(half[None, :], (8, 1024)), jnp.broadcast_to(seg[:, None], (2048, 128)),
    )
    dx, ga, gb, gc = scatter_grads(dq.reshape(4, T, 256), dkv.reshape(8, T, 384), tokens, dz1, w0, g1, g2)
    vectors = gb[:6, 3840:3846]
    return (
        result, dx, ga[:6, : 3 * D], ga[:6, 3 * D], ga[:6, 3 * D + 1],
        gb[:6, :D], vectors[:, 0], vectors[:, 1], vectors[:, 2],
        gb[:6, D:3840], gc[:24, D], gc[:24, :D], vectors[:, 3], vectors[:, 4], vectors[:, 5],
    )


def solution(mesh):
    both = ("fsdp", "seq")
    whole, flat, group = P(both, None), P(both), P("fsdp", None)
    return jax.shard_map(
        shards,
        mesh=mesh,
        in_specs=(whole, group, group, whole, flat, flat, whole, flat, flat, flat, whole, flat, whole, flat, flat, flat, whole),
        out_specs=(whole, whole, whole, flat, flat, whole, flat, flat, flat, whole, flat, whole, flat, flat, flat),
        check_vma=False,
    )
```

```python
import jax
import jax.numpy as jnp
from jax import lax
from jax.experimental import pallas as pl
from jax.experimental.pallas import tpu as pltpu
from jax.sharding import PartitionSpec as P

MESH = pl.DeviceIdType.MESH
BF, F32 = jnp.bfloat16, jnp.float32
EPS = 1e-12
D, FF, T = 768, 3072, 256
NA, NB, NC = 768, 3968, 896
WIDE = ((24, NA), (24, NB), (96, NC))
TALL = ((16, NA), (16, NB), (32, NC))
ROWS = (6, 6, 24)
EARLY = (
    ("yz", (((0, 0, 256),), ((0, 256, 128),))),
    ("zy", (((0, 384, 256),), ((0, 640, 128),))),
)
LATE = (
    ("yz", (((2, 0, 512),), ((1, 0, 1792),))),
    ("zy", (((1, 1792, 2176),), ((2, 512, 384),))),
)
BOTH = (0, 1)
TURNS = (2, 1, 3, 0)
ANY = pl.BlockSpec(memory_space=pl.ANY)
VM = pl.BlockSpec(memory_space=pltpu.VMEM)
SM = pl.BlockSpec(memory_space=pltpu.SMEM)
DMA = pltpu.SemaphoreType.DMA


def struct(shape, kind):
    return jax.ShapeDtypeStruct(shape, kind)


def chunks_of(route):
    return tuple(part for piece in route[1] for part in piece)


def coords():
    f, s = lax.axis_index("fsdp"), lax.axis_index("seq")
    return s % 4, (f // 2) % 4, (f // 8) * 2 + s // 4, f % 2


def ident(x, y, z, core):
    return {"fsdp": (z // 2) * 8 + y * 2 + core, "seq": (z % 2) * 4 + x}


def block_of(y, z, core):
    return (z // 2) * 16 + y * 4 + core * 2 + z % 2


def greet(partners):
    barrier = pltpu.get_barrier_semaphore()
    for who in partners:
        pl.semaphore_signal(barrier, inc=1, device_id=who, device_id_type=MESH)
    pl.semaphore_wait(barrier, len(partners))


def remote(src, dst, send, recv, who):
    return pltpu.make_async_remote_copy(
        src, dst, send, recv, device_id=who, device_id_type=MESH
    )


def dot(a, b):
    return jnp.dot(a, b, preferred_element_type=F32)


def dot_t(a, b):
    return lax.dot_general(a, b, (((1,), (1,)), ((), ())), preferred_element_type=F32)


def dot_rows(a, b):
    return lax.dot_general(a, b, (((0,), (0,)), ((), ())), preferred_element_type=F32)


def picker(shape, rows, at, transposed):
    i = lax.broadcasted_iota(jnp.int32, shape, 0)
    j = lax.broadcasted_iota(jnp.int32, shape, 1)
    if transposed:
        i, j = j, i
    return jnp.where((i == at * rows + j) & (j < rows), 1.0, 0.0).astype(BF)


def neighbours(x, y, z, core):
    peers = [ident((x + d) % 4, y, z, core) for d in (1, 2, 3)]
    rings = {
        "y": [ident(x, (y + d) % 4, z, core) for d in (1, 3)],
        "z": [ident(x, y, (z + d) % 4, core) for d in (1, 3)],
    }
    return peers, rings, ident(x, y, z, 1 - core)


def seg_of(lengths, table, j):
    place = table[0, j]
    end = lengths[0, 0]
    return (place >= end).astype(jnp.int32) + (place >= end + lengths[0, 1]).astype(jnp.int32)


def head_lanes(h):
    lane = lax.broadcasted_iota(jnp.int32, (1, 128), 1)
    return (lane < 64) if h % 2 == 0 else (lane >= 64)


def key_value(kv, h):
    rows = kv.shape[0] * T
    if h < 2:
        return kv[:, :, 0:128].reshape(rows, 128), kv[:, :, 128:256].reshape(rows, 128)
    both = kv[:, :, 256:384].reshape(rows, 128)
    return both, both


def interleave(events, count):
    for _ in range(min(count, len(events))):
        events.pop(0)()


def gather_events(routes, base, own, wide, where, rings, sibling, sems, started):
    y, z, core = where
    send, recv, core_send, core_recv = sems
    shared = []

    def place(route, a, b, c):
        dy, dz = (a, b) if routes[route][0] == "yz" else (b, a)
        return block_of((y + dy) % 4, (z + dz) % 4, c)

    def source(k, route, a, b):
        return own[k] if a == 0 and b == 0 else wide[k].at[place(route, a, b, core)]

    def push(route, i, a, b, who, sem):
        at = place(route, a, b, core)
        for j, (k, first, cols) in enumerate(routes[route][1][i]):
            view = pl.ds(first, cols)
            c = remote(source(k, route, a, b).at[:, view], wide[k].at[at, :, view], send.at[sem + j], recv.at[sem + j], who)
            c.start()
            started.append(c)

    def arrive(route, i, a, b, sem):
        for j, (k, first, cols) in enumerate(routes[route][1][i]):
            view = wide[k].at[place(route, a, b, core), :, pl.ds(first, cols)]
            remote(view, view, send.at[sem + j], recv.at[sem + j], sibling).wait_recv()

    def share(route, a, b):
        at = place(route, a, b, core)
        for k, first, cols in chunks_of(routes[route]):
            n, view = base // 90 * 64 + len(shared), pl.ds(first, cols)
            c = remote(source(k, route, a, b).at[:, view], wide[k].at[at, :, view], core_send.at[n], core_recv.at[n], sibling)
            c.start()
            started.append(c)
            shared.append((n, route, a, b, k, view))

    def slot(route, group, kind, i):
        return base + (route * 5 + group) * 9 + kind * 3 + (len(routes[route][1][0]) if i else 0)

    def axis(route, group):
        return rings[routes[route][0][0 if group == 0 else 1]]

    def begin(route, group, a, b):
        for turn in BOTH:
            for i in BOTH:
                push(route, i, a, b, axis(route, group)[turn], slot(route, group, turn, i))

    def onward(route, group, turn, a, b):
        for i in BOTH:
            arrive(route, i, a, b, slot(route, group, turn, i))
        push(route, turn, a, b, axis(route, group)[turn], slot(route, group, 2, turn))

    def finish(route, group, a, b):
        for i in BOTH:
            arrive(route, i, a, b, slot(route, group, 2, i))

    events = []

    def event(*steps):
        events.append(lambda: [f(*args) for f, *args in steps])

    event(*[(begin, r, 0, 0, 0) for r in BOTH])
    event(*[(begin, r, 1, 0, 0) for r in BOTH], *[(share, r, 0, 0) for r in BOTH])
    for turn, a in ((0, 3), (1, 1)):
        for r in BOTH:
            event((onward, r, 0, turn, a, 0), (begin, r, 1 + a, a, 0), (share, r, a, 0))
    for turn, b in ((0, 3), (1, 1)):
        for r in BOTH:
            event((onward, r, 1, turn, 0, b), (share, r, 0, b))
    for r in BOTH:
        event((finish, r, 0, 2, 0), (begin, r, 3, 2, 0), (share, r, 2, 0))
    for a in (3, 1):
        for turn, b in ((0, 3), (1, 1)):
            for r in BOTH:
                event((onward, r, 1 + a, turn, a, b), (share, r, a, b))
    for r in BOTH:
        event((finish, r, 1, 0, 2), (share, r, 0, 2))
    for turn, b in ((0, 3), (1, 1)):
        for r in BOTH:
            event((onward, r, 3, turn, 2, b), (share, r, 2, b))
    for a in (3, 1, 2):
        for r in BOTH:
            event((finish, r, 1 + a, a, 2), (share, r, a, 2))

    def settle():
        for n, route, a, b, k, view in shared:
            got = wide[k].at[place(route, a, b, 1 - core), :, view]
            remote(got, got, core_send.at[n], core_recv.at[n], sibling).wait_recv()

    events.append(settle)
    return events


def normalize(v):
    centered = v - jnp.mean(v, axis=-1, keepdims=True)
    factor = lax.rsqrt(jnp.mean(centered * centered, axis=-1, keepdims=True) + EPS)
    return centered * factor, factor


def norm_back(grad, normed, factor, gain):
    scaled = grad * gain
    inner = jnp.mean(scaled * normed, axis=-1, keepdims=True)
    return factor * (scaled - jnp.mean(scaled, axis=-1, keepdims=True) - normed * inner)


def columns(v):
    return jnp.sum(v, axis=0, keepdims=True)


def as_columns(rows):
    wide = [jnp.zeros((128 - len(rows), D), F32)]
    return jnp.concatenate(rows + wide, axis=0).T.astype(BF)


def eye(rows, cols):
    i = lax.broadcasted_iota(jnp.int32, (rows, cols), 0)
    j = lax.broadcasted_iota(jnp.int32, (rows, cols), 1)
    return jnp.where(i == j, 1.0, 0.0).astype(BF)


def pack_slabs(qkv_w, out_w, up_w, down_w, vectors, slabs):
    s0, s1, s2 = slabs
    spread, spread_tall = eye(16, 6), eye(32, 24)
    rows = dot(spread, qkv_w[...])
    for g in range(4):
        q, k, v = (rows[:, n * D + g * 192 : n * D + g * 192 + 192] for n in range(3))
        s0[g, :, 0:640] = jnp.concatenate(
            [q, jnp.zeros((16, 64), F32), k[:, 0:128], v[:, 0:128], k[:, 128:192], v[:, 128:192]], axis=1
        ).astype(BF)
    s1[:, 0:D] = dot(spread, out_w[...]).astype(BF)
    s1[:, D:3840] = dot(spread, up_w[...]).astype(BF)
    s2[:, 0:D] = dot(spread_tall, down_w[...]).astype(BF)
    flat = vectors[...].astype(F32)
    lane = lax.broadcasted_iota(jnp.int32, (16, 128), 1)
    row = lax.broadcasted_iota(jnp.int32, (16, 128), 0)
    rows = jnp.where((lane % 6 == row) & (lane < 48), jnp.broadcast_to(flat, (16, 128)), 0.0).astype(BF)
    i = lax.broadcasted_iota(jnp.int32, (128, 128), 0)
    j = lax.broadcasted_iota(jnp.int32, (128, 128), 1)
    biases = dot(rows, jnp.where((i // 6 == j) & (j < 2), 1.0, 0.0).astype(BF)).astype(BF)
    for g in range(4):
        s0[g, :, 640:768] = biases
    s1[:, 3840:] = dot(rows, jnp.where((i // 6 == j + 2) & (j < 6), 1.0, 0.0).astype(BF)).astype(BF)
    lane = lax.broadcasted_iota(jnp.int32, (32, 128), 1)
    row = lax.broadcasted_iota(jnp.int32, (32, 128), 0)
    rows = jnp.where((lane == row + 48) & (row < 24), jnp.broadcast_to(flat, (32, 128)), 0.0).astype(BF)
    s2[:, D:] = dot(rows, jnp.where(j == 0, 1.0, 0.0).astype(BF)).astype(BF)


def forward_kernel(
    lengths, table, qkv_w, out_w, up_w, down_w, vectors, tokens, cotangent,
    result, dz1_ref, w0, q_land, kv_land, o_slab, lse_ref, do_land, g1, g2, group_tokens,
    s0, s1, s2, x0, x1, x2, own0, own1, own2, land0, land1, land2, words, o_land, do_slab,
    ext, act, slope, grad1, grad2,
    x_send, x_recv, put_sem, send, recv, core_send, core_recv, t_send, t_recv,
    o_send, o_recv, d_send, d_recv, keep_sem,
):
    x, y, z, core = coords()
    side = z % 2
    slabs, arrived, own, wide = (s0, s1, s2), (x0, x1, x2), (own0, own1, own2), (land0, land1, land2)
    peers, rings, sibling = neighbours(x, y, z, core)
    partner = ident(x, y, z + 1 - 2 * side, core)
    pack_slabs(qkv_w, out_w, up_w, down_w, vectors, slabs)
    greet(peers + rings["y"] + rings["z"] + [sibling])
    started, x_copies = [], {}

    def token_send(src, at, who, n, part=slice(None)):
        c = remote(src.at[part], words.at[at].at[part], t_send.at[n], t_recv.at[n], who)
        c.start()
        started.append(c)

    def token_wait(at, n, part=slice(None)):
        view = words.at[at].at[part]
        remote(view, view, t_send.at[n], t_recv.at[n], sibling).wait_recv()

    right, left = peers[0], peers[2]
    halves = (pl.ds(0, T // 2), pl.ds(T // 2, T // 2))

    def line_tokens(src, which, n):
        token_send(src, which * 4 + x, right, n)
        token_send(src, which * 4 + x, left, n + 1)

    def line_onward(which, n):
        before, after = which * 4 + (x + 3) % 4, which * 4 + (x + 1) % 4
        token_wait(before, n)
        token_send(words.at[before], before, right, n + 2, halves[0])
        token_wait(after, n + 1)
        token_send(words.at[after], after, left, n + 3, halves[1])

    def line_finish(which, n):
        for i in BOTH:
            token_wait(which * 4 + (x + 2) % 4, n + 2 + i, halves[i])

    mine = side * 4 + x
    token_send(tokens, mine, partner, 0)

    for k in range(3):
        for d in (1, 3, 2):
            src = slabs[0].at[(x + d) % 4] if k == 0 else slabs[k]
            c = remote(src, arrived[k].at[d - 1], x_send.at[d - 1, k], x_recv.at[d - 1, k], peers[d - 1])
            c.start()
            x_copies[k, d] = c
            started.append(c)
    me = block_of(y, z, core)
    puts = [pltpu.make_async_copy(own[k], wide[k].at[me], put_sem.at[k]) for k in range(3)]

    def line(k):
        rows = ROWS[k]
        for d in (1, 3, 2):
            x_copies[k, d].wait_recv()
        total = jnp.zeros(WIDE[k], F32)
        for d in range(4):
            slab = arrived[k][d - 1] if d else slabs[0][x] if k == 0 else slabs[k][...]
            total += dot(picker((4 * rows, TALL[k][0]), rows, (x + 4 - d) % 4, False), slab)
        own[k][...] = total.astype(BF)
        puts[k].start()

    sems = (send, recv, core_send, core_recv)
    early = gather_events(EARLY, 0, own, wide, (y, z, core), rings, sibling, sems, started)
    late = gather_events(LATE, 90, own, wide, (y, z, core), rings, sibling, sems, started)
    line_tokens(tokens, side, 1)
    words[mine] = tokens[...]
    line(0)
    interleave(early, 2)
    line(1)
    line(2)
    token_wait((1 - side) * 4 + x, 0)
    line_tokens(words.at[(1 - side) * 4 + x], 1 - side, 5)
    interleave(early, 4)
    interleave(late, 1)
    interleave(early, 4)
    line_onward(side, 1)
    interleave(late, 1)
    interleave(early, 100)
    puts[0].wait()
    kept = [pltpu.make_async_copy(land0, w0, keep_sem.at[0])]
    kept[0].start()

    weight = land0[...].reshape(D, NA)
    biases = weight[:, 640:].astype(F32).T
    query_bias = key_bias = jnp.zeros((1, 192), F32)
    for g in range(4):
        here = slice(g * 192, g * 192 + 192)
        query_bias = jnp.where(x == g, biases[0:1, here], query_bias)
        key_bias = jnp.where(x == g, biases[1:2, here], key_bias)
    none = jnp.zeros((1, 64), F32)
    query_bias = jnp.concatenate([query_bias, none], axis=1)
    key_bias = jnp.concatenate([none, none, key_bias[:, :128], none, key_bias[:, 128:]], axis=1)

    def project(at, with_query):
        if with_query:
            both = dot(words[at], weight[:, 0:640])
            q_land[at % 4] = ((both[:, :256] + query_bias).astype(BF).astype(F32) * 0.125).astype(BF)
            kv_land[at] = (both[:, 256:] + key_bias).astype(BF)
        else:
            kv_land[at] = (dot(words[at], weight[:, 256:640]) + key_bias).astype(BF)

    project(mine, True)
    project((1 - side) * 4 + x, False)
    project(side * 4 + (x + 3) % 4, True)
    project(side * 4 + (x + 1) % 4, True)
    interleave(late, EVENTS_SWAP)
    line_onward(1 - side, 5)
    project((1 - side) * 4 + (x + 3) % 4, False)
    project((1 - side) * 4 + (x + 1) % 4, False)
    line_finish(side, 1)
    project(side * 4 + (x + 2) % 4, True)
    line_finish(1 - side, 5)
    project((1 - side) * 4 + (x + 2) % 4, False)

    kept.append(pltpu.make_async_copy(words.at[pl.ds(side * 4, 4)], group_tokens, keep_sem.at[1]))
    kept[1].start()
    copies = []

    def deliver(src, landing, to_slot, from_slot, ss, rr, who):
        c = remote(src, landing.at[to_slot], ss, rr, who)
        c.start()
        started.append(c)
        copies.append((landing.at[from_slot], ss, rr))

    key_seg = jnp.concatenate([jnp.full((1, 128), seg_of(lengths, table, j), jnp.int32) for j in range(16)], axis=1)
    first = head_lanes(0)
    lane = lax.broadcasted_iota(jnp.int32, (1, 128), 1)
    for d in TURNS:
        to = (x + d) % 4
        block = (side * 4 + to) * 2
        query_seg = jnp.concatenate([jnp.full((128, 1), seg_of(lengths, table, block + i), jnp.int32) for i in BOTH], axis=0)
        allowed = query_seg == key_seg
        outs, logs = [], []
        for h in range(3):
            interleave(late, EVENTS_UNIT)
            tile = h // 2 * 128
            q = jnp.where(head_lanes(h), q_land[to, :, tile : tile + 128].astype(F32), 0.0).astype(BF)
            k, v = key_value(kv_land[...], h)
            s = jnp.where(allowed, dot_t(q, k), -1e30)
            top = jnp.max(s, axis=1, keepdims=True)
            e = jnp.exp(s - top)
            total = jnp.sum(e, axis=1, keepdims=True)
            outs.append(dot(e.astype(BF), v) / total)
            logs.append(top + jnp.log(total))
        o_slab[to, :, 0:128] = jnp.where(first, outs[0], outs[1]).astype(BF)
        o_slab[to, :, 128:256] = jnp.where(first, 0.0, outs[2]).astype(BF)
        lse_ref[to] = jnp.where(lane == 0, logs[0], jnp.where(lane == 1, logs[1], logs[2]))
        if d:
            deliver(o_slab.at[to], o_land, x, (x + 4 - d) % 4, o_send.at[d], o_recv.at[d], peers[d - 1])
        else:
            o_land[x] = o_slab[x]
    interleave(late, 100)
    puts[1].wait()
    puts[2].wait()

    vecs = land1[:, :, 3840:].reshape(D, 128).astype(F32).T
    out_bias, gain_one, shift_one, down_bias, gain_two, shift_two = (vecs[i : i + 1] for i in range(6))
    for g in range(4):
        part = land1[g * 8 : g * 8 + 8, :, 0:D].reshape(192, D)
        ext[g, 0:128] = part[0:128]
        ext[g, 128:192] = jnp.zeros((64, D), BF)
        ext[g, 192:256] = part[128:192]
    for got, ss, rr in copies:
        remote(got, got, ss, rr, sibling).wait_recv()
    copies.clear()
    branch = dot(o_land[0], ext[0])
    for g in range(1, 4):
        branch += dot(o_land[g], ext[g])
    normed_one, factor_one = normalize(tokens[...].astype(F32) + (branch + out_bias))
    hidden = normed_one * gain_one + shift_one
    low = hidden.astype(BF)
    feed = jnp.zeros((T, D), F32)
    for n in range(4):
        up = land1[:, :, D + n * D : 2 * D + n * D].reshape(D, D)
        down = land2[n * 8 : n * 8 + 8].reshape(D, NC)
        upper = dot(low, up) + down[:, D:].astype(F32).T[0:1]
        square = upper * upper
        t = jnp.tanh(0.7978845608028654 * (upper + 0.044715 * (square * upper)))
        half = 0.5 * (1.0 + t)
        slope[n] = half + 0.5 * upper * (1.0 - t * t) * (0.7978845608028654 * (1.0 + 3.0 * 0.044715 * square))
        act[n] = (upper * half).astype(BF)
        feed += dot(act[n], down[:, :D])
    normed_two, factor_two = normalize(hidden + (feed + down_bias))
    result[...] = (normed_two * gain_two + shift_two).astype(BF)

    grad = cotangent[...].astype(F32)
    dz2 = norm_back(grad, normed_two, factor_two, gain_two)
    gain_two_grad, shift_two_grad = columns(grad * normed_two), columns(grad)
    dfeed = dz2.astype(BF)
    down_bias_grad = columns(dfeed.astype(F32))
    dhidden = dz2

    def keep(src, dst):
        c = pltpu.make_async_copy(src, dst, keep_sem.at[len(kept)])
        c.start()
        kept.append(c)

    for n in range(4):
        up = land1[:, :, D + n * D : 2 * D + n * D].reshape(D, D)
        down = land2[n * 8 : n * 8 + 8, :, :D].reshape(D, D)
        dupper = (dot_t(dfeed, down) * slope[n]).astype(BF)
        rows, cols = slice(n * 8, n * 8 + 8), slice(D + n * D, 2 * D + n * D)
        grad2[rows, :, :D] = dot_rows(act[n], dfeed).astype(BF).reshape(8, 96, D)
        grad2[rows, :, D:] = as_columns([columns(dupper.astype(F32))]).reshape(8, 96, 128)
        keep(grad2.at[pl.ds(n * 8, 8)], g2.at[pl.ds(n * 8, 8)])
        grad1[:, :, cols] = dot_rows(low, dupper).astype(BF).reshape(32, 24, D)
        keep(grad1.at[:, :, pl.ds(D + n * D, D)], g1.at[:, :, pl.ds(D + n * D, D)])
        dhidden += dot_t(dupper, up)
    dz1 = norm_back(dhidden, normed_one, factor_one, gain_one)
    dz1_ref[...] = dz1
    dbranch = dz1.astype(BF)
    for d in TURNS:
        to = (x + d) % 4
        do_slab[to] = dot_t(dbranch, ext[to]).astype(BF)
        if d:
            deliver(do_slab.at[to], do_land, x, (x + 4 - d) % 4, d_send.at[d], d_recv.at[d], peers[d - 1])
        else:
            do_land[x] = do_slab[x]
    for g in range(4):
        part = dot_rows(o_land[g], dbranch).astype(BF)
        grad1[g * 8 : g * 8 + 8, :, 0:D] = jnp.concatenate([part[0:128], part[192:256]], axis=0).reshape(8, 24, D)
    grad1[:, :, 3840:] = as_columns(
        [columns(dbranch.astype(F32)), columns(dhidden * normed_one), columns(dhidden),
         down_bias_grad, gain_two_grad, shift_two_grad]
    ).reshape(32, 24, 128)
    keep(grad1.at[:, :, pl.ds(0, D)], g1.at[:, :, pl.ds(0, D)])
    keep(grad1.at[:, :, pl.ds(3840, 128)], g1.at[:, :, pl.ds(3840, 128)])
    for got, ss, rr in copies:
        remote(got, got, ss, rr, sibling).wait_recv()
    for c in started:
        c.wait_send()
    for c in kept:
        c.wait()


EVENTS_SWAP, EVENTS_UNIT = 8, 1


def forward(*args):
    slab = (4, T, 256)
    return pl.pallas_call(
        forward_kernel,
        out_shape=(
            struct((T, D), BF), struct((T, D), F32), struct((32,) + WIDE[0], BF), struct(slab, BF), struct((8, T, 384), BF),
            struct(slab, BF), struct((4, T, 128), F32), struct(slab, BF),
            struct((32,) + WIDE[1], BF), struct((32,) + WIDE[2], BF), struct((4, T, D), BF),
        ),
        in_specs=[SM] * 2 + [VM] * 7,
        out_specs=(VM, VM, ANY, VM, VM, VM, VM, VM, ANY, ANY, ANY),
        scratch_shapes=[pltpu.VMEM((4,) + TALL[0], BF)] + [pltpu.VMEM(t, BF) for t in TALL[1:]]
        + [pltpu.VMEM((3,) + t, BF) for t in TALL]
        + [pltpu.VMEM(w, BF) for w in WIDE]
        + [pltpu.VMEM((32,) + w, BF) for w in WIDE]
        + [pltpu.VMEM((8, T, D), BF), pltpu.VMEM(slab, BF), pltpu.VMEM(slab, BF)]
        + [pltpu.VMEM((4, 256, D), BF), pltpu.VMEM((4, T, D), BF), pltpu.VMEM((4, T, D), F32)]
        + [pltpu.VMEM((32,) + w, BF) for w in WIDE[1:]]
        + [DMA((3, 3)), DMA((3, 3)), DMA((3,)), DMA((180,)), DMA((180,)), DMA((128,)), DMA((128,))]
        + [DMA((9,)), DMA((9,)), DMA((4,)), DMA((4,)), DMA((4,)), DMA((4,)), DMA((12,))],
        compiler_params=pltpu.CompilerParams(collective_id=0, has_side_effects=True, vmem_limit_bytes=62 << 20),
        name="forward",
    )(*args)


def scatter_events(routes, base, grads, acc, fro, buf, where, rings, sibling, sems, started):
    y, z, core = where
    load_sem, core_send, core_recv, send, recv = sems
    swaps, loads = {}, {}

    def spot(route, a, b):
        dy, dz = (a, b) if routes[route][0] == "yz" else (b, a)
        return dy, dz, dy * 4 + dz

    def begin():
        for b in TURNS:
            for a in TURNS:
                for r in BOTH:
                    dy, dz, at = spot(r, a, b)
                    here = block_of((y + dy) % 4, (z + dz) % 4, core)
                    there = block_of((y + dy) % 4, (z + dz) % 4, 1 - core)
                    for j, (k, first, cols) in enumerate(chunks_of(routes[r])):
                        n, view = (r * 16 + a * 4 + b) * 2 + j, pl.ds(first, cols)
                        m = n + base // 90 * 64
                        swaps[n] = remote(
                            grads[k].at[there, :, view], fro[k].at[at, :, view], core_send.at[m], core_recv.at[m], sibling
                        )
                        loads[n] = pltpu.make_async_copy(grads[k].at[here, :, view], acc[k].at[at, :, view], load_sem.at[m])
                        swaps[n].start()
                        loads[n].start()
                        started.append(swaps[n])

    def fold(r, a, b):
        _, _, at = spot(r, a, b)
        for j, (k, first, cols) in enumerate(chunks_of(routes[r])):
            n = (r * 16 + a * 4 + b) * 2 + j
            loads[n].wait()
            swaps[n].wait_recv()
            view = (at, slice(None), pl.ds(first, cols))
            acc[k][view] = acc[k][view] + fro[k][view]

    def slot(r, group, kind, i):
        return base + (r * 5 + group) * 9 + kind * 3 + (len(routes[r][1][0]) if i else 0)

    def axis(r, group):
        return rings[routes[r][0][0 if group == 0 else 1]]

    def at_of(r, group, step):
        return spot(r, *((step, 0) if group == 0 else (group - 1, step)))[2]

    def push(r, group, kind, i, step, who):
        for j, (k, first, cols) in enumerate(routes[r][1][i]):
            n, view = slot(r, group, kind, i) + j, pl.ds(first, cols)
            c = remote(
                acc[k].at[at_of(r, group, step), :, view], buf[k].at[group * 3 + kind, :, view], send.at[n], recv.at[n], who
            )
            c.start()
            started.append(c)

    def add(r, group, kind, i, step):
        for j, (k, first, cols) in enumerate(routes[r][1][i]):
            n, view = slot(r, group, kind, i) + j, pl.ds(first, cols)
            got = buf[k].at[group * 3 + kind, :, view]
            remote(got, got, send.at[n], recv.at[n], sibling).wait_recv()
            at = (at_of(r, group, step), slice(None), view)
            acc[k][at] = acc[k][at] + buf[k][group * 3 + kind, :, view]

    def one(r, group):
        right, left = axis(r, group)
        push(r, group, 0, 0, 2, right)
        push(r, group, 0, 1, 2, left)

    def two(r, group):
        right, left = axis(r, group)
        add(r, group, 0, 0, 1)
        push(r, group, 1, 0, 1, right)
        push(r, group, 1, 1, 1, right)
        add(r, group, 0, 1, 3)
        push(r, group, 2, 0, 3, left)
        push(r, group, 2, 1, 3, left)

    def three(r, group):
        for kind in (1, 2):
            for i in BOTH:
                add(r, group, kind, i, 0)

    events = []

    def event(*steps):
        events.append(lambda: [f(*args) for f, *args in steps])

    for a in TURNS:
        for r in BOTH:
            event((fold, r, a, 2), (one, r, 1 + a))
    for a in TURNS:
        for r in BOTH:
            event((fold, r, a, 1), (fold, r, a, 3), (two, r, 1 + a))
    for a in TURNS:
        for r in BOTH:
            more = {2: [(one, r, 0)], 3: [(two, r, 0)]}.get(a, [])
            event((fold, r, a, 0), (three, r, 1 + a), *more)
    for r in BOTH:
        event((three, r, 0))
    return begin, events


def backward_kernel(
    lengths, table, q_ref, kv_ref, do_ref, o_ref, lse_ref, dz1, group_tokens, w0, g1, g2, dx_ref, o0, o1, o2,
    wa, words, g0, a0, a1, a2, c0, c1, c2, b0, b1, b2, xs0, xs1, xs2, xr0, xr1, xr2, dx_slab, dx_land, kv_slab, kv_land,
    total, q_total, grads_low,
    load_sem, core_send, core_recv, send, recv, x_send, x_recv, dx_send, dx_recv, kv_send, kv_recv, w_sem,
):
    x, y, z, core = coords()
    side = z % 2
    mine = side * 4 + x
    grads, outs, acc, fro, buf = (g0, g1, g2), (o0, o1, o2), (a0, a1, a2), (c0, c1, c2), (b0, b1, b2)
    out_slabs, in_slabs = (xs0, xs1, xs2), (xr0, xr1, xr2)
    peers, rings, sibling = neighbours(x, y, z, core)
    partner = ident(x, y, z + 1 - 2 * side, core)
    fetch = [pltpu.make_async_copy(w0, wa, w_sem.at[0]), pltpu.make_async_copy(group_tokens, words, w_sem.at[1])]
    for c in fetch:
        c.start()
    greet(peers + rings["y"] + rings["z"] + [sibling])
    started, copies = [], []
    sems = (load_sem, core_send, core_recv, send, recv)
    begin_early, early = scatter_events(EARLY, 0, grads, acc, fro, buf, (y, z, core), rings, sibling, sems, started)
    begin_late, late = scatter_events(LATE, 90, grads, acc, fro, buf, (y, z, core), rings, sibling, sems, started)
    begin_late()

    def deliver(src, landing, to_slot, from_slot, ss, rr, who):
        c = remote(src, landing.at[to_slot], ss, rr, who)
        c.start()
        started.append(c)
        copies.append((landing.at[from_slot], ss, rr))

    first = head_lanes(0)
    swap = remote(kv_slab, kv_land, kv_send.at[0], kv_recv.at[0], partner)
    for part, which in enumerate((1 - side, side)):
        key_seg = jnp.concatenate([jnp.full((128, 1), seg_of(lengths, table, which * 8 + j), jnp.int32) for j in range(8)], axis=0)
        for turn, d in enumerate(TURNS):
            to = (x + d) % 4
            block = (side * 4 + to) * 2
            query_seg = jnp.concatenate([jnp.full((1, 128), seg_of(lengths, table, block + i), jnp.int32) for i in BOTH], axis=1)
            allowed = key_seg == query_seg
            logs = lse_ref[to].T
            parts = []
            for h in range(3):
                interleave(late, EVENTS_BACK)
                tile = h // 2 * 128
                cols = slice(tile, tile + 128)
                lanes = head_lanes(h)
                out_lanes = lanes if h < 2 else jnp.logical_not(lanes)
                q = jnp.where(lanes, q_ref[to, :, cols].astype(F32), 0.0).astype(BF)
                do = jnp.where(out_lanes, do_ref[to, :, cols].astype(F32), 0.0)
                inner = jnp.sum(do * o_ref[to, :, cols].astype(F32), axis=1, keepdims=True)
                inner = jnp.broadcast_to(inner, (T, 128)).T[0:1]
                do = do.astype(BF)
                k, v = key_value(kv_ref[pl.ds(which * 4, 4)], h)
                p = jnp.where(allowed, jnp.exp(dot_t(k, q) - logs[h : h + 1]), 0.0)
                ds = (p * (dot_t(v, do) - inner)).astype(BF)
                dk, dv = dot(ds, q), dot(p.astype(BF), do)
                if h < 2:
                    places = ((slice(0, 128), dk), (slice(128, 256), dv))
                else:
                    places = ((slice(256, 384), dk + dv),)
                for at, piece in places:
                    if turn == 0 and h in (0, 2):
                        total[:, at] = piece
                    else:
                        total[:, at] += piece
                parts.append(dot_rows(ds, k) * 0.125)
            for at, piece in (
                (slice(0, 128), jnp.where(first, parts[0], parts[1])), (slice(128, 256), jnp.where(first, parts[2], 0.0)),
            ):
                if part == 0:
                    q_total[to, :, at] = piece
                else:
                    grads_low[to, :, at] = (q_total[to, :, at] + piece).astype(BF)
        if part == 0:
            kv_slab[...] = total[...].astype(BF).reshape(4, T, 384)
            swap.start()
            started.append(swap)
    swap.wait_recv()
    for g in range(4):
        grads_low[g, :, 256:] = (total[g * T : g * T + T] + kv_land[g].astype(F32)).astype(BF)
    for c in fetch:
        c.wait()
    weight = wa[:, :, 0:640].reshape(D, 640)
    for d in TURNS:
        to = (x + d) % 4
        share = dot_t(grads_low[to], weight)
        if d:
            dx_slab[to] = share.astype(BF)
            deliver(dx_slab.at[to], dx_land, x, (x + 4 - d) % 4, dx_send.at[d], dx_recv.at[d], peers[d - 1])
        else:
            dx_ref[...] = dz1[...] + share
    grads_all = grads_low[...].reshape(4 * T, 640)
    g0[:, :, 0:640] = dot_rows(words[...].reshape(4 * T, D), grads_all).astype(BF).reshape(32, 24, 640)
    sums = columns(grads_all.astype(F32))
    bias = (sums[:, 0:192], jnp.concatenate([sums[:, 384:512], sums[:, 576:640]], axis=1))
    bias = [jnp.concatenate([jnp.where(x == g, b, 0.0) for g in range(4)], axis=1) for b in bias]
    g0[:, :, 640:] = as_columns(bias).reshape(32, 24, 128)
    begin_early()
    interleave(late, EVENTS_BACK_SWAP)
    for got, ss, rr in copies:
        remote(got, got, ss, rr, sibling).wait_recv()
    dx = dx_ref[...]
    for d in (1, 2, 3):
        dx += dx_land[(x + d) % 4].astype(F32)
    dx_ref[...] = dx

    def line_out(k):
        rows = ROWS[k]
        for d in (2, 1, 3):
            pick = picker((TALL[k][0], 4 * rows), rows, (x + d) % 4, True)
            out_slabs[k][d - 1] = dot(pick, acc[k][0]).astype(BF)
            c = remote(out_slabs[k].at[d - 1], in_slabs[k].at[d - 1], x_send.at[d - 1, k], x_recv.at[d - 1, k], peers[d - 1])
            c.start()
            started.append(c)
            x_copies.append((k, c))
        mine_rows = dot(picker((TALL[k][0], 4 * rows), rows, x, True), acc[k][0])
        if k:
            outs[k][...] = mine_rows
        else:
            xr0[3] = mine_rows.astype(BF)

    x_copies = []
    while late or early:
        interleave(late, 1)
        interleave(early, 1)
    line_out(1)
    line_out(2)
    line_out(0)
    for k, c in x_copies:
        c.wait_recv()
    for k in (1, 2):
        outs[k][...] += in_slabs[k][0].astype(F32) + in_slabs[k][1].astype(F32) + in_slabs[k][2].astype(F32)
    groups = []
    for g in range(4):
        groups.append(xr0[(x - g + 3) % 4].astype(F32))
    o0[:, 0 : 3 * D] = jnp.concatenate(
        [v[:, 0:192] for v in groups]
        + [p for v in groups for p in (v[:, 256:384], v[:, 512:576])]
        + [p for v in groups for p in (v[:, 384:512], v[:, 576:640])], axis=1
    )
    o0[:, 3 * D :] = groups[0][:, 640:] + groups[1][:, 640:] + groups[2][:, 640:] + groups[3][:, 640:]
    for c in started:
        c.wait_send()


EVENTS_BACK, EVENTS_BACK_SWAP = 1, 4


def backward(*args):
    return pl.pallas_call(
        backward_kernel,
        out_shape=(struct((T, D), F32), struct((16, 2432), F32)) + tuple(struct(t, F32) for t in TALL[1:]),
        in_specs=[SM] * 2 + [VM] * 6 + [ANY] * 4,
        out_specs=(VM,) * 4,
        scratch_shapes=[pltpu.VMEM((32,) + WIDE[0], BF), pltpu.VMEM((4, T, D), BF), pltpu.VMEM((32,) + WIDE[0], BF)]
        + [pltpu.VMEM((16,) + w, BF) for w in WIDE] * 2
        + [pltpu.VMEM((15,) + w, BF) for w in WIDE]
        + [pltpu.VMEM((3,) + t, BF) for t in TALL]
        + [pltpu.VMEM((4,) + TALL[0], BF)] + [pltpu.VMEM((3,) + t, BF) for t in TALL[1:]]
        + [pltpu.VMEM((4, T, D), BF)] * 2 + [pltpu.VMEM((4, T, 384), BF)] * 2
        + [pltpu.VMEM((4 * T, 384), F32), pltpu.VMEM((4, T, 256), F32), pltpu.VMEM((4, T, 640), BF)]
        + [DMA((128,)), DMA((128,)), DMA((128,)), DMA((180,)), DMA((180,)), DMA((3, 3)), DMA((3, 3))]
        + [DMA((4,)), DMA((4,)), DMA((1,)), DMA((1,)), DMA((2,))],
        compiler_params=pltpu.CompilerParams(collective_id=1, has_side_effects=True, vmem_limit_bytes=62 << 20),
        name="backward",
    )(*args)


def shards(
    tokens, lengths, block_table, qkv_weight, query_bias, value_bias, out_weight, out_bias, first_gain, first_shift,
    up_weight, up_bias, down_weight, down_bias, second_gain, second_shift, cotangent,
):
    vectors = jnp.zeros((128,), BF)
    at = 0
    for v in (query_bias, value_bias, out_bias, first_gain, first_shift, down_bias, second_gain, second_shift, up_bias):
        vectors += jnp.pad(v, (at, 128 - at - v.shape[0]))
        at += v.shape[0]
    vectors = vectors[None, :]
    result, dz1, w0, q, kv, o, lse, do, g1, g2, words = forward(
        lengths, block_table, qkv_weight, out_weight, up_weight, down_weight, vectors, tokens, cotangent
    )
    dx, ga, gb, gc = backward(lengths, block_table, q, kv, do, o, lse, dz1, words, w0, g1, g2)
    tail = gb[:6, 3840:3846]
    return (
        result, dx, ga[:6, : 3 * D], ga[:6, 3 * D], ga[:6, 3 * D + 1],
        gb[:6, :D], tail[:, 0], tail[:, 1], tail[:, 2],
        gb[:6, D:3840], gc[:24, D], gc[:24, :D], tail[:, 3], tail[:, 4], tail[:, 5],
    )


def solution(mesh):
    both = ("fsdp", "seq")
    whole, flat, group = P(both, None), P(both), P("fsdp", None)
    return jax.shard_map(
        shards,
        mesh=mesh,
        in_specs=(whole, group, group, whole, flat, flat, whole, flat, flat, flat, whole, flat, whole, flat, flat, flat, whole),
        out_specs=(whole, whole, whole, flat, flat, whole, flat, flat, flat, whole, flat, whole, flat, flat, flat),
        check_vma=False,
    )
```

```python
import jax
import jax.numpy as jnp
from jax import lax
from jax.experimental import pallas as pl
from jax.experimental.pallas import tpu as pltpu
from jax.sharding import PartitionSpec as P

MESH = pl.DeviceIdType.MESH
BF, F32 = jnp.bfloat16, jnp.float32
EPS = 1e-12
D, FF, T = 768, 3072, 256
NB, NC = 3968, 896
WIDE = ((24, D), (24, NB), (96, D))
SUMS = ((24, D), (24, NB), (96, NC))
SLAB = ((16, D), (16, 2048), (32, D))
SUM_SLAB = ((16, D), (16, 2048), (32, NC))
ROWS = (6, 6, 24)
MID = (
    ("yz", (((1, 0, 1024),), ((1, 1024, 1024),))),
    ("zy", (((1, 2048, 1024),), ((1, 3072, 896),))),
)
LATE = (
    ("yz", (((2, 0, 256),), ((2, 256, 128),))),
    ("zy", (((2, 384, 256),), ((2, 640, 128),))),
)
BACK_LATE = (
    ("yz", (((2, 0, 256),), ((1, 0, 1408),))),
    ("zy", (((1, 1408, 2560),), ((2, 256, 640),))),
)
BOTH = (0, 1)
TURNS = (2, 1, 3, 0)
ANY = pl.BlockSpec(memory_space=pl.ANY)
VM = pl.BlockSpec(memory_space=pltpu.VMEM)
SM = pl.BlockSpec(memory_space=pltpu.SMEM)
DMA = pltpu.SemaphoreType.DMA


def struct(shape, kind):
    return jax.ShapeDtypeStruct(shape, kind)


def whole_of(route):
    ((k, first, cols),), ((_, _, more),) = route[1]
    return ((k, first, cols + more),)


def chunks_of(route):
    return tuple(part for piece in route[1] for part in piece)


def coords():
    f, s = lax.axis_index("fsdp"), lax.axis_index("seq")
    return s % 4, (f // 2) % 4, (f // 8) * 2 + s // 4, f % 2


def ident(x, y, z, core):
    return {"fsdp": (z // 2) * 8 + y * 2 + core, "seq": (z % 2) * 4 + x}


def block_of(y, z, core):
    return (z // 2) * 16 + y * 4 + core * 2 + z % 2


def greet(partners):
    barrier = pltpu.get_barrier_semaphore()
    for who in partners:
        pl.semaphore_signal(barrier, inc=1, device_id=who, device_id_type=MESH)
    pl.semaphore_wait(barrier, len(partners))


def remote(src, dst, send, recv, who):
    return pltpu.make_async_remote_copy(
        src, dst, send, recv, device_id=who, device_id_type=MESH
    )


def dot(a, b):
    return jnp.dot(a, b, preferred_element_type=F32)


def dot_t(a, b):
    return lax.dot_general(a, b, (((1,), (1,)), ((), ())), preferred_element_type=F32)


def dot_rows(a, b):
    return lax.dot_general(a, b, (((0,), (0,)), ((), ())), preferred_element_type=F32)


def picker(shape, rows, at, transposed, base=0):
    i = lax.broadcasted_iota(jnp.int32, shape, 0)
    j = lax.broadcasted_iota(jnp.int32, shape, 1)
    if transposed:
        i, j = j, i
    j = j - base
    return jnp.where((i == at * rows + j) & (j >= 0) & (j < rows), 1.0, 0.0).astype(BF)


def plane(x, y, z, core):
    return {n: ident(x, (y + n // 4) % 4, (z + n % 4) % 4, core) for n in range(1, 16)}


def neighbours(x, y, z, core):
    peers = [ident((x + d) % 4, y, z, core) for d in (1, 2, 3)]
    rings = {
        "y": [ident(x, (y + d) % 4, z, core) for d in (1, 3)],
        "z": [ident(x, y, (z + d) % 4, core) for d in (1, 3)],
    }
    return peers, rings, ident(x, y, z, 1 - core)


def seg_of(lengths, table, j):
    place = table[0, j]
    end = lengths[0, 0]
    return (place >= end).astype(jnp.int32) + (place >= end + lengths[0, 1]).astype(jnp.int32)


def head_lanes(h):
    lane = lax.broadcasted_iota(jnp.int32, (1, 128), 1)
    return (lane < 64) if h % 2 == 0 else (lane >= 64)


def key_value(kv, h):
    rows = kv.shape[0] * T
    if h < 2:
        return kv[:, :, 0:128].reshape(rows, 128), kv[:, :, 128:256].reshape(rows, 128)
    both = kv[:, :, 256:384].reshape(rows, 128)
    return both, both


def interleave(events, count):
    for _ in range(min(count, len(events))):
        events.pop(0)()


def gather_events(routes, base, own, wide, where, rings, sibling, sems, started):
    y, z, core = where
    send, recv, core_send, core_recv = sems
    shared = []

    def place(route, a, b, c):
        dy, dz = (a, b) if routes[route][0] == "yz" else (b, a)
        return block_of((y + dy) % 4, (z + dz) % 4, c)

    def source(k, route, a, b):
        return own[k] if a == 0 and b == 0 else wide[k].at[place(route, a, b, core)]

    def push(route, i, a, b, who, sem):
        at = place(route, a, b, core)
        for j, (k, first, cols) in enumerate(routes[route][1][i]):
            view = pl.ds(first, cols)
            c = remote(source(k, route, a, b).at[:, view], wide[k].at[at, :, view], send.at[sem + j], recv.at[sem + j], who)
            c.start()
            started.append(c)

    def arrive(route, i, a, b, sem):
        for j, (k, first, cols) in enumerate(routes[route][1][i]):
            view = wide[k].at[place(route, a, b, core), :, pl.ds(first, cols)]
            remote(view, view, send.at[sem + j], recv.at[sem + j], sibling).wait_recv()

    def share(route, a, b):
        at = place(route, a, b, core)
        for k, first, cols in whole_of(routes[route]):
            n, view = base // 60 * 32 + len(shared), pl.ds(first, cols)
            c = remote(source(k, route, a, b).at[:, view], wide[k].at[at, :, view], core_send.at[n], core_recv.at[n], sibling)
            c.start()
            started.append(c)
            shared.append((n, route, a, b, k, view))

    def slot(route, group, kind, i):
        return base + (route * 5 + group) * 6 + kind * 2 + i

    def axis(route, group):
        return rings[routes[route][0][0 if group == 0 else 1]]

    def begin(route, group, a, b):
        for turn in BOTH:
            for i in BOTH:
                push(route, i, a, b, axis(route, group)[turn], slot(route, group, turn, i))

    def onward(route, group, turn, a, b):
        for i in BOTH:
            arrive(route, i, a, b, slot(route, group, turn, i))
        push(route, turn, a, b, axis(route, group)[turn], slot(route, group, 2, turn))

    def finish(route, group, a, b):
        for i in BOTH:
            arrive(route, i, a, b, slot(route, group, 2, i))

    events = []

    def event(*steps):
        events.append(lambda: [f(*args) for f, *args in steps])

    event(*[(begin, r, 0, 0, 0) for r in BOTH])
    event(*[(begin, r, 1, 0, 0) for r in BOTH], *[(share, r, 0, 0) for r in BOTH])
    for turn, a in ((0, 3), (1, 1)):
        for r in BOTH:
            event((onward, r, 0, turn, a, 0), (begin, r, 1 + a, a, 0), (share, r, a, 0))
    for turn, b in ((0, 3), (1, 1)):
        for r in BOTH:
            event((onward, r, 1, turn, 0, b), (share, r, 0, b))
    for r in BOTH:
        event((finish, r, 0, 2, 0), (begin, r, 3, 2, 0), (share, r, 2, 0))
    for a in (3, 1):
        for turn, b in ((0, 3), (1, 1)):
            for r in BOTH:
                event((onward, r, 1 + a, turn, a, b), (share, r, a, b))
    for r in BOTH:
        event((finish, r, 1, 0, 2), (share, r, 0, 2))
    for turn, b in ((0, 3), (1, 1)):
        for r in BOTH:
            event((onward, r, 3, turn, 2, b), (share, r, 2, b))
    for a in (3, 1, 2):
        for r in BOTH:
            event((finish, r, 1 + a, a, 2), (share, r, a, 2))

    def settle():
        for n, route, a, b, k, view in shared:
            got = wide[k].at[place(route, a, b, 1 - core), :, view]
            remote(got, got, core_send.at[n], core_recv.at[n], sibling).wait_recv()

    events.append(settle)
    return events


def normalize(v):
    centered = v - jnp.mean(v, axis=-1, keepdims=True)
    factor = lax.rsqrt(jnp.mean(centered * centered, axis=-1, keepdims=True) + EPS)
    return centered * factor, factor


def norm_back(grad, normed, factor, gain):
    scaled = grad * gain
    inner = jnp.mean(scaled * normed, axis=-1, keepdims=True)
    return factor * (scaled - jnp.mean(scaled, axis=-1, keepdims=True) - normed * inner)


def columns(v):
    return jnp.sum(v, axis=0, keepdims=True)


def as_columns(rows):
    wide = [jnp.zeros((128 - len(rows), D), F32)]
    return jnp.concatenate(rows + wide, axis=0).T.astype(BF)


def eye(rows, cols):
    i = lax.broadcasted_iota(jnp.int32, (rows, cols), 0)
    j = lax.broadcasted_iota(jnp.int32, (rows, cols), 1)
    return jnp.where(i == j, 1.0, 0.0).astype(BF)


def pack_slabs(qkv_w, out_w, up_w, down_w, vectors, slabs):
    s0, s1, s2 = slabs
    spread = eye(16, 6)
    i = lax.broadcasted_iota(jnp.int32, (16, 6), 0)
    j = lax.broadcasted_iota(jnp.int32, (16, 6), 1)
    below = jnp.where(i == j + 8, 1.0, 0.0).astype(BF)
    rows = dot(spread, qkv_w[...])
    lane = lax.broadcasted_iota(jnp.int32, (16, 128), 1)
    row = lax.broadcasted_iota(jnp.int32, (16, 128), 0)
    flat = jnp.broadcast_to(vectors[...].astype(F32), (16, 128))
    i = lax.broadcasted_iota(jnp.int32, (128, 128), 0)
    j = lax.broadcasted_iota(jnp.int32, (128, 128), 1)

    def place(base, picks):
        r = row - base
        mine = ((lane < 48) & (lane % 6 == r) & (r >= 0) & (r < 6)) | ((lane >= 48) & (lane < 72) & ((lane - 48) // 4 == r))
        return dot(jnp.where(mine, flat, 0.0).astype(BF), jnp.where(picks, 1.0, 0.0).astype(BF))

    biases = place(0, (i // 6 == j) & (j < 2)).astype(BF)
    for g in range(4):
        q, k, v = (rows[:, n * D + g * 192 : n * D + g * 192 + 192] for n in range(3))
        s0[g, :, 0:640] = jnp.concatenate(
            [q, jnp.zeros((16, 64), F32), k[:, 0:128], v[:, 0:128], k[:, 128:192], v[:, 128:192]], axis=1
        ).astype(BF)
        s0[g, :, 640:768] = biases
    s1[:, 0:D] = (dot(spread, out_w[...]) + dot(below, up_w[:, 1280:2048])).astype(BF)
    s1[:, D:1792] = (dot(spread, up_w[:, 0:1024]) + dot(below, up_w[:, 2048:3072])).astype(BF)
    rest = place(8, ((i < 48) & (i // 6 == j + 2) & (j < 6)) | ((i >= 48) & (j == 8 + i % 4)))
    s1[:, 1792:1920] = (dot(spread, up_w[:, 1024:1152]) + rest).astype(BF)
    s1[:, 1920:2048] = dot(spread, up_w[:, 1152:1280]).astype(BF)
    s2[...] = dot(eye(32, 24), down_w[...]).astype(BF)


def forward_kernel(
    lengths, table, qkv_w, out_w, up_w, down_w, vectors, tokens, cotangent,
    result_out, dz1_out, w0, q_out, kv_out, o_out, lse_out, do_out, g1, g2, group_tokens,
    result, dz1_ref, q_land, kv_land, o_slab, lse_ref, do_land,
    s0, s1, s2, x0, x1, x2, own0, own1, own2, land0, land1, land2, words, o_land, do_slab, part_out, part_stat,
    ext, act, slope, grad1, grad2,
    x_send, x_recv, put_sem, send, recv, core_send, core_recv, e_send, e_recv, e_core_send, e_core_recv, t_send, t_recv,
    o_send, o_recv, d_send, d_recv, keep_sem,
):
    x, y, z, core = coords()
    side = z % 2
    slabs, arrived, own, wide = (s0, s1, s2), (x0, x1, x2), (own0, own1, own2), (land0, land1, land2)
    peers, rings, sibling = neighbours(x, y, z, core)
    partner = ident(x, y, z + 1 - 2 * side, core)
    places = plane(x, y, z, core)
    pack_slabs(qkv_w, out_w, up_w, down_w, vectors, slabs)
    greet(peers + list(places.values()) + [sibling])
    started, x_copies = [], {}

    def token_send(src, at, who, n, part=slice(None)):
        c = remote(src.at[part], words.at[at].at[part], t_send.at[n], t_recv.at[n], who)
        c.start()
        started.append(c)

    def token_wait(at, n, part=slice(None)):
        view = words.at[at].at[part]
        remote(view, view, t_send.at[n], t_recv.at[n], sibling).wait_recv()

    right, left = peers[0], peers[2]
    halves = (pl.ds(0, T // 2), pl.ds(T // 2, T // 2))

    def line_tokens(src, which, n):
        token_send(src, which * 4 + x, right, n)
        token_send(src, which * 4 + x, left, n + 1)

    def line_onward(which, n):
        before, after = which * 4 + (x + 3) % 4, which * 4 + (x + 1) % 4
        token_wait(before, n)
        token_send(words.at[before], before, right, n + 2, halves[0])
        token_wait(after, n + 1)
        token_send(words.at[after], after, left, n + 3, halves[1])

    def line_finish(which, n):
        for i in BOTH:
            token_wait(which * 4 + (x + 2) % 4, n + 2 + i, halves[i])

    mine = side * 4 + x
    beyond = (1 - side) * 4 + x

    def send_slab(k):
        for d in (1, 3, 2):
            src = slabs[0].at[(x + d) % 4] if k == 0 else slabs[k]
            c = remote(src, arrived[k].at[d - 1], x_send.at[d - 1, k], x_recv.at[d - 1, k], peers[d - 1])
            c.start()
            x_copies[k, d] = c
            started.append(c)

    for k in range(3):
        send_slab(k)
    token_send(tokens, mine, partner, 0)
    words[mine] = tokens[...]
    me = block_of(y, z, core)
    puts = [pltpu.make_async_copy(own[k], wide[k].at[me], put_sem.at[k]) for k in range(3)]

    def line(k):
        rows = ROWS[k]
        for d in (1, 3, 2):
            x_copies[k, d].wait_recv()
        shape = (4 * rows, SLAB[k][0])
        for base, first, cols in ((0, 0, 2048), (8, 2048, 1920)) if k == 1 else ((0, 0, D),):
            total = jnp.zeros((4 * rows, cols), F32)
            for d in range(4):
                slab = arrived[k][d - 1, :, 0:cols] if d else slabs[0][x] if k == 0 else slabs[k][:, 0:cols]
                total += dot(picker(shape, rows, (x + 4 - d) % 4, False, base), slab)
            own[k][:, first : first + cols] = total.astype(BF)
        puts[k].start()

    sems = (send, recv, core_send, core_recv)
    mid, late = (
        gather_events(routes, 60 * n, own, wide, (y, z, core), rings, sibling, sems, started)
        for n, routes in enumerate((MID, LATE))
    )

    def share_first(n, src, at):
        c = remote(src, land0.at[at], e_core_send.at[n], e_core_recv.at[n], sibling)
        c.start()
        started.append(c)

    line(0)
    for n, who in places.items():
        c = remote(own0, land0.at[me], e_send.at[n], e_recv.at[n], who)
        c.start()
        started.append(c)
    share_first(0, own0, me)
    line(1)
    interleave(mid, 2)
    line(2)
    line_tokens(tokens, side, 1)
    for n in places:
        at = block_of((y + 4 - n // 4) % 4, (z + 4 - n % 4) % 4, core)
        view = land0.at[at]
        remote(view, view, e_send.at[n], e_recv.at[n], sibling).wait_recv()
        share_first(n, view, at)
    interleave(mid, 2)
    for n in range(16):
        view = land0.at[block_of((y + 4 - n // 4) % 4, (z + 4 - n % 4) % 4, 1 - core)]
        remote(view, view, e_core_send.at[n], e_core_recv.at[n], sibling).wait_recv()
    puts[0].wait()
    kept = [pltpu.make_async_copy(land0, w0, keep_sem.at[0])]
    kept[0].start()

    weight = land0[...].reshape(D, D)
    biases = weight[:, 640:].astype(F32).T
    query_bias = key_bias = jnp.zeros((1, 192), F32)
    for g in range(4):
        here = slice(g * 192, g * 192 + 192)
        query_bias = jnp.where(x == g, biases[0:1, here], query_bias)
        key_bias = jnp.where(x == g, biases[1:2, here], key_bias)
    none = jnp.zeros((1, 64), F32)
    query_bias = jnp.concatenate([query_bias, none], axis=1)
    key_bias = jnp.concatenate([none, none, key_bias[:, :128], none, key_bias[:, 128:]], axis=1)

    def project(at, with_query):
        if with_query:
            both = dot(words[at], weight[:, 0:640])
            q_land[at % 4] = ((both[:, :256] + query_bias).astype(BF).astype(F32) * 0.125).astype(BF)
            kv_land[at] = (both[:, 256:] + key_bias).astype(BF)
        else:
            kv_land[at] = (dot(words[at], weight[:, 256:640]) + key_bias).astype(BF)

    project(mine, True)
    interleave(mid, 2)
    line_onward(side, 1)
    token_wait(beyond, 0)
    line_tokens(words.at[beyond], 1 - side, 5)
    project(side * 4 + (x + 3) % 4, True)
    project(side * 4 + (x + 1) % 4, True)
    interleave(mid, 6)
    interleave(late, 2)
    project(beyond, False)
    line_finish(side, 1)
    project(side * 4 + (x + 2) % 4, True)

    def keep(src, dst):
        c = pltpu.make_async_copy(src, dst, keep_sem.at[len(kept)])
        c.start()
        kept.append(c)

    keep(q_land, q_out)
    copies = []

    def deliver(src, landing, to_slot, from_slot, ss, rr, who):
        c = remote(src, landing.at[to_slot], ss, rr, who)
        c.start()
        started.append(c)
        copies.append((landing.at[from_slot], ss, rr))

    first = head_lanes(0)
    lane = lax.broadcasted_iota(jnp.int32, (1, 128), 1)

    def attend(part, which, events):
        key_seg = jnp.concatenate(
            [jnp.full((1, 128), seg_of(lengths, table, which * 8 + j), jnp.int32) for j in range(8)], axis=1
        )
        for d in TURNS:
            to = (x + d) % 4
            block = (side * 4 + to) * 2
            query_seg = jnp.concatenate([jnp.full((128, 1), seg_of(lengths, table, block + i), jnp.int32) for i in BOTH], axis=0)
            allowed = query_seg == key_seg
            outs, stats = [], []
            for h in range(3):
                interleave(events, 1)
                tile = h // 2 * 128
                q = jnp.where(head_lanes(h), q_land[to, :, tile : tile + 128].astype(F32), 0.0).astype(BF)
                k, v = key_value(kv_land[pl.ds(which * 4, 4)], h)
                s = jnp.where(allowed, dot_t(q, k), -1e30)
                top = jnp.max(s, axis=1, keepdims=True)
                e = jnp.exp(s - top)
                total = jnp.sum(e, axis=1, keepdims=True)
                out = dot(e.astype(BF), v)
                if part == 0:
                    part_out[to, h] = out
                    stats += [top, total]
                else:
                    top_was, total_was = part_stat[to, :, 2 * h : 2 * h + 1], part_stat[to, :, 2 * h + 1 : 2 * h + 2]
                    highest = jnp.maximum(top, top_was)
                    now, was = jnp.exp(top - highest), jnp.exp(top_was - highest)
                    total = total * now + total_was * was
                    outs.append((out * now + part_out[to, h] * was) / total)
                    stats.append(highest + jnp.log(total))
            table_of = jnp.zeros((T, 128), F32)
            for i, v in enumerate(stats):
                table_of = jnp.where(lane == i, v, table_of)
            if part == 0:
                part_stat[to] = table_of
                continue
            lse_ref[to] = table_of
            o_slab[to, :, 0:128] = jnp.where(first, outs[0], outs[1]).astype(BF)
            o_slab[to, :, 128:256] = jnp.where(first, 0.0, outs[2]).astype(BF)
            if d:
                deliver(o_slab.at[to], o_land, x, (x + 4 - d) % 4, o_send.at[d], o_recv.at[d], peers[d - 1])
            else:
                o_land[x] = o_slab[x]

    attend(0, side, mid)
    line_onward(1 - side, 5)
    project((1 - side) * 4 + (x + 3) % 4, False)
    project((1 - side) * 4 + (x + 1) % 4, False)
    interleave(mid, 100)
    interleave(late, 4)
    line_finish(1 - side, 5)
    project((1 - side) * 4 + (x + 2) % 4, False)
    keep(kv_land, kv_out)
    keep(words, group_tokens)
    attend(1, 1 - side, late)
    keep(o_slab, o_out)
    keep(lse_ref, lse_out)
    puts[1].wait()
    puts[2].wait()

    vecs = land1[:, :, 3840:].reshape(D, 128).astype(F32).T
    out_bias, gain_one, shift_one, down_bias, gain_two, shift_two = (vecs[i : i + 1] for i in range(6))
    i = lax.broadcasted_iota(jnp.int32, (192, D), 0)
    j = lax.broadcasted_iota(jnp.int32, (192, D), 1)
    stretch = jnp.where(i == j // 4, 1.0, 0.0).astype(BF)
    i = lax.broadcasted_iota(jnp.int32, (8, D), 0)
    j = lax.broadcasted_iota(jnp.int32, (8, D), 1)
    four = vecs[8:16].astype(BF)
    up_biases = [columns(jnp.where(i == j % 4, dot(four[:, n * 192 : n * 192 + 192], stretch), 0.0)) for n in range(4)]
    interleave(late, 4)
    for g in range(4):
        part = land1[g * 8 : g * 8 + 8, :, 0:D].reshape(192, D)
        ext[g, 0:128] = part[0:128]
        ext[g, 128:192] = jnp.zeros((64, D), BF)
        ext[g, 192:256] = part[128:192]
    for got, ss, rr in copies:
        remote(got, got, ss, rr, sibling).wait_recv()
    copies.clear()
    branch = dot(o_land[0], ext[0])
    for g in range(1, 4):
        branch += dot(o_land[g], ext[g])
    normed_one, factor_one = normalize(tokens[...].astype(F32) + (branch + out_bias))
    hidden = normed_one * gain_one + shift_one
    low = hidden.astype(BF)
    for n in range(4):
        up = land1[:, :, D + n * D : 2 * D + n * D].reshape(D, D)
        upper = dot(low, up) + up_biases[n]
        square = upper * upper
        t = jnp.tanh(0.7978845608028654 * (upper + 0.044715 * (square * upper)))
        half = 0.5 * (1.0 + t)
        slope[n] = half + 0.5 * upper * (1.0 - t * t) * (0.7978845608028654 * (1.0 + 3.0 * 0.044715 * square))
        act[n] = (upper * half).astype(BF)
        interleave(late, 3)
    interleave(late, 100)
    feed = jnp.zeros((T, D), F32)
    for n in range(4):
        feed += dot(act[n], land2[n * 8 : n * 8 + 8].reshape(D, D))
    normed_two, factor_two = normalize(hidden + (feed + down_bias))
    result[...] = (normed_two * gain_two + shift_two).astype(BF)
    keep(result, result_out)

    grad = cotangent[...].astype(F32)
    dz2 = norm_back(grad, normed_two, factor_two, gain_two)
    gain_two_grad, shift_two_grad = columns(grad * normed_two), columns(grad)
    dfeed = dz2.astype(BF)
    down_bias_grad = columns(dfeed.astype(F32))
    dhidden = dz2

    for n in range(4):
        up = land1[:, :, D + n * D : 2 * D + n * D].reshape(D, D)
        down = land2[n * 8 : n * 8 + 8].reshape(D, D)
        dupper = (dot_t(dfeed, down) * slope[n]).astype(BF)
        rows, cols = slice(n * 8, n * 8 + 8), slice(D + n * D, 2 * D + n * D)
        grad2[rows, :, :D] = dot_rows(act[n], dfeed).astype(BF).reshape(8, 96, D)
        grad2[rows, :, D:] = as_columns([columns(dupper.astype(F32))]).reshape(8, 96, 128)
        keep(grad2.at[pl.ds(n * 8, 8)], g2.at[pl.ds(n * 8, 8)])
        grad1[:, :, cols] = dot_rows(low, dupper).astype(BF).reshape(32, 24, D)
        keep(grad1.at[:, :, pl.ds(D + n * D, D)], g1.at[:, :, pl.ds(D + n * D, D)])
        dhidden += dot_t(dupper, up)
    dz1 = norm_back(dhidden, normed_one, factor_one, gain_one)
    dz1_ref[...] = dz1
    keep(dz1_ref, dz1_out)
    dbranch = dz1.astype(BF)
    for d in TURNS:
        to = (x + d) % 4
        do_slab[to] = dot_t(dbranch, ext[to]).astype(BF)
        if d:
            deliver(do_slab.at[to], do_land, x, (x + 4 - d) % 4, d_send.at[d], d_recv.at[d], peers[d - 1])
        else:
            do_land[x] = do_slab[x]
    for g in range(4):
        part = dot_rows(o_land[g], dbranch).astype(BF)
        grad1[g * 8 : g * 8 + 8, :, 0:D] = jnp.concatenate([part[0:128], part[192:256]], axis=0).reshape(8, 24, D)
    grad1[:, :, 3840:] = as_columns(
        [columns(dbranch.astype(F32)), columns(dhidden * normed_one), columns(dhidden),
         down_bias_grad, gain_two_grad, shift_two_grad]
    ).reshape(32, 24, 128)
    keep(grad1.at[:, :, pl.ds(0, D)], g1.at[:, :, pl.ds(0, D)])
    keep(grad1.at[:, :, pl.ds(3840, 128)], g1.at[:, :, pl.ds(3840, 128)])
    for got, ss, rr in copies:
        remote(got, got, ss, rr, sibling).wait_recv()
    keep(do_land, do_out)
    for c in started:
        c.wait_send()
    for c in kept:
        c.wait()


def forward(*args):
    slab = (4, T, 256)
    return pl.pallas_call(
        forward_kernel,
        out_shape=(
            struct((T, D), BF), struct((T, D), F32), struct((32,) + WIDE[0], BF), struct(slab, BF), struct((8, T, 384), BF),
            struct(slab, BF), struct((4, T, 128), F32), struct(slab, BF),
            struct((32,) + SUMS[1], BF), struct((32,) + SUMS[2], BF), struct((8, T, D), BF),
        ),
        in_specs=[SM] * 2 + [VM] * 7,
        out_specs=(ANY,) * 11,
        scratch_shapes=[pltpu.VMEM((T, D), BF), pltpu.VMEM((T, D), F32), pltpu.VMEM(slab, BF), pltpu.VMEM((8, T, 384), BF)]
        + [pltpu.VMEM(slab, BF), pltpu.VMEM((4, T, 128), F32), pltpu.VMEM(slab, BF)]
        + [pltpu.VMEM((4,) + SLAB[0], BF)] + [pltpu.VMEM(t, BF) for t in SLAB[1:]]
        + [pltpu.VMEM((3,) + t, BF) for t in SLAB]
        + [pltpu.VMEM(w, BF) for w in WIDE]
        + [pltpu.VMEM((32,) + w, BF) for w in WIDE]
        + [pltpu.VMEM((8, T, D), BF), pltpu.VMEM(slab, BF), pltpu.VMEM(slab, BF)]
        + [pltpu.VMEM((4, 3, T, 128), F32), pltpu.VMEM((4, T, 128), F32)]
        + [pltpu.VMEM((4, 256, D), BF), pltpu.VMEM((4, T, D), BF), pltpu.VMEM((4, T, D), F32)]
        + [pltpu.VMEM((32,) + w, BF) for w in SUMS[1:]]
        + [DMA((3, 3)), DMA((3, 3)), DMA((3,)), DMA((120,)), DMA((120,)), DMA((64,)), DMA((64,))]
        + [DMA((16,))] * 4
        + [DMA((9,)), DMA((9,)), DMA((4,)), DMA((4,)), DMA((4,)), DMA((4,)), DMA((24,))],
        compiler_params=pltpu.CompilerParams(collective_id=0, has_side_effects=True, vmem_limit_bytes=62 << 20),
        name="forward",
    )(*args)


def scatter_events(routes, grads, acc, fro, buf, where, rings, sibling, sems, started):
    y, z, core = where
    load_sem, core_send, core_recv, send, recv = sems
    moves, waited = {}, set()

    def spot(route, a, b):
        dy, dz = (a, b) if routes[route][0] == "yz" else (b, a)
        return dy, dz, dy * 4 + dz

    def begin():
        for r, a, b in [(r, a, b) for b in TURNS for a in TURNS for r in BOTH]:
            dy, dz, at = spot(r, a, b)
            if at in moves:
                continue
            here = block_of((y + dy) % 4, (z + dz) % 4, core)
            there = block_of((y + dy) % 4, (z + dz) % 4, 1 - core)
            moves[at] = []
            for k in (1, 2):
                n = at * 2 + k - 1
                swap = remote(grads[k].at[there], fro[k].at[at], core_send.at[n], core_recv.at[n], sibling)
                load = pltpu.make_async_copy(grads[k].at[here], acc[k].at[at], load_sem.at[n])
                swap.start()
                load.start()
                started.append(swap)
                moves[at].append((load, swap))

    def fold(r, a, b):
        _, _, at = spot(r, a, b)
        if at not in waited:
            waited.add(at)
            for load, swap in moves[at]:
                load.wait()
                swap.wait_recv()
        for k, first, cols in chunks_of(routes[r]):
            view = (at, slice(None), pl.ds(first, cols))
            acc[k][view] = acc[k][view] + fro[k][view]

    def slot(r, group, kind, i):
        return (r * 5 + group) * 9 + kind * 3 + (len(routes[r][1][0]) if i else 0)

    def axis(r, group):
        return rings[routes[r][0][0 if group == 0 else 1]]

    def at_of(r, group, step):
        return spot(r, *((step, 0) if group == 0 else (group - 1, step)))[2]

    def push(r, group, kind, i, step, who):
        for j, (k, first, cols) in enumerate(routes[r][1][i]):
            n, view = slot(r, group, kind, i) + j, pl.ds(first, cols)
            c = remote(
                acc[k].at[at_of(r, group, step), :, view], buf[k].at[group * 3 + kind, :, view], send.at[n], recv.at[n], who
            )
            c.start()
            started.append(c)

    def add(r, group, kind, i, step):
        for j, (k, first, cols) in enumerate(routes[r][1][i]):
            n, view = slot(r, group, kind, i) + j, pl.ds(first, cols)
            got = buf[k].at[group * 3 + kind, :, view]
            remote(got, got, send.at[n], recv.at[n], sibling).wait_recv()
            at = (at_of(r, group, step), slice(None), view)
            acc[k][at] = acc[k][at] + buf[k][group * 3 + kind, :, view]

    def one(r, group):
        right, left = axis(r, group)
        push(r, group, 0, 0, 2, right)
        push(r, group, 0, 1, 2, left)

    def two(r, group):
        right, left = axis(r, group)
        add(r, group, 0, 0, 1)
        push(r, group, 1, 0, 1, right)
        push(r, group, 1, 1, 1, right)
        add(r, group, 0, 1, 3)
        push(r, group, 2, 0, 3, left)
        push(r, group, 2, 1, 3, left)

    def three(r, group):
        for kind in (1, 2):
            for i in BOTH:
                add(r, group, kind, i, 0)

    events = []

    def event(*steps):
        events.append(lambda: [f(*args) for f, *args in steps])

    for a in TURNS:
        for r in BOTH:
            event((fold, r, a, 2), (one, r, 1 + a))
    for a in TURNS:
        for r in BOTH:
            event((fold, r, a, 1), (fold, r, a, 3), (two, r, 1 + a))
    for a in TURNS:
        for r in BOTH:
            more = {2: [(one, r, 0)], 3: [(two, r, 0)]}.get(a, [])
            event((fold, r, a, 0), (three, r, 1 + a), *more)
    for r in BOTH:
        event((three, r, 0))
    return begin, events


def backward_kernel(
    lengths, table, q_in, kv_in, do_in, o_in, lse_in, dz1_in, group_tokens, w0, g1, g2, dx_ref, o0, o1, o2,
    q_ref, kv_ref, do_ref, o_ref, lse_ref, dz1, wa, words, g0, a0, a1, a2, c0, c1, c2, b0, b1, b2, xs0, xs1, xs2, xr0, xr1, xr2, dx_slab, dx_land, kv_slab, kv_land,
    total, q_total, grads_low,
    load_sem, core_send, core_recv, send, recv, e_send, e_recv, e_core_send, e_core_recv, x_send, x_recv, dx_send, dx_recv, kv_send, kv_recv, w_sem,
):
    x, y, z, core = coords()
    side = z % 2
    mine = side * 4 + x
    grads, outs, acc, fro, buf = (g0, g1, g2), (o0, o1, o2), (a0, a1, a2), (c0, c1, c2), (b0, b1, b2)
    out_slabs, in_slabs = (xs0, xs1, xs2), (xr0, xr1, xr2)
    peers, rings, sibling = neighbours(x, y, z, core)
    partner = ident(x, y, z + 1 - 2 * side, core)
    first_in, fetch = [], []
    for src, dst, cuts in (
        (q_in, q_ref, (0, 128, 256)), (kv_in, kv_ref, (0, 128, 256, 384)), (do_in, do_ref, (0, 128, 256)),
        (o_in, o_ref, (0, 128, 256)), (lse_in, lse_ref, (0, 128)),
    ):
        for at, end in zip(cuts, cuts[1:]):
            view = pl.ds(at, end - at)
            first_in.append(pltpu.make_async_copy(src.at[:, :, view], dst.at[:, :, view], w_sem.at[len(first_in)]))
            first_in[-1].start()
    places = plane(x, y, z, core)
    greet(peers + list(places.values()) + [sibling])
    started, copies = [], []
    sems = (load_sem, core_send, core_recv, send, recv)
    begin_late, late = scatter_events(BACK_LATE, grads, acc, fro, buf, (y, z, core), rings, sibling, sems, started)
    begin_late()
    for n, (src, dst) in enumerate(((w0, wa), (group_tokens, words), (dz1_in, dz1))):
        fetch.append(pltpu.make_async_copy(src, dst, w_sem.at[len(first_in) + n]))
        fetch[-1].start()
    for c in first_in:
        c.wait()

    def deliver(src, landing, to_slot, from_slot, ss, rr, who):
        c = remote(src, landing.at[to_slot], ss, rr, who)
        c.start()
        started.append(c)
        copies.append((landing.at[from_slot], ss, rr))

    first = head_lanes(0)
    swap = remote(kv_slab, kv_land, kv_send.at[0], kv_recv.at[0], partner)
    for part, which in enumerate((1 - side, side)):
        key_seg = jnp.concatenate([jnp.full((128, 1), seg_of(lengths, table, which * 8 + j), jnp.int32) for j in range(8)], axis=0)
        for turn, d in enumerate(TURNS):
            to = (x + d) % 4
            block = (side * 4 + to) * 2
            query_seg = jnp.concatenate([jnp.full((1, 128), seg_of(lengths, table, block + i), jnp.int32) for i in BOTH], axis=1)
            allowed = key_seg == query_seg
            logs = lse_ref[to].T
            parts = []
            for h in range(3):
                interleave(late, BACK_PLAN[part * 12 + turn * 3 + h])
                tile = h // 2 * 128
                cols = slice(tile, tile + 128)
                lanes = head_lanes(h)
                out_lanes = lanes if h < 2 else jnp.logical_not(lanes)
                q = jnp.where(lanes, q_ref[to, :, cols].astype(F32), 0.0).astype(BF)
                do = jnp.where(out_lanes, do_ref[to, :, cols].astype(F32), 0.0)
                inner = jnp.sum(do * o_ref[to, :, cols].astype(F32), axis=1, keepdims=True)
                inner = jnp.broadcast_to(inner, (T, 128)).T[0:1]
                do = do.astype(BF)
                k, v = key_value(kv_ref[pl.ds(which * 4, 4)], h)
                p = jnp.where(allowed, jnp.exp(dot_t(k, q) - logs[h : h + 1]), 0.0)
                ds = (p * (dot_t(v, do) - inner)).astype(BF)
                dk, dv = dot(ds, q), dot(p.astype(BF), do)
                if h < 2:
                    targets = ((slice(0, 128), dk), (slice(128, 256), dv))
                else:
                    targets = ((slice(256, 384), dk + dv),)
                for at, piece in targets:
                    if turn == 0 and h in (0, 2):
                        total[:, at] = piece
                    else:
                        total[:, at] += piece
                parts.append(dot_rows(ds, k) * 0.125)
            for at, piece in (
                (slice(0, 128), jnp.where(first, parts[0], parts[1])), (slice(128, 256), jnp.where(first, parts[2], 0.0)),
            ):
                if part == 0:
                    q_total[to, :, at] = piece
                else:
                    grads_low[to, :, at] = (q_total[to, :, at] + piece).astype(BF)
        if part == 0:
            kv_slab[...] = total[...].astype(BF).reshape(4, T, 384)
            swap.start()
            started.append(swap)
    for c in fetch:
        c.wait()
    own_part = total[...].astype(BF)
    for at, piece in (
        (slice(0, 256), dot_rows(words[pl.ds(side * 4, 4)].reshape(4 * T, D), grads_low[:, :, 0:256].reshape(4 * T, 256))),
        (slice(256, 640), dot_rows(words[pl.ds(side * 4, 4)].reshape(4 * T, D), own_part)
         + dot_rows(words[pl.ds(4 - side * 4, 4)].reshape(4 * T, D), kv_slab[...].reshape(4 * T, 384))),
    ):
        g0[:, :, at] = piece.astype(BF).reshape(32, 24, at.stop - at.start)
    q_sums = columns(grads_low[:, :, 0:256].reshape(4 * T, 256).astype(F32))
    kv_sums = columns(own_part.astype(F32)) + columns(kv_slab[...].reshape(4 * T, 384).astype(F32))
    bias = (q_sums[:, 0:192], jnp.concatenate([kv_sums[:, 128:256], kv_sums[:, 320:384]], axis=1))
    bias = [jnp.concatenate([jnp.where(x == g, b, 0.0) for g in range(4)], axis=1) for b in bias]
    g0[:, :, 640:] = as_columns(bias).reshape(32, 24, 128)
    folds = {}
    for n in list(places) + [0]:
        there = block_of((y + n // 4) % 4, (z + n % 4) % 4, 1 - core)
        folds[n] = remote(g0.at[there], c0.at[n], e_core_send.at[n], e_core_recv.at[n], sibling)
        folds[n].start()
        started.append(folds[n])
    interleave(late, 2)
    for n in list(places) + [0]:
        folds[n].wait_recv()
        a0[n] = g0[block_of((y + n // 4) % 4, (z + n % 4) % 4, core)] + c0[n]
        if n:
            c = remote(a0.at[n], b0.at[n], e_send.at[n], e_recv.at[n], places[n])
            c.start()
            started.append(c)
    interleave(late, LATE_BEFORE_SHARE)
    swap.wait_recv()
    for g in range(4):
        grads_low[g, :, 256:] = (total[g * T : g * T + T] + kv_land[g].astype(F32)).astype(BF)
    weight = wa[:, :, 0:640].reshape(D, 640)
    for d in TURNS:
        to = (x + d) % 4
        share = dot_t(grads_low[to], weight)
        if d:
            dx_slab[to] = share.astype(BF)
            deliver(dx_slab.at[to], dx_land, x, (x + 4 - d) % 4, dx_send.at[d], dx_recv.at[d], peers[d - 1])
        else:
            dx_ref[...] = dz1[...] + share

    def line_out(k):
        rows = ROWS[k]
        shape = (SUM_SLAB[k][0], 4 * rows)

        def slab(at):
            if k != 1:
                return dot(picker(shape, rows, at, True), acc[k][0])
            upper, lower = picker(shape, rows, at, True), picker(shape, rows, at, True, 8)
            rest = jnp.concatenate([acc[1][0, :, 2048:NB], jnp.zeros((24, 128), BF)], axis=1)
            return dot(upper, acc[1][0, :, 0:2048]) + dot(lower, rest)

        for d in (2, 1, 3):
            out_slabs[k][d - 1] = slab((x + d) % 4).astype(BF)
            c = remote(out_slabs[k].at[d - 1], in_slabs[k].at[d - 1], x_send.at[d - 1, k], x_recv.at[d - 1, k], peers[d - 1])
            c.start()
            started.append(c)
            x_copies[k].append(c)
        in_slabs[k][3] = slab(x).astype(BF)

    def gathered(k):
        for c in x_copies[k]:
            c.wait_recv()
        return [in_slabs[k][i].astype(F32) for i in range(4)]

    x_copies = {0: [], 1: [], 2: []}
    interleave(late, 100)
    line_out(1)
    line_out(2)
    first_sum = a0[0].astype(F32)
    for n in places:
        remote(b0.at[n], b0.at[n], e_send.at[n], e_recv.at[n], sibling).wait_recv()
        first_sum += b0[n].astype(F32)
    a0[0] = first_sum.astype(BF)
    line_out(0)
    one, two, three, four = gathered(1)
    both = one + two + three + four
    o1[:, 0:2048] = both[0:8]
    o1[:, 2048:NB] = both[8:16, 0:1920]
    one, two, three, four = gathered(2)
    o2[...] = (one + two + three + four)[0:24]
    for got, ss, rr in copies:
        remote(got, got, ss, rr, sibling).wait_recv()
    dx = dx_ref[...]
    for d in (1, 2, 3):
        dx += dx_land[(x + d) % 4].astype(F32)
    dx_ref[...] = dx
    gathered(0)
    groups = []
    for g in range(4):
        groups.append(xr0[(x - g + 3) % 4].astype(F32))
    groups = [v[0:8] for v in groups]
    o0[:, 0 : 3 * D] = jnp.concatenate(
        [v[:, 0:192] for v in groups]
        + [p for v in groups for p in (v[:, 256:384], v[:, 512:576])]
        + [p for v in groups for p in (v[:, 384:512], v[:, 576:640])], axis=1
    )
    o0[:, 3 * D :] = groups[0][:, 640:] + groups[1][:, 640:] + groups[2][:, 640:] + groups[3][:, 640:]
    for c in started:
        c.wait_send()


BACK_PLAN = (2, 2, 2, 2, 0, 1, 1, 1, 1, 1, 1, 1, 1, 0, 0, 0, 0, 1, 0, 1, 0, 1, 0, 1)
LATE_BEFORE_SHARE = 2


def backward(*args):
    return pl.pallas_call(
        backward_kernel,
        out_shape=(struct((T, D), F32), struct((8, 2432), F32), struct((8, NB), F32), struct((24, NC), F32)),
        in_specs=[SM] * 2 + [ANY] * 10,
        out_specs=(VM,) * 4,
        scratch_shapes=[pltpu.VMEM((4, T, 256), BF), pltpu.VMEM((8, T, 384), BF), pltpu.VMEM((4, T, 256), BF)]
        + [pltpu.VMEM((4, T, 256), BF), pltpu.VMEM((4, T, 128), F32), pltpu.VMEM((T, D), F32)]
        + [pltpu.VMEM((32,) + WIDE[0], BF), pltpu.VMEM((8, T, D), BF), pltpu.VMEM((32,) + WIDE[0], BF)]
        + [pltpu.VMEM((16,) + w, BF) for w in SUMS] * 2
        + [pltpu.VMEM((16,) + SUMS[0], BF)] + [pltpu.VMEM((15,) + w, BF) for w in SUMS[1:]]
        + [pltpu.VMEM((3,) + t, BF) for t in SUM_SLAB] + [pltpu.VMEM((4,) + t, BF) for t in SUM_SLAB]
        + [pltpu.VMEM((4, T, D), BF)] * 2 + [pltpu.VMEM((4, T, 384), BF)] * 2
        + [pltpu.VMEM((4 * T, 384), F32), pltpu.VMEM((4, T, 256), F32), pltpu.VMEM((4, T, 640), BF)]
        + [DMA((32,)), DMA((32,)), DMA((32,)), DMA((90,)), DMA((90,))] + [DMA((16,))] * 4 + [DMA((3, 3)), DMA((3, 3))]
        + [DMA((4,)), DMA((4,)), DMA((1,)), DMA((1,)), DMA((16,))],
        compiler_params=pltpu.CompilerParams(collective_id=1, has_side_effects=True, vmem_limit_bytes=62 << 20),
        name="backward",
    )(*args)


def unpack_kernel(o0, o1, o2, dx_in, low_in, low, dx, qkv, query, value, out, out_bias, gain_one, shift_one, up, up_bias,
                  down, down_bias, gain_two, shift_two):
    dx[...] = dx_in[...]
    low[...] = low_in[...]
    qkv[...] = o0[0:6, 0 : 3 * D]
    out[...] = o1[0:6, 0:D]
    up[...] = o1[0:6, D:3840]
    down[...] = o2[:, 0:D]
    first, second = o0[:, 3 * D :].T, o1[:, 3840:].T
    third = jnp.concatenate([o2[:, D:], jnp.zeros((104, 128), F32)], axis=0).T
    query[...], value[...] = first[0, 0:6], first[1, 0:6]
    for i, ref in enumerate((out_bias, gain_one, shift_one, down_bias, gain_two, shift_two)):
        ref[...] = second[i, 0:6]
    up_bias[...] = third[0, 0:24]


def unpack(*args):
    six = struct((6,), F32)
    return pl.pallas_call(
        unpack_kernel,
        out_shape=(
            struct((T, D), BF), struct((T, D), F32), struct((6, 3 * D), F32), six, six, struct((6, D), F32), six, six, six,
            struct((6, FF), F32), struct((24,), F32), struct((24, D), F32), six, six, six,
        ),
        in_specs=[VM] * 5,
        out_specs=(VM,) * 15,
        name="unpack",
    )(*args)


def shards(
    tokens, lengths, block_table, qkv_weight, query_bias, value_bias, out_weight, out_bias, first_gain, first_shift,
    up_weight, up_bias, down_weight, down_bias, second_gain, second_shift, cotangent,
):
    vectors = jnp.zeros((128,), BF)
    at = 0
    for v in (query_bias, value_bias, out_bias, first_gain, first_shift, down_bias, second_gain, second_shift, up_bias):
        vectors += jnp.pad(v, (at, 128 - at - v.shape[0]))
        at += v.shape[0]
    vectors = vectors[None, :]
    result, dz1, w0, q, kv, o, lse, do, g1, g2, words = forward(
        lengths, block_table, qkv_weight, out_weight, up_weight, down_weight, vectors, tokens, cotangent
    )
    dx, ga, gb, gc = backward(lengths, block_table, q, kv, do, o, lse, dz1, words, w0, g1, g2)
    return unpack(ga, gb, gc, dx, result)


def solution(mesh):
    both = ("fsdp", "seq")
    whole, flat, group = P(both, None), P(both), P("fsdp", None)
    return jax.shard_map(
        shards,
        mesh=mesh,
        in_specs=(whole, group, group, whole, flat, flat, whole, flat, flat, flat, whole, flat, whole, flat, flat, flat, whole),
        out_specs=(whole, whole, whole, flat, flat, whole, flat, flat, flat, whole, flat, whole, flat, flat, flat),
        check_vma=False,
    )
```

```python
import jax
import jax.numpy as jnp
from jax import lax
from jax.experimental import pallas as pl
from jax.experimental.pallas import tpu as pltpu
from jax.sharding import PartitionSpec as P

MESH = pl.DeviceIdType.MESH
BF, F32 = jnp.bfloat16, jnp.float32
EPS = 1e-12
D, FF, T = 768, 3072, 256
NB, NC = 3968, 896
WIDE = ((24, D), (24, NB), (96, D))
SUMS = ((24, D), (24, NB), (96, NC))
SLAB = ((16, D), (16, 2048), (32, D))
SUM_SLAB = ((16, D), (16, 2048), (32, NC))
ROWS = (6, 6, 24)
MID = (
    ("yz", (((1, 0, 768),), ((1, 768, 768),))),
    ("zy", (((1, 1536, 1280),), ((1, 2816, 1152),))),
)
LATE = (
    ("yz", (((2, 0, 128),), ((2, 128, 128),))),
    ("zy", (((2, 256, 256),), ((2, 512, 256),))),
)
BACK_LATE = (
    ("yz", (((2, 0, 256),), ((1, 0, 1408),))),
    ("zy", (((1, 1408, 2560),), ((2, 256, 640),))),
)
BOTH = (0, 1)
TURNS = (2, 1, 3, 0)
ANY = pl.BlockSpec(memory_space=pl.ANY)
VM = pl.BlockSpec(memory_space=pltpu.VMEM)
SM = pl.BlockSpec(memory_space=pltpu.SMEM)
DMA = pltpu.SemaphoreType.DMA


def struct(shape, kind):
    return jax.ShapeDtypeStruct(shape, kind)


def whole_of(route):
    ((k, first, cols),), ((_, _, more),) = route[1]
    return ((k, first, cols + more),)


def chunks_of(route):
    return tuple(part for piece in route[1] for part in piece)


def coords():
    f, s = lax.axis_index("fsdp"), lax.axis_index("seq")
    return s % 4, (f // 2) % 4, (f // 8) * 2 + s // 4, f % 2


def ident(x, y, z, core):
    return {"fsdp": (z // 2) * 8 + y * 2 + core, "seq": (z % 2) * 4 + x}


def block_of(y, z, core):
    return (z // 2) * 16 + y * 4 + core * 2 + z % 2


def greet(partners):
    barrier = pltpu.get_barrier_semaphore()
    for who in partners:
        pl.semaphore_signal(barrier, inc=1, device_id=who, device_id_type=MESH)
    pl.semaphore_wait(barrier, len(partners))


def remote(src, dst, send, recv, who):
    return pltpu.make_async_remote_copy(
        src, dst, send, recv, device_id=who, device_id_type=MESH
    )


def dot(a, b):
    return jnp.dot(a, b, preferred_element_type=F32)


def dot_t(a, b):
    return lax.dot_general(a, b, (((1,), (1,)), ((), ())), preferred_element_type=F32)


def dot_rows(a, b):
    return lax.dot_general(a, b, (((0,), (0,)), ((), ())), preferred_element_type=F32)


def picker(shape, rows, at, transposed, base=0):
    i = lax.broadcasted_iota(jnp.int32, shape, 0)
    j = lax.broadcasted_iota(jnp.int32, shape, 1)
    if transposed:
        i, j = j, i
    j = j - base
    return jnp.where((i == at * rows + j) & (j >= 0) & (j < rows), 1.0, 0.0).astype(BF)


def plane(x, y, z, core):
    return {n: ident(x, (y + n // 4) % 4, (z + n % 4) % 4, core) for n in range(1, 16)}


def neighbours(x, y, z, core):
    peers = [ident((x + d) % 4, y, z, core) for d in (1, 2, 3)]
    rings = {
        "y": [ident(x, (y + d) % 4, z, core) for d in (1, 3)],
        "z": [ident(x, y, (z + d) % 4, core) for d in (1, 3)],
    }
    return peers, rings, ident(x, y, z, 1 - core)


def seg_of(lengths, table, j):
    place = table[0, j]
    end = lengths[0, 0]
    return (place >= end).astype(jnp.int32) + (place >= end + lengths[0, 1]).astype(jnp.int32)


def head_lanes(h):
    lane = lax.broadcasted_iota(jnp.int32, (1, 128), 1)
    return (lane < 64) if h % 2 == 0 else (lane >= 64)


def key_value(kv, h):
    rows = kv.shape[0] * T
    if h < 2:
        return kv[:, :, 0:128].reshape(rows, 128), kv[:, :, 128:256].reshape(rows, 128)
    both = kv[:, :, 256:384].reshape(rows, 128)
    return both, both


def launch(started, make):
    make().start()
    started.append(make)


def planned(events, turn, plan):
    for t, count in enumerate(plan):
        if count and events:
            mine = [events.pop(0) for _ in range(min(count, len(events)))]
            pl.when(turn == t)(lambda mine=mine: [f() for f in mine] and None)


def offset_of(turn):
    return jnp.where(turn == 0, 2, jnp.where(turn == 1, 1, jnp.where(turn == 2, 3, 0)))


def interleave(events, count):
    for _ in range(min(count, len(events))):
        events.pop(0)()


def gather_events(routes, base, own, wide, where, rings, sibling, sems, started):
    y, z, core = where
    send, recv, core_send, core_recv = sems
    shared = []

    def place(route, a, b, c):
        dy, dz = (a, b) if routes[route][0] == "yz" else (b, a)
        return block_of((y + dy) % 4, (z + dz) % 4, c)

    def source(k, route, a, b):
        return own[k] if a == 0 and b == 0 else wide[k].at[place(route, a, b, core)]

    def push(route, i, a, b, who, sem):
        for j, (k, first, cols) in enumerate(routes[route][1][i]):
            view = pl.ds(first, cols)

            def make(k=k, view=view, n=sem + j):
                at = place(route, a, b, core)
                return remote(source(k, route, a, b).at[:, view], wide[k].at[at, :, view], send.at[n], recv.at[n], who)

            launch(started, make)

    def arrive(route, i, a, b, sem):
        for j, (k, first, cols) in enumerate(routes[route][1][i]):
            view = wide[k].at[place(route, a, b, core), :, pl.ds(first, cols)]
            remote(view, view, send.at[sem + j], recv.at[sem + j], sibling).wait_recv()

    def share(route, a, b):
        for k, first, cols in whole_of(routes[route]):
            n, view = base // 60 * 32 + len(shared), pl.ds(first, cols)

            def make(k=k, view=view, n=n):
                at = place(route, a, b, core)
                src = source(k, route, a, b).at[:, view]
                return remote(src, wide[k].at[at, :, view], core_send.at[n], core_recv.at[n], sibling)

            launch(started, make)
            shared.append((n, route, a, b, k, view))

    def slot(route, group, kind, i):
        return base + (route * 5 + group) * 6 + kind * 2 + i

    def axis(route, group):
        return rings[routes[route][0][0 if group == 0 else 1]]

    def begin(route, group, a, b):
        for turn in BOTH:
            for i in BOTH:
                push(route, i, a, b, axis(route, group)[turn], slot(route, group, turn, i))

    def onward(route, group, turn, a, b):
        for i in BOTH:
            arrive(route, i, a, b, slot(route, group, turn, i))
        push(route, turn, a, b, axis(route, group)[turn], slot(route, group, 2, turn))

    def finish(route, group, a, b):
        for i in BOTH:
            arrive(route, i, a, b, slot(route, group, 2, i))

    events = []

    def event(*steps):
        events.append(lambda: [f(*args) for f, *args in steps])

    event(*[(begin, r, 0, 0, 0) for r in BOTH])
    event(*[(begin, r, 1, 0, 0) for r in BOTH], *[(share, r, 0, 0) for r in BOTH])
    for turn, a in ((0, 3), (1, 1)):
        for r in BOTH:
            event((onward, r, 0, turn, a, 0), (begin, r, 1 + a, a, 0), (share, r, a, 0))
    for turn, b in ((0, 3), (1, 1)):
        for r in BOTH:
            event((onward, r, 1, turn, 0, b), (share, r, 0, b))
    for r in BOTH:
        event((finish, r, 0, 2, 0), (begin, r, 3, 2, 0), (share, r, 2, 0))
    for a in (3, 1):
        for turn, b in ((0, 3), (1, 1)):
            for r in BOTH:
                event((onward, r, 1 + a, turn, a, b), (share, r, a, b))
    for r in BOTH:
        event((finish, r, 1, 0, 2), (share, r, 0, 2))
    for turn, b in ((0, 3), (1, 1)):
        for r in BOTH:
            event((onward, r, 3, turn, 2, b), (share, r, 2, b))
    for a in (3, 1, 2):
        for r in BOTH:
            event((finish, r, 1 + a, a, 2), (share, r, a, 2))

    def settle():
        for n, route, a, b, k, view in shared:
            got = wide[k].at[place(route, a, b, 1 - core), :, view]
            remote(got, got, core_send.at[n], core_recv.at[n], sibling).wait_recv()

    events.append(settle)
    return events


def normalize(v):
    centered = v - jnp.mean(v, axis=-1, keepdims=True)
    factor = lax.rsqrt(jnp.mean(centered * centered, axis=-1, keepdims=True) + EPS)
    return centered * factor, factor


def norm_back(grad, normed, factor, gain):
    scaled = grad * gain
    inner = jnp.mean(scaled * normed, axis=-1, keepdims=True)
    return factor * (scaled - jnp.mean(scaled, axis=-1, keepdims=True) - normed * inner)


def columns(v):
    return jnp.sum(v, axis=0, keepdims=True)


def as_columns(rows):
    wide = [jnp.zeros((128 - len(rows), D), F32)]
    return jnp.concatenate(rows + wide, axis=0).T.astype(BF)


def eye(rows, cols):
    i = lax.broadcasted_iota(jnp.int32, (rows, cols), 0)
    j = lax.broadcasted_iota(jnp.int32, (rows, cols), 1)
    return jnp.where(i == j, 1.0, 0.0).astype(BF)


def pack_slabs(qkv_w, out_w, up_w, down_w, vectors, slabs):
    s0, s1, s2 = slabs
    spread = eye(16, 6)
    i = lax.broadcasted_iota(jnp.int32, (16, 6), 0)
    j = lax.broadcasted_iota(jnp.int32, (16, 6), 1)
    below = jnp.where(i == j + 8, 1.0, 0.0).astype(BF)
    rows = dot(spread, qkv_w[...])
    lane = lax.broadcasted_iota(jnp.int32, (16, 128), 1)
    row = lax.broadcasted_iota(jnp.int32, (16, 128), 0)
    flat = jnp.broadcast_to(vectors[...].astype(F32), (16, 128))
    i = lax.broadcasted_iota(jnp.int32, (128, 128), 0)
    j = lax.broadcasted_iota(jnp.int32, (128, 128), 1)

    def place(base, picks):
        r = row - base
        mine = ((lane < 48) & (lane % 6 == r) & (r >= 0) & (r < 6)) | ((lane >= 48) & (lane < 72) & ((lane - 48) // 4 == r))
        return dot(jnp.where(mine, flat, 0.0).astype(BF), jnp.where(picks, 1.0, 0.0).astype(BF))

    biases = place(0, (i // 6 == j) & (j < 2)).astype(BF)
    for g in range(4):
        q, k, v = (rows[:, n * D + g * 192 : n * D + g * 192 + 192] for n in range(3))
        s0[g, :, 0:640] = jnp.concatenate(
            [q, jnp.zeros((16, 64), F32), k[:, 0:128], v[:, 0:128], k[:, 128:192], v[:, 128:192]], axis=1
        ).astype(BF)
        s0[g, :, 640:768] = biases
    s1[:, 0:D] = (dot(spread, out_w[...]) + dot(below, up_w[:, 1280:2048])).astype(BF)
    s1[:, D:1792] = (dot(spread, up_w[:, 0:1024]) + dot(below, up_w[:, 2048:3072])).astype(BF)
    rest = place(8, ((i < 48) & (i // 6 == j + 2) & (j < 6)) | ((i >= 48) & (j == 8 + i % 4)))
    s1[:, 1792:1920] = (dot(spread, up_w[:, 1024:1152]) + rest).astype(BF)
    s1[:, 1920:2048] = dot(spread, up_w[:, 1152:1280]).astype(BF)
    s2[...] = dot(eye(32, 24), down_w[...]).astype(BF)


def forward_kernel(
    lengths, table, qkv_w, out_w, up_w, down_w, vectors, tokens, cotangent,
    result_out, dz1_out, w0, q_out, kv_out, o_out, lse_out, do_out, g1, g2, group_tokens,
    result, dz1_ref, q_land, kv_land, o_slab, lse_ref, do_land,
    s0, s1, s2, x0, x1, x2, own0, own1, own2, land0, land1, land2, words, o_land, do_slab, part_out, part_stat,
    ext, act, slope, grad1, grad2,
    x_send, x_recv, put_sem, send, recv, core_send, core_recv, e_send, e_recv, e_core_send, e_core_recv, t_send, t_recv,
    o_send, o_recv, d_send, d_recv, keep_sem,
):
    x, y, z, core = coords()
    side = z % 2
    slabs, arrived, own, wide = (s0, s1, s2), (x0, x1, x2), (own0, own1, own2), (land0, land1, land2)
    peers, rings, sibling = neighbours(x, y, z, core)
    partner = ident(x, y, z + 1 - 2 * side, core)
    places = plane(x, y, z, core)
    pack_slabs(qkv_w, out_w, up_w, down_w, vectors, slabs)
    greet(peers + list(places.values()) + [sibling])
    started, x_copies = [], {}

    def token_send(src, at, who, n, part=slice(None)):
        launch(started, lambda: remote(src.at[part], words.at[at].at[part], t_send.at[n], t_recv.at[n], who))

    def token_wait(at, n, part=slice(None)):
        view = words.at[at].at[part]
        remote(view, view, t_send.at[n], t_recv.at[n], sibling).wait_recv()

    right, left = peers[0], peers[2]
    halves = (pl.ds(0, T // 2), pl.ds(T // 2, T // 2))

    def line_tokens(src, which, n):
        token_send(src, which * 4 + x, right, n)
        token_send(src, which * 4 + x, left, n + 1)

    def line_onward(which, n):
        before, after = which * 4 + (x + 3) % 4, which * 4 + (x + 1) % 4
        token_wait(before, n)
        token_send(words.at[before], before, right, n + 2, halves[0])
        token_wait(after, n + 1)
        token_send(words.at[after], after, left, n + 3, halves[1])

    def line_finish(which, n):
        for i in BOTH:
            token_wait(which * 4 + (x + 2) % 4, n + 2 + i, halves[i])

    mine = side * 4 + x
    beyond = (1 - side) * 4 + x

    def send_slab(k):
        for d in (1, 3, 2):
            src = slabs[0].at[(x + d) % 4] if k == 0 else slabs[k]
            c = remote(src, arrived[k].at[d - 1], x_send.at[d - 1, k], x_recv.at[d - 1, k], peers[d - 1])
            c.start()
            x_copies[k, d] = c
            started.append(lambda c=c: c)

    for k in range(3):
        send_slab(k)
    token_send(tokens, mine, partner, 0)
    words[mine] = tokens[...]
    me = block_of(y, z, core)
    puts = [pltpu.make_async_copy(own[k], wide[k].at[me], put_sem.at[k]) for k in range(3)]

    def line(k):
        rows = ROWS[k]
        for d in (1, 3, 2):
            x_copies[k, d].wait_recv()
        shape = (4 * rows, SLAB[k][0])
        for base, first, cols in ((0, 0, 2048), (8, 2048, 1920)) if k == 1 else ((0, 0, D),):
            total = jnp.zeros((4 * rows, cols), F32)
            for d in range(4):
                slab = arrived[k][d - 1, :, 0:cols] if d else slabs[0][x] if k == 0 else slabs[k][:, 0:cols]
                total += dot(picker(shape, rows, (x + 4 - d) % 4, False, base), slab)
            own[k][:, first : first + cols] = total.astype(BF)
        puts[k].start()

    sems = (send, recv, core_send, core_recv)
    mid, late = (
        gather_events(routes, 60 * n, own, wide, (y, z, core), rings, sibling, sems, started)
        for n, routes in enumerate((MID, LATE))
    )

    def share_first(n, src, at):
        launch(started, lambda: remote(src, land0.at[at], e_core_send.at[n], e_core_recv.at[n], sibling))

    line(0)
    for n, who in places.items():
        launch(started, lambda n=n, who=who: remote(own0, land0.at[me], e_send.at[n], e_recv.at[n], who))
    share_first(0, own0, me)
    line_tokens(tokens, side, 1)
    line(1)
    interleave(mid, 2)
    line(2)
    interleave(late, 2)
    for n in places:
        at = block_of((y + 4 - n // 4) % 4, (z + 4 - n % 4) % 4, core)
        view = land0.at[at]
        remote(view, view, e_send.at[n], e_recv.at[n], sibling).wait_recv()
        share_first(n, view, at)
    interleave(mid, 2)
    for n in range(16):
        view = land0.at[block_of((y + 4 - n // 4) % 4, (z + 4 - n % 4) % 4, 1 - core)]
        remote(view, view, e_core_send.at[n], e_core_recv.at[n], sibling).wait_recv()
    puts[0].wait()
    kept = [pltpu.make_async_copy(land0, w0, keep_sem.at[0])]
    kept[0].start()

    weight = land0[...].reshape(D, D)
    biases = weight[:, 640:].astype(F32).T
    query_bias = key_bias = jnp.zeros((1, 192), F32)
    for g in range(4):
        here = slice(g * 192, g * 192 + 192)
        query_bias = jnp.where(x == g, biases[0:1, here], query_bias)
        key_bias = jnp.where(x == g, biases[1:2, here], key_bias)
    none = jnp.zeros((1, 64), F32)
    query_bias = jnp.concatenate([query_bias, none], axis=1)
    key_bias = jnp.concatenate([none, none, key_bias[:, :128], none, key_bias[:, 128:]], axis=1)

    def project(at, with_query):
        if with_query:
            both = dot(words[at], weight[:, 0:640])
            q_land[at % 4] = ((both[:, :256] + query_bias).astype(BF).astype(F32) * 0.125).astype(BF)
            kv_land[at] = (both[:, 256:] + key_bias).astype(BF)
        else:
            kv_land[at] = (dot(words[at], weight[:, 256:640]) + key_bias).astype(BF)

    project(mine, True)
    interleave(mid, 2)
    line_onward(side, 1)
    token_wait(beyond, 0)
    line_tokens(words.at[beyond], 1 - side, 5)
    project(side * 4 + (x + 3) % 4, True)
    project(side * 4 + (x + 1) % 4, True)
    interleave(mid, 6)
    interleave(late, 4)
    project(beyond, False)
    line_finish(side, 1)
    project(side * 4 + (x + 2) % 4, True)

    def keep(src, dst):
        c = pltpu.make_async_copy(src, dst, keep_sem.at[len(kept)])
        c.start()
        kept.append(c)

    keep(q_land, q_out)
    copies = []

    def deliver(src, landing, to_slot, from_slot, ss, rr, who):
        launch(started, lambda: remote(src, landing.at[to_slot], ss, rr, who))
        copies.append((landing.at[from_slot], ss, rr))

    first = head_lanes(0)
    lane = lax.broadcasted_iota(jnp.int32, (1, 128), 1)

    def attend(part, which, events, events_plan):
        key_seg = jnp.concatenate(
            [jnp.full((1, 128), seg_of(lengths, table, which * 8 + j), jnp.int32) for j in range(8)], axis=1
        )
        plans = [events_plan[h::3] for h in range(3)]

        def chunk(turn, carry):
            d = offset_of(turn)
            to = (x + d) % 4
            block = (side * 4 + to) * 2
            query_seg = jnp.concatenate([jnp.full((128, 1), seg_of(lengths, table, block + i), jnp.int32) for i in BOTH], axis=0)
            allowed = query_seg == key_seg
            outs, stats = [], []
            for h in range(3):
                planned(by_head[h], turn, plans[h])
                tile = h // 2 * 128
                q = jnp.where(head_lanes(h), q_land[to, :, tile : tile + 128].astype(F32), 0.0).astype(BF)
                k, v = key_value(kv_land[pl.ds(which * 4, 4)], h)
                s = jnp.where(allowed, dot_t(q, k), -1e30)
                top = jnp.max(s, axis=1, keepdims=True)
                e = jnp.exp(s - top)
                total = jnp.sum(e, axis=1, keepdims=True)
                out = dot(e.astype(BF), v)
                if part == 0:
                    part_out[to, h] = out
                    stats += [top, total]
                else:
                    top_was, total_was = part_stat[to, :, 2 * h : 2 * h + 1], part_stat[to, :, 2 * h + 1 : 2 * h + 2]
                    highest = jnp.maximum(top, top_was)
                    now, was = jnp.exp(top - highest), jnp.exp(top_was - highest)
                    total = total * now + total_was * was
                    outs.append((out * now + part_out[to, h] * was) / total)
                    stats.append(highest + jnp.log(total))
            table_of = jnp.zeros((T, 128), F32)
            for i, v in enumerate(stats):
                table_of = jnp.where(lane == i, v, table_of)
            if part == 0:
                part_stat[to] = table_of
                return carry
            lse_ref[to] = table_of
            o_slab[to, :, 0:128] = jnp.where(first, outs[0], outs[1]).astype(BF)
            o_slab[to, :, 128:256] = jnp.where(first, 0.0, outs[2]).astype(BF)

            @pl.when(turn < 3)
            def _():
                who = ident(to, y, z, core)
                remote(o_slab.at[to], o_land.at[x], o_send.at[d], o_recv.at[d], who).start()

            return carry

        by_head = [[], [], []]
        for n, count in enumerate(events_plan):
            for _ in range(min(count, len(events))):
                by_head[n % 3].append(events.pop(0))
        lax.fori_loop(0, 4, chunk, 0)
        if part:
            o_land[x] = o_slab[x]
            for d in (2, 1, 3):
                to, fro = (x + d) % 4, (x + 4 - d) % 4
                started.append(lambda d=d, to=to: remote(o_slab.at[to], o_land.at[x], o_send.at[d], o_recv.at[d], peers[d - 1]))
                copies.append((o_land.at[fro], o_send.at[d], o_recv.at[d]))

    attend(0, side, mid, (1,) * 12)
    line_onward(1 - side, 5)
    project((1 - side) * 4 + (x + 3) % 4, False)
    project((1 - side) * 4 + (x + 1) % 4, False)
    interleave(mid, 100)
    interleave(late, 8)
    line_finish(1 - side, 5)
    project((1 - side) * 4 + (x + 2) % 4, False)
    keep(kv_land, kv_out)
    keep(words, group_tokens)
    attend(1, 1 - side, late, (1,) * 12)
    keep(o_slab, o_out)
    keep(lse_ref, lse_out)
    puts[1].wait()
    puts[2].wait()

    vecs = land1[:, :, 3840:].reshape(D, 128).astype(F32).T
    out_bias, gain_one, shift_one, down_bias, gain_two, shift_two = (vecs[i : i + 1] for i in range(6))
    i = lax.broadcasted_iota(jnp.int32, (192, D), 0)
    j = lax.broadcasted_iota(jnp.int32, (192, D), 1)
    stretch = jnp.where(i == j // 4, 1.0, 0.0).astype(BF)
    i = lax.broadcasted_iota(jnp.int32, (8, D), 0)
    j = lax.broadcasted_iota(jnp.int32, (8, D), 1)
    four = vecs[8:16].astype(BF)
    up_biases = [columns(jnp.where(i == j % 4, dot(four[:, n * 192 : n * 192 + 192], stretch), 0.0)) for n in range(4)]
    interleave(late, 100)
    for g in range(4):
        part = land1[g * 8 : g * 8 + 8, :, 0:D].reshape(192, D)
        ext[g, 0:128] = part[0:128]
        ext[g, 128:192] = jnp.zeros((64, D), BF)
        ext[g, 192:256] = part[128:192]
    for got, ss, rr in copies:
        remote(got, got, ss, rr, sibling).wait_recv()
    copies.clear()
    branch = dot(o_land[0], ext[0])
    for g in range(1, 4):
        branch += dot(o_land[g], ext[g])
    normed_one, factor_one = normalize(tokens[...].astype(F32) + (branch + out_bias))
    hidden = normed_one * gain_one + shift_one
    low = hidden.astype(BF)
    for n in range(4):
        up = land1[:, :, D + n * D : 2 * D + n * D].reshape(D, D)
        upper = dot(low, up) + up_biases[n]
        square = upper * upper
        t = jnp.tanh(0.7978845608028654 * (upper + 0.044715 * (square * upper)))
        half = 0.5 * (1.0 + t)
        slope[n] = half + 0.5 * upper * (1.0 - t * t) * (0.7978845608028654 * (1.0 + 3.0 * 0.044715 * square))
        act[n] = (upper * half).astype(BF)
    feed = jnp.zeros((T, D), F32)
    for n in range(4):
        feed += dot(act[n], land2[n * 8 : n * 8 + 8].reshape(D, D))
    normed_two, factor_two = normalize(hidden + (feed + down_bias))
    result[...] = (normed_two * gain_two + shift_two).astype(BF)
    keep(result, result_out)

    grad = cotangent[...].astype(F32)
    dz2 = norm_back(grad, normed_two, factor_two, gain_two)
    gain_two_grad, shift_two_grad = columns(grad * normed_two), columns(grad)
    dfeed = dz2.astype(BF)
    down_bias_grad = columns(dfeed.astype(F32))
    dhidden = dz2

    for n in range(4):
        up = land1[:, :, D + n * D : 2 * D + n * D].reshape(D, D)
        down = land2[n * 8 : n * 8 + 8].reshape(D, D)
        dupper = (dot_t(dfeed, down) * slope[n]).astype(BF)
        rows, cols = slice(n * 8, n * 8 + 8), slice(D + n * D, 2 * D + n * D)
        grad2[rows, :, :D] = dot_rows(act[n], dfeed).astype(BF).reshape(8, 96, D)
        grad2[rows, :, D:] = as_columns([columns(dupper.astype(F32))]).reshape(8, 96, 128)
        keep(grad2.at[pl.ds(n * 8, 8)], g2.at[pl.ds(n * 8, 8)])
        grad1[:, :, cols] = dot_rows(low, dupper).astype(BF).reshape(32, 24, D)
        keep(grad1.at[:, :, pl.ds(D + n * D, D)], g1.at[:, :, pl.ds(D + n * D, D)])
        dhidden += dot_t(dupper, up)
    dz1 = norm_back(dhidden, normed_one, factor_one, gain_one)
    dz1_ref[...] = dz1
    keep(dz1_ref, dz1_out)
    dbranch = dz1.astype(BF)
    for d in TURNS:
        to = (x + d) % 4
        do_slab[to] = dot_t(dbranch, ext[to]).astype(BF)
        if d:
            deliver(do_slab.at[to], do_land, x, (x + 4 - d) % 4, d_send.at[d], d_recv.at[d], peers[d - 1])
        else:
            do_land[x] = do_slab[x]
    for g in range(4):
        part = dot_rows(o_land[g], dbranch).astype(BF)
        grad1[g * 8 : g * 8 + 8, :, 0:D] = jnp.concatenate([part[0:128], part[192:256]], axis=0).reshape(8, 24, D)
    grad1[:, :, 3840:] = as_columns(
        [columns(dbranch.astype(F32)), columns(dhidden * normed_one), columns(dhidden),
         down_bias_grad, gain_two_grad, shift_two_grad]
    ).reshape(32, 24, 128)
    keep(grad1.at[:, :, pl.ds(0, D)], g1.at[:, :, pl.ds(0, D)])
    keep(grad1.at[:, :, pl.ds(3840, 128)], g1.at[:, :, pl.ds(3840, 128)])
    for got, ss, rr in copies:
        remote(got, got, ss, rr, sibling).wait_recv()
    keep(do_land, do_out)
    for make in started:
        make().wait_send()
    for c in kept:
        c.wait()


def forward(*args):
    slab = (4, T, 256)
    return pl.pallas_call(
        forward_kernel,
        out_shape=(
            struct((T, D), BF), struct((T, D), F32), struct((32,) + WIDE[0], BF), struct(slab, BF), struct((8, T, 384), BF),
            struct(slab, BF), struct((4, T, 128), F32), struct(slab, BF),
            struct((32,) + SUMS[1], BF), struct((32,) + SUMS[2], BF), struct((8, T, D), BF),
        ),
        in_specs=[SM] * 2 + [VM] * 7,
        out_specs=(ANY,) * 11,
        scratch_shapes=[pltpu.VMEM((T, D), BF), pltpu.VMEM((T, D), F32), pltpu.VMEM(slab, BF), pltpu.VMEM((8, T, 384), BF)]
        + [pltpu.VMEM(slab, BF), pltpu.VMEM((4, T, 128), F32), pltpu.VMEM(slab, BF)]
        + [pltpu.VMEM((4,) + SLAB[0], BF)] + [pltpu.VMEM(t, BF) for t in SLAB[1:]]
        + [pltpu.VMEM((3,) + t, BF) for t in SLAB]
        + [pltpu.VMEM(w, BF) for w in WIDE]
        + [pltpu.VMEM((32,) + w, BF) for w in WIDE]
        + [pltpu.VMEM((8, T, D), BF), pltpu.VMEM(slab, BF), pltpu.VMEM(slab, BF)]
        + [pltpu.VMEM((4, 3, T, 128), F32), pltpu.VMEM((4, T, 128), F32)]
        + [pltpu.VMEM((4, 256, D), BF), pltpu.VMEM((4, T, D), BF), pltpu.VMEM((4, T, D), F32)]
        + [pltpu.VMEM((32,) + w, BF) for w in SUMS[1:]]
        + [DMA((3, 3)), DMA((3, 3)), DMA((3,)), DMA((120,)), DMA((120,)), DMA((64,)), DMA((64,))]
        + [DMA((16,))] * 4
        + [DMA((9,)), DMA((9,)), DMA((4,)), DMA((4,)), DMA((4,)), DMA((4,)), DMA((24,))],
        compiler_params=pltpu.CompilerParams(collective_id=0, has_side_effects=True, vmem_limit_bytes=62 << 20),
        name="forward",
    )(*args)


def scatter_events(routes, grads, acc, fro, buf, where, rings, sibling, sems, started):
    y, z, core = where
    load_sem, core_send, core_recv, send, recv = sems
    moves, waited = {}, set()

    def spot(route, a, b):
        dy, dz = (a, b) if routes[route][0] == "yz" else (b, a)
        return dy, dz, dy * 4 + dz

    def begin():
        for r, a, b in [(r, a, b) for b in TURNS for a in TURNS for r in BOTH]:
            dy, dz, at = spot(r, a, b)
            if at in moves:
                continue
            here = block_of((y + dy) % 4, (z + dz) % 4, core)
            there = block_of((y + dy) % 4, (z + dz) % 4, 1 - core)
            moves[at] = []
            for k in (1, 2):
                n = at * 2 + k - 1
                swap = remote(grads[k].at[there], fro[k].at[at], core_send.at[n], core_recv.at[n], sibling)
                load = pltpu.make_async_copy(grads[k].at[here], acc[k].at[at], load_sem.at[n])
                swap.start()
                load.start()
                started.append(lambda swap=swap: swap)
                moves[at].append((load, swap))

    def folding(r, a, b):
        at = spot(r, a, b)[2]
        fresh = at not in waited
        waited.add(at)
        return fold, r, a, b, fresh

    def fold(r, a, b, fresh):
        _, _, at = spot(r, a, b)
        if fresh:
            for load, swap in moves[at]:
                load.wait()
                swap.wait_recv()
        for k, first, cols in chunks_of(routes[r]):
            view = (at, slice(None), pl.ds(first, cols))
            acc[k][view] = acc[k][view] + fro[k][view]

    def slot(r, group, kind, i):
        return (r * 5 + group) * 9 + kind * 3 + (len(routes[r][1][0]) if i else 0)

    def axis(r, group):
        return rings[routes[r][0][0 if group == 0 else 1]]

    def at_of(r, group, step):
        return spot(r, *((step, 0) if group == 0 else (group - 1, step)))[2]

    def push(r, group, kind, i, step, who):
        for j, (k, first, cols) in enumerate(routes[r][1][i]):
            n, view = slot(r, group, kind, i) + j, pl.ds(first, cols)

            def make(k=k, n=n, view=view):
                src = acc[k].at[at_of(r, group, step), :, view]
                return remote(src, buf[k].at[group * 3 + kind, :, view], send.at[n], recv.at[n], who)

            launch(started, make)

    def add(r, group, kind, i, step):
        for j, (k, first, cols) in enumerate(routes[r][1][i]):
            n, view = slot(r, group, kind, i) + j, pl.ds(first, cols)
            got = buf[k].at[group * 3 + kind, :, view]
            remote(got, got, send.at[n], recv.at[n], sibling).wait_recv()
            at = (at_of(r, group, step), slice(None), view)
            acc[k][at] = acc[k][at] + buf[k][group * 3 + kind, :, view]

    def one(r, group):
        right, left = axis(r, group)
        push(r, group, 0, 0, 2, right)
        push(r, group, 0, 1, 2, left)

    def two(r, group):
        right, left = axis(r, group)
        add(r, group, 0, 0, 1)
        push(r, group, 1, 0, 1, right)
        push(r, group, 1, 1, 1, right)
        add(r, group, 0, 1, 3)
        push(r, group, 2, 0, 3, left)
        push(r, group, 2, 1, 3, left)

    def three(r, group):
        for kind in (1, 2):
            for i in BOTH:
                add(r, group, kind, i, 0)

    events = []

    def event(*steps):
        events.append(lambda: [f(*args) for f, *args in steps])

    for a in TURNS:
        for r in BOTH:
            event(folding(r, a, 2), (one, r, 1 + a))
    for a in TURNS:
        for r in BOTH:
            event(folding(r, a, 1), folding(r, a, 3), (two, r, 1 + a))
    for a in TURNS:
        for r in BOTH:
            more = {2: [(one, r, 0)], 3: [(two, r, 0)]}.get(a, [])
            event(folding(r, a, 0), (three, r, 1 + a), *more)
    for r in BOTH:
        event((three, r, 0))
    return begin, events


def backward_kernel(
    lengths, table, q_in, kv_in, do_in, o_in, lse_in, dz1_in, group_tokens, w0, g1, g2, dx_ref, o0, o1, o2,
    q_ref, kv_ref, do_ref, o_ref, lse_ref, dz1, wa, words, g0, a0, a1, a2, c0, c1, c2, b0, b1, b2, xs0, xs1, xs2, xr0, xr1, xr2, dx_slab, dx_land, kv_slab, kv_land,
    total, q_total, grads_low,
    load_sem, core_send, core_recv, send, recv, e_send, e_recv, e_core_send, e_core_recv, x_send, x_recv, dx_send, dx_recv, kv_send, kv_recv, w_sem,
):
    x, y, z, core = coords()
    side = z % 2
    mine = side * 4 + x
    grads, outs, acc, fro, buf = (g0, g1, g2), (o0, o1, o2), (a0, a1, a2), (c0, c1, c2), (b0, b1, b2)
    out_slabs, in_slabs = (xs0, xs1, xs2), (xr0, xr1, xr2)
    peers, rings, sibling = neighbours(x, y, z, core)
    partner = ident(x, y, z + 1 - 2 * side, core)
    first_in, fetch = [], []
    for src, dst, cuts in (
        (q_in, q_ref, (0, 128, 256)), (kv_in, kv_ref, (0, 128, 256, 384)), (do_in, do_ref, (0, 128, 256)),
        (o_in, o_ref, (0, 128, 256)), (lse_in, lse_ref, (0, 128)),
    ):
        for at, end in zip(cuts, cuts[1:]):
            view = pl.ds(at, end - at)
            first_in.append(pltpu.make_async_copy(src.at[:, :, view], dst.at[:, :, view], w_sem.at[len(first_in)]))
            first_in[-1].start()
    places = plane(x, y, z, core)
    greet(peers + list(places.values()) + [sibling])
    started, copies = [], []
    sems = (load_sem, core_send, core_recv, send, recv)
    begin_late, late = scatter_events(BACK_LATE, grads, acc, fro, buf, (y, z, core), rings, sibling, sems, started)
    begin_late()
    for n, (src, dst) in enumerate(((w0, wa), (group_tokens, words), (dz1_in, dz1))):
        fetch.append(pltpu.make_async_copy(src, dst, w_sem.at[len(first_in) + n]))
        fetch[-1].start()
    for c in first_in:
        c.wait()

    def deliver(src, landing, to_slot, from_slot, ss, rr, who):
        launch(started, lambda: remote(src, landing.at[to_slot], ss, rr, who))
        copies.append((landing.at[from_slot], ss, rr))

    first = head_lanes(0)
    swap = remote(kv_slab, kv_land, kv_send.at[0], kv_recv.at[0], partner)
    for part, which in enumerate((1 - side, side)):
        key_seg = jnp.concatenate([jnp.full((128, 1), seg_of(lengths, table, which * 8 + j), jnp.int32) for j in range(8)], axis=0)
        plan = BACK_PLAN[part * 12 : part * 12 + 12]
        plans = [plan[h::3] for h in range(3)]
        by_head = [[], [], []]
        for n, count in enumerate(plan):
            for _ in range(min(count, len(late))):
                by_head[n % 3].append(late.pop(0))
        total[...] = jnp.zeros_like(total)

        def chunk(turn, carry):
            to = (x + offset_of(turn)) % 4
            block = (side * 4 + to) * 2
            query_seg = jnp.concatenate([jnp.full((1, 128), seg_of(lengths, table, block + i), jnp.int32) for i in BOTH], axis=1)
            allowed = key_seg == query_seg
            logs = lse_ref[to].T
            parts = []
            for h in range(3):
                planned(by_head[h], turn, plans[h])
                tile = h // 2 * 128
                cols = slice(tile, tile + 128)
                lanes = head_lanes(h)
                out_lanes = lanes if h < 2 else jnp.logical_not(lanes)
                q = jnp.where(lanes, q_ref[to, :, cols].astype(F32), 0.0).astype(BF)
                do = jnp.where(out_lanes, do_ref[to, :, cols].astype(F32), 0.0)
                inner = jnp.sum(do * o_ref[to, :, cols].astype(F32), axis=1, keepdims=True)
                inner = jnp.broadcast_to(inner, (T, 128)).T[0:1]
                do = do.astype(BF)
                k, v = key_value(kv_ref[pl.ds(which * 4, 4)], h)
                p = jnp.where(allowed, jnp.exp(dot_t(k, q) - logs[h : h + 1]), 0.0)
                ds = (p * (dot_t(v, do) - inner)).astype(BF)
                dk, dv = dot(ds, q), dot(p.astype(BF), do)
                if h < 2:
                    total[:, 0:128] += dk
                    total[:, 128:256] += dv
                else:
                    total[:, 256:384] += dk + dv
                parts.append(dot_rows(ds, k) * 0.125)
            for at, piece in (
                (slice(0, 128), jnp.where(first, parts[0], parts[1])), (slice(128, 256), jnp.where(first, parts[2], 0.0)),
            ):
                if part == 0:
                    q_total[to, :, at] = piece
                else:
                    grads_low[to, :, at] = (q_total[to, :, at] + piece).astype(BF)
            return carry

        lax.fori_loop(0, 4, chunk, 0)
        if part == 0:
            kv_slab[...] = total[...].astype(BF).reshape(4, T, 384)
            swap.start()
            started.append(lambda: swap)
    for c in fetch:
        c.wait()
    own_part = total[...].astype(BF)
    for at, piece in (
        (slice(0, 256), dot_rows(words[pl.ds(side * 4, 4)].reshape(4 * T, D), grads_low[:, :, 0:256].reshape(4 * T, 256))),
        (slice(256, 640), dot_rows(words[pl.ds(side * 4, 4)].reshape(4 * T, D), own_part)
         + dot_rows(words[pl.ds(4 - side * 4, 4)].reshape(4 * T, D), kv_slab[...].reshape(4 * T, 384))),
    ):
        g0[:, :, at] = piece.astype(BF).reshape(32, 24, at.stop - at.start)
    q_sums = columns(grads_low[:, :, 0:256].reshape(4 * T, 256).astype(F32))
    kv_sums = columns(own_part.astype(F32)) + columns(kv_slab[...].reshape(4 * T, 384).astype(F32))
    bias = (q_sums[:, 0:192], jnp.concatenate([kv_sums[:, 128:256], kv_sums[:, 320:384]], axis=1))
    bias = [jnp.concatenate([jnp.where(x == g, b, 0.0) for g in range(4)], axis=1) for b in bias]
    g0[:, :, 640:] = as_columns(bias).reshape(32, 24, 128)
    folds = {}
    for n in list(places) + [0]:
        there = block_of((y + n // 4) % 4, (z + n % 4) % 4, 1 - core)
        folds[n] = remote(g0.at[there], c0.at[n], e_core_send.at[n], e_core_recv.at[n], sibling)
        folds[n].start()
        started.append(lambda n=n: folds[n])
    interleave(late, 2)
    for n in list(places) + [0]:
        folds[n].wait_recv()
        a0[n] = g0[block_of((y + n // 4) % 4, (z + n % 4) % 4, core)] + c0[n]
        if n:
            launch(started, lambda n=n: remote(a0.at[n], b0.at[n], e_send.at[n], e_recv.at[n], places[n]))
    interleave(late, LATE_BEFORE_SHARE)
    swap.wait_recv()
    for g in range(4):
        grads_low[g, :, 256:] = (total[g * T : g * T + T] + kv_land[g].astype(F32)).astype(BF)
    weight = wa[:, :, 0:640].reshape(D, 640)
    for d in TURNS:
        to = (x + d) % 4
        share = dot_t(grads_low[to], weight)
        if d:
            dx_slab[to] = share.astype(BF)
            deliver(dx_slab.at[to], dx_land, x, (x + 4 - d) % 4, dx_send.at[d], dx_recv.at[d], peers[d - 1])
        else:
            dx_ref[...] = dz1[...] + share

    def line_out(k):
        rows = ROWS[k]
        shape = (SUM_SLAB[k][0], 4 * rows)

        def slab(at):
            if k != 1:
                return dot(picker(shape, rows, at, True), acc[k][0])
            upper, lower = picker(shape, rows, at, True), picker(shape, rows, at, True, 8)
            rest = jnp.concatenate([acc[1][0, :, 2048:NB], jnp.zeros((24, 128), BF)], axis=1)
            return dot(upper, acc[1][0, :, 0:2048]) + dot(lower, rest)

        for d in (2, 1, 3):
            out_slabs[k][d - 1] = slab((x + d) % 4).astype(BF)
            c = remote(out_slabs[k].at[d - 1], in_slabs[k].at[d - 1], x_send.at[d - 1, k], x_recv.at[d - 1, k], peers[d - 1])
            c.start()
            started.append(lambda c=c: c)
            x_copies[k].append(c)
        in_slabs[k][3] = slab(x).astype(BF)

    def gathered(k):
        for c in x_copies[k]:
            c.wait_recv()
        return [in_slabs[k][i].astype(F32) for i in range(4)]

    x_copies = {0: [], 1: [], 2: []}
    interleave(late, 100)
    line_out(1)
    line_out(2)
    first_sum = a0[0].astype(F32)
    for n in places:
        remote(b0.at[n], b0.at[n], e_send.at[n], e_recv.at[n], sibling).wait_recv()
        first_sum += b0[n].astype(F32)
    a0[0] = first_sum.astype(BF)
    line_out(0)
    one, two, three, four = gathered(1)
    both = one + two + three + four
    o1[:, 0:2048] = both[0:8]
    o1[:, 2048:NB] = both[8:16, 0:1920]
    one, two, three, four = gathered(2)
    o2[...] = (one + two + three + four)[0:24]
    for got, ss, rr in copies:
        remote(got, got, ss, rr, sibling).wait_recv()
    dx = dx_ref[...]
    for d in (1, 2, 3):
        dx += dx_land[(x + d) % 4].astype(F32)
    dx_ref[...] = dx
    gathered(0)
    groups = []
    for g in range(4):
        groups.append(xr0[(x - g + 3) % 4].astype(F32))
    groups = [v[0:8] for v in groups]
    o0[:, 0 : 3 * D] = jnp.concatenate(
        [v[:, 0:192] for v in groups]
        + [p for v in groups for p in (v[:, 256:384], v[:, 512:576])]
        + [p for v in groups for p in (v[:, 384:512], v[:, 576:640])], axis=1
    )
    o0[:, 3 * D :] = groups[0][:, 640:] + groups[1][:, 640:] + groups[2][:, 640:] + groups[3][:, 640:]
    for make in started:
        make().wait_send()


BACK_PLAN = (2, 2, 2, 2, 0, 1, 1, 1, 1, 1, 1, 1, 1, 0, 0, 0, 0, 1, 0, 1, 0, 1, 0, 1)
LATE_BEFORE_SHARE = 2


def backward(*args):
    return pl.pallas_call(
        backward_kernel,
        out_shape=(struct((T, D), F32), struct((8, 2432), F32), struct((8, NB), F32), struct((24, NC), F32)),
        in_specs=[SM] * 2 + [ANY] * 10,
        out_specs=(VM,) * 4,
        scratch_shapes=[pltpu.VMEM((4, T, 256), BF), pltpu.VMEM((8, T, 384), BF), pltpu.VMEM((4, T, 256), BF)]
        + [pltpu.VMEM((4, T, 256), BF), pltpu.VMEM((4, T, 128), F32), pltpu.VMEM((T, D), F32)]
        + [pltpu.VMEM((32,) + WIDE[0], BF), pltpu.VMEM((8, T, D), BF), pltpu.VMEM((32,) + WIDE[0], BF)]
        + [pltpu.VMEM((16,) + w, BF) for w in SUMS] * 2
        + [pltpu.VMEM((16,) + SUMS[0], BF)] + [pltpu.VMEM((15,) + w, BF) for w in SUMS[1:]]
        + [pltpu.VMEM((3,) + t, BF) for t in SUM_SLAB] + [pltpu.VMEM((4,) + t, BF) for t in SUM_SLAB]
        + [pltpu.VMEM((4, T, D), BF)] * 2 + [pltpu.VMEM((4, T, 384), BF)] * 2
        + [pltpu.VMEM((4 * T, 384), F32), pltpu.VMEM((4, T, 256), F32), pltpu.VMEM((4, T, 640), BF)]
        + [DMA((32,)), DMA((32,)), DMA((32,)), DMA((90,)), DMA((90,))] + [DMA((16,))] * 4 + [DMA((3, 3)), DMA((3, 3))]
        + [DMA((4,)), DMA((4,)), DMA((1,)), DMA((1,)), DMA((16,))],
        compiler_params=pltpu.CompilerParams(collective_id=1, has_side_effects=True, vmem_limit_bytes=62 << 20),
        name="backward",
    )(*args)


def unpack_kernel(o0, o1, o2, dx_in, low_in, low, dx, qkv, query, value, out, out_bias, gain_one, shift_one, up, up_bias,
                  down, down_bias, gain_two, shift_two):
    dx[...] = dx_in[...]
    low[...] = low_in[...]
    qkv[...] = o0[0:6, 0 : 3 * D]
    out[...] = o1[0:6, 0:D]
    up[...] = o1[0:6, D:3840]
    down[...] = o2[:, 0:D]
    first, second = o0[:, 3 * D :].T, o1[:, 3840:].T
    third = jnp.concatenate([o2[:, D:], jnp.zeros((104, 128), F32)], axis=0).T
    query[...], value[...] = first[0, 0:6], first[1, 0:6]
    for i, ref in enumerate((out_bias, gain_one, shift_one, down_bias, gain_two, shift_two)):
        ref[...] = second[i, 0:6]
    up_bias[...] = third[0, 0:24]


def unpack(*args):
    six = struct((6,), F32)
    return pl.pallas_call(
        unpack_kernel,
        out_shape=(
            struct((T, D), BF), struct((T, D), F32), struct((6, 3 * D), F32), six, six, struct((6, D), F32), six, six, six,
            struct((6, FF), F32), struct((24,), F32), struct((24, D), F32), six, six, six,
        ),
        in_specs=[VM] * 5,
        out_specs=(VM,) * 15,
        name="unpack",
    )(*args)


def shards(
    tokens, lengths, block_table, qkv_weight, query_bias, value_bias, out_weight, out_bias, first_gain, first_shift,
    up_weight, up_bias, down_weight, down_bias, second_gain, second_shift, cotangent,
):
    vectors = jnp.zeros((128,), BF)
    at = 0
    for v in (query_bias, value_bias, out_bias, first_gain, first_shift, down_bias, second_gain, second_shift, up_bias):
        vectors += jnp.pad(v, (at, 128 - at - v.shape[0]))
        at += v.shape[0]
    vectors = vectors[None, :]
    result, dz1, w0, q, kv, o, lse, do, g1, g2, words = forward(
        lengths, block_table, qkv_weight, out_weight, up_weight, down_weight, vectors, tokens, cotangent
    )
    dx, ga, gb, gc = backward(lengths, block_table, q, kv, do, o, lse, dz1, words, w0, g1, g2)
    return unpack(ga, gb, gc, dx, result)


def solution(mesh):
    both = ("fsdp", "seq")
    whole, flat, group = P(both, None), P(both), P("fsdp", None)
    return jax.shard_map(
        shards,
        mesh=mesh,
        in_specs=(whole, group, group, whole, flat, flat, whole, flat, flat, flat, whole, flat, whole, flat, flat, flat, whole),
        out_specs=(whole, whole, whole, flat, flat, whole, flat, flat, flat, whole, flat, whole, flat, flat, flat),
        check_vma=False,
    )
```

```python
import jax
import jax.numpy as jnp
from jax import lax
from jax.experimental import pallas as pl
from jax.experimental.pallas import tpu as pltpu
from jax.sharding import PartitionSpec as P

MESH = pl.DeviceIdType.MESH
BF, F32 = jnp.bfloat16, jnp.float32
EPS = 1e-12
D, FF, T = 768, 3072, 256
NB, NC = 3968, 896
WIDE = ((24, D), (24, NB), (96, D))
SUMS = ((24, D), (24, NB), (96, NC))
SLAB = ((16, D), (16, 2048), (32, D))
SUM_SLAB = ((16, D), (16, 2048), (32, NC))
ROWS = (6, 6, 24)
MID = (
    ("yz", (((1, 0, 768),), ((1, 768, 768),))),
    ("zy", (((1, 1536, 1280),), ((1, 2816, 1152),))),
)
LATE = (
    ("yz", (((2, 0, 128),), ((2, 128, 128),))),
    ("zy", (((2, 256, 256),), ((2, 512, 256),))),
)
BACK_LATE = (
    ("yz", (((2, 0, 256),), ((1, 0, 1024),))),
    ("zy", (((1, 1024, 2944),), ((2, 256, 640),))),
)
BOTH = (0, 1)
TURNS = (2, 1, 3, 0)
ANY = pl.BlockSpec(memory_space=pl.ANY)
VM = pl.BlockSpec(memory_space=pltpu.VMEM)
SM = pl.BlockSpec(memory_space=pltpu.SMEM)
DMA = pltpu.SemaphoreType.DMA


def struct(shape, kind):
    return jax.ShapeDtypeStruct(shape, kind)


def whole_of(route):
    ((k, first, cols),), ((_, _, more),) = route[1]
    return ((k, first, cols + more),)


def chunks_of(route):
    return tuple(part for piece in route[1] for part in piece)


def coords():
    f, s = lax.axis_index("fsdp"), lax.axis_index("seq")
    return s % 4, (f // 2) % 4, (f // 8) * 2 + s // 4, f % 2


def ident(x, y, z, core):
    return {"fsdp": (z // 2) * 8 + y * 2 + core, "seq": (z % 2) * 4 + x}


def block_of(y, z, core):
    return (z // 2) * 16 + y * 4 + core * 2 + z % 2


def greet(partners):
    barrier = pltpu.get_barrier_semaphore()
    for who in partners:
        pl.semaphore_signal(barrier, inc=1, device_id=who, device_id_type=MESH)
    pl.semaphore_wait(barrier, len(partners))


def remote(src, dst, send, recv, who):
    return pltpu.make_async_remote_copy(
        src, dst, send, recv, device_id=who, device_id_type=MESH
    )


def dot(a, b):
    return jnp.dot(a, b, preferred_element_type=F32)


def dot_t(a, b):
    return lax.dot_general(a, b, (((1,), (1,)), ((), ())), preferred_element_type=F32)


def dot_rows(a, b):
    return lax.dot_general(a, b, (((0,), (0,)), ((), ())), preferred_element_type=F32)


def picker(shape, rows, at, transposed, base=0):
    i = lax.broadcasted_iota(jnp.int32, shape, 0)
    j = lax.broadcasted_iota(jnp.int32, shape, 1)
    if transposed:
        i, j = j, i
    j = j - base
    return jnp.where((i == at * rows + j) & (j >= 0) & (j < rows), 1.0, 0.0).astype(BF)


def plane(x, y, z, core):
    return {n: ident(x, (y + n // 4) % 4, (z + n % 4) % 4, core) for n in range(1, 16)}


def neighbours(x, y, z, core):
    peers = [ident((x + d) % 4, y, z, core) for d in (1, 2, 3)]
    rings = {
        "y": [ident(x, (y + d) % 4, z, core) for d in (1, 3)],
        "z": [ident(x, y, (z + d) % 4, core) for d in (1, 3)],
    }
    return peers, rings, ident(x, y, z, 1 - core)


def seg_of(lengths, table, j):
    place = table[0, j]
    end = lengths[0, 0]
    return (place >= end).astype(jnp.int32) + (place >= end + lengths[0, 1]).astype(jnp.int32)


def head_lanes(h):
    lane = lax.broadcasted_iota(jnp.int32, (1, 128), 1)
    return (lane < 64) if h % 2 == 0 else (lane >= 64)


def key_value(kv, h):
    rows = kv.shape[0] * T
    if h < 2:
        return kv[:, :, 0:128].reshape(rows, 128), kv[:, :, 128:256].reshape(rows, 128)
    both = kv[:, :, 256:384].reshape(rows, 128)
    return both, both


def launch(started, make):
    make().start()
    started.append(make)


def planned(events, turn, plan):
    for t, count in enumerate(plan):
        if count and events:
            mine = [events.pop(0) for _ in range(min(count, len(events)))]
            pl.when(turn == t)(lambda mine=mine: [f() for f in mine] and None)


def offset_of(turn):
    return jnp.where(turn == 0, 2, jnp.where(turn == 1, 1, jnp.where(turn == 2, 3, 0)))


def interleave(events, count):
    for _ in range(min(count, len(events))):
        events.pop(0)()


def gather_events(routes, base, own, wide, where, rings, sibling, sems, started):
    y, z, core = where
    send, recv, core_send, core_recv = sems
    shared = []

    def place(route, a, b, c):
        dy, dz = (a, b) if routes[route][0] == "yz" else (b, a)
        return block_of((y + dy) % 4, (z + dz) % 4, c)

    def source(k, route, a, b):
        return own[k] if a == 0 and b == 0 else wide[k].at[place(route, a, b, core)]

    def push(route, i, a, b, who, sem):
        for j, (k, first, cols) in enumerate(routes[route][1][i]):
            view = pl.ds(first, cols)

            def make(k=k, view=view, n=sem + j):
                at = place(route, a, b, core)
                return remote(source(k, route, a, b).at[:, view], wide[k].at[at, :, view], send.at[n], recv.at[n], who)

            launch(started, make)

    def arrive(route, i, a, b, sem):
        for j, (k, first, cols) in enumerate(routes[route][1][i]):
            view = wide[k].at[place(route, a, b, core), :, pl.ds(first, cols)]
            remote(view, view, send.at[sem + j], recv.at[sem + j], sibling).wait_recv()

    def share(route, a, b):
        for k, first, cols in whole_of(routes[route]):
            n, view = base // 60 * 32 + len(shared), pl.ds(first, cols)

            def make(k=k, view=view, n=n):
                at = place(route, a, b, core)
                src = source(k, route, a, b).at[:, view]
                return remote(src, wide[k].at[at, :, view], core_send.at[n], core_recv.at[n], sibling)

            launch(started, make)
            shared.append((n, route, a, b, k, view))

    def slot(route, group, kind, i):
        return base + (route * 5 + group) * 6 + kind * 2 + i

    def axis(route, group):
        return rings[routes[route][0][0 if group == 0 else 1]]

    def begin(route, group, a, b):
        for turn in BOTH:
            for i in BOTH:
                push(route, i, a, b, axis(route, group)[turn], slot(route, group, turn, i))

    def onward(route, group, turn, a, b):
        for i in BOTH:
            arrive(route, i, a, b, slot(route, group, turn, i))
        push(route, turn, a, b, axis(route, group)[turn], slot(route, group, 2, turn))

    def finish(route, group, a, b):
        for i in BOTH:
            arrive(route, i, a, b, slot(route, group, 2, i))

    events = []

    def event(*steps):
        events.append(lambda: [f(*args) for f, *args in steps])

    event(*[(begin, r, 0, 0, 0) for r in BOTH])
    event(*[(begin, r, 1, 0, 0) for r in BOTH], *[(share, r, 0, 0) for r in BOTH])
    for turn, a in ((0, 3), (1, 1)):
        for r in BOTH:
            event((onward, r, 0, turn, a, 0), (begin, r, 1 + a, a, 0), (share, r, a, 0))
    for turn, b in ((0, 3), (1, 1)):
        for r in BOTH:
            event((onward, r, 1, turn, 0, b), (share, r, 0, b))
    for r in BOTH:
        event((finish, r, 0, 2, 0), (begin, r, 3, 2, 0), (share, r, 2, 0))
    for a in (3, 1):
        for turn, b in ((0, 3), (1, 1)):
            for r in BOTH:
                event((onward, r, 1 + a, turn, a, b), (share, r, a, b))
    for r in BOTH:
        event((finish, r, 1, 0, 2), (share, r, 0, 2))
    for turn, b in ((0, 3), (1, 1)):
        for r in BOTH:
            event((onward, r, 3, turn, 2, b), (share, r, 2, b))
    for a in (3, 1, 2):
        for r in BOTH:
            event((finish, r, 1 + a, a, 2), (share, r, a, 2))

    def settle():
        for n, route, a, b, k, view in shared:
            got = wide[k].at[place(route, a, b, 1 - core), :, view]
            remote(got, got, core_send.at[n], core_recv.at[n], sibling).wait_recv()

    events.append(settle)
    return events


def normalize(v):
    centered = v - jnp.mean(v, axis=-1, keepdims=True)
    factor = lax.rsqrt(jnp.mean(centered * centered, axis=-1, keepdims=True) + EPS)
    return centered * factor, factor


def norm_back(grad, normed, factor, gain):
    scaled = grad * gain
    inner = jnp.mean(scaled * normed, axis=-1, keepdims=True)
    return factor * (scaled - jnp.mean(scaled, axis=-1, keepdims=True) - normed * inner)


def columns(v):
    return jnp.sum(v, axis=0, keepdims=True)


def as_columns(rows):
    wide = [jnp.zeros((128 - len(rows), D), F32)]
    return jnp.concatenate(rows + wide, axis=0).T.astype(BF)


def eye(rows, cols):
    i = lax.broadcasted_iota(jnp.int32, (rows, cols), 0)
    j = lax.broadcasted_iota(jnp.int32, (rows, cols), 1)
    return jnp.where(i == j, 1.0, 0.0).astype(BF)


def pack_slabs(qkv_w, out_w, up_w, down_w, vectors, slabs):
    s0, s1, s2 = slabs
    spread = eye(16, 6)
    i = lax.broadcasted_iota(jnp.int32, (16, 6), 0)
    j = lax.broadcasted_iota(jnp.int32, (16, 6), 1)
    below = jnp.where(i == j + 8, 1.0, 0.0).astype(BF)
    rows = dot(spread, qkv_w[...])
    lane = lax.broadcasted_iota(jnp.int32, (16, 128), 1)
    row = lax.broadcasted_iota(jnp.int32, (16, 128), 0)
    flat = jnp.broadcast_to(vectors[...].astype(F32), (16, 128))
    i = lax.broadcasted_iota(jnp.int32, (128, 128), 0)
    j = lax.broadcasted_iota(jnp.int32, (128, 128), 1)

    def place(base, picks):
        r = row - base
        mine = ((lane < 48) & (lane % 6 == r) & (r >= 0) & (r < 6)) | ((lane >= 48) & (lane < 72) & ((lane - 48) // 4 == r))
        return dot(jnp.where(mine, flat, 0.0).astype(BF), jnp.where(picks, 1.0, 0.0).astype(BF))

    biases = place(0, (i // 6 == j) & (j < 2)).astype(BF)
    for g in range(4):
        q, k, v = (rows[:, n * D + g * 192 : n * D + g * 192 + 192] for n in range(3))
        s0[g, :, 0:640] = jnp.concatenate(
            [q, jnp.zeros((16, 64), F32), k[:, 0:128], v[:, 0:128], k[:, 128:192], v[:, 128:192]], axis=1
        ).astype(BF)
        s0[g, :, 640:768] = biases
    s1[:, 0:D] = (dot(spread, out_w[...]) + dot(below, up_w[:, 1280:2048])).astype(BF)
    s1[:, D:1792] = (dot(spread, up_w[:, 0:1024]) + dot(below, up_w[:, 2048:3072])).astype(BF)
    rest = place(8, ((i < 48) & (i // 6 == j + 2) & (j < 6)) | ((i >= 48) & (j == 8 + i % 4)))
    s1[:, 1792:1920] = (dot(spread, up_w[:, 1024:1152]) + rest).astype(BF)
    s1[:, 1920:2048] = dot(spread, up_w[:, 1152:1280]).astype(BF)
    s2[...] = dot(eye(32, 24), down_w[...]).astype(BF)


def forward_kernel(
    lengths, table, qkv_w, out_w, up_w, down_w, vectors, tokens, cotangent,
    result_out, dz1_out, w0, q_out, kv_out, o_out, lse_out, do_out, g1, g2, group_tokens,
    result, dz1_ref, q_land, kv_land, o_slab, lse_ref, do_land,
    s0, s1, s2, x0, x1, x2, own0, own1, own2, land0, land1, land2, words, o_land, do_slab, part_out, part_stat,
    ext, act, slope, grad1, grad2,
    x_send, x_recv, put_sem, send, recv, core_send, core_recv, e_send, e_recv, e_core_send, e_core_recv, t_send, t_recv,
    o_send, o_recv, d_send, d_recv, keep_sem,
):
    x, y, z, core = coords()
    side = z % 2
    slabs, arrived, own, wide = (s0, s1, s2), (x0, x1, x2), (own0, own1, own2), (land0, land1, land2)
    peers, rings, sibling = neighbours(x, y, z, core)
    partner = ident(x, y, z + 1 - 2 * side, core)
    places = plane(x, y, z, core)
    pack_slabs(qkv_w, out_w, up_w, down_w, vectors, slabs)
    greet(peers + list(places.values()) + [sibling])
    started, x_copies = [], {}

    def token_send(src, at, who, n, part=slice(None)):
        launch(started, lambda: remote(src.at[part], words.at[at].at[part], t_send.at[n], t_recv.at[n], who))

    def token_wait(at, n, part=slice(None)):
        view = words.at[at].at[part]
        remote(view, view, t_send.at[n], t_recv.at[n], sibling).wait_recv()

    right, left = peers[0], peers[2]
    halves = (pl.ds(0, T // 2), pl.ds(T // 2, T // 2))

    def line_tokens(src, which, n):
        token_send(src, which * 4 + x, right, n)
        token_send(src, which * 4 + x, left, n + 1)

    def line_onward(which, n):
        before, after = which * 4 + (x + 3) % 4, which * 4 + (x + 1) % 4
        token_wait(before, n)
        token_send(words.at[before], before, right, n + 2, halves[0])
        token_wait(after, n + 1)
        token_send(words.at[after], after, left, n + 3, halves[1])

    def line_finish(which, n):
        for i in BOTH:
            token_wait(which * 4 + (x + 2) % 4, n + 2 + i, halves[i])

    mine = side * 4 + x
    beyond = (1 - side) * 4 + x

    def send_slab(k):
        for d in (1, 3, 2):
            src = slabs[0].at[(x + d) % 4] if k == 0 else slabs[k]
            c = remote(src, arrived[k].at[d - 1], x_send.at[d - 1, k], x_recv.at[d - 1, k], peers[d - 1])
            c.start()
            x_copies[k, d] = c
            started.append(lambda c=c: c)

    for k in range(3):
        send_slab(k)
    token_send(tokens, mine, partner, 0)
    words[mine] = tokens[...]
    me = block_of(y, z, core)
    puts = [pltpu.make_async_copy(own[k], wide[k].at[me], put_sem.at[k]) for k in range(3)]

    def line(k):
        rows = ROWS[k]
        for d in (1, 3, 2):
            x_copies[k, d].wait_recv()
        shape = (4 * rows, SLAB[k][0])
        for base, first, cols in ((0, 0, 2048), (8, 2048, 1920)) if k == 1 else ((0, 0, D),):
            total = jnp.zeros((4 * rows, cols), F32)
            for d in range(4):
                slab = arrived[k][d - 1, :, 0:cols] if d else slabs[0][x] if k == 0 else slabs[k][:, 0:cols]
                total += dot(picker(shape, rows, (x + 4 - d) % 4, False, base), slab)
            own[k][:, first : first + cols] = total.astype(BF)
        puts[k].start()

    sems = (send, recv, core_send, core_recv)
    mid, late = (
        gather_events(routes, 60 * n, own, wide, (y, z, core), rings, sibling, sems, started)
        for n, routes in enumerate((MID, LATE))
    )

    def share_first(n, src, at):
        launch(started, lambda: remote(src, land0.at[at], e_core_send.at[n], e_core_recv.at[n], sibling))

    line(0)
    for n, who in places.items():
        launch(started, lambda n=n, who=who: remote(own0, land0.at[me], e_send.at[n], e_recv.at[n], who))
    share_first(0, own0, me)
    line_tokens(tokens, side, 1)
    line(1)
    interleave(mid, 2)
    line(2)
    interleave(late, 2)
    for n in places:
        at = block_of((y + 4 - n // 4) % 4, (z + 4 - n % 4) % 4, core)
        view = land0.at[at]
        remote(view, view, e_send.at[n], e_recv.at[n], sibling).wait_recv()
        share_first(n, view, at)
    interleave(mid, 2)
    for n in range(16):
        view = land0.at[block_of((y + 4 - n // 4) % 4, (z + 4 - n % 4) % 4, 1 - core)]
        remote(view, view, e_core_send.at[n], e_core_recv.at[n], sibling).wait_recv()
    puts[0].wait()
    kept = [pltpu.make_async_copy(land0, w0, keep_sem.at[0])]
    kept[0].start()

    weight = land0[...].reshape(D, D)
    biases = weight[:, 640:].astype(F32).T
    query_bias = key_bias = jnp.zeros((1, 192), F32)
    for g in range(4):
        here = slice(g * 192, g * 192 + 192)
        query_bias = jnp.where(x == g, biases[0:1, here], query_bias)
        key_bias = jnp.where(x == g, biases[1:2, here], key_bias)
    none = jnp.zeros((1, 64), F32)
    query_bias = jnp.concatenate([query_bias, none], axis=1)
    key_bias = jnp.concatenate([none, none, key_bias[:, :128], none, key_bias[:, 128:]], axis=1)

    def project(at, with_query):
        if with_query:
            both = dot(words[at], weight[:, 0:640])
            q_land[at % 4] = ((both[:, :256] + query_bias).astype(BF).astype(F32) * 0.125).astype(BF)
            kv_land[at] = (both[:, 256:] + key_bias).astype(BF)
        else:
            kv_land[at] = (dot(words[at], weight[:, 256:640]) + key_bias).astype(BF)

    project(mine, True)
    interleave(mid, 2)
    line_onward(side, 1)
    token_wait(beyond, 0)
    line_tokens(words.at[beyond], 1 - side, 5)
    project(side * 4 + (x + 3) % 4, True)
    project(side * 4 + (x + 1) % 4, True)
    interleave(mid, 6)
    interleave(late, 4)
    project(beyond, False)
    line_finish(side, 1)
    project(side * 4 + (x + 2) % 4, True)

    def keep(src, dst):
        c = pltpu.make_async_copy(src, dst, keep_sem.at[len(kept)])
        c.start()
        kept.append(c)

    keep(q_land, q_out)
    copies = []

    def deliver(src, landing, to_slot, from_slot, ss, rr, who):
        launch(started, lambda: remote(src, landing.at[to_slot], ss, rr, who))
        copies.append((landing.at[from_slot], ss, rr))

    first = head_lanes(0)
    lane = lax.broadcasted_iota(jnp.int32, (1, 128), 1)

    def attend(part, which, events, events_plan):
        key_seg = jnp.concatenate(
            [jnp.full((1, 128), seg_of(lengths, table, which * 8 + j), jnp.int32) for j in range(8)], axis=1
        )
        plans = [events_plan[h::3] for h in range(3)]

        def chunk(turn, carry):
            d = offset_of(turn)
            to = (x + d) % 4
            block = (side * 4 + to) * 2
            query_seg = jnp.concatenate([jnp.full((128, 1), seg_of(lengths, table, block + i), jnp.int32) for i in BOTH], axis=0)
            allowed = query_seg == key_seg
            outs, stats = [], []
            for h in range(3):
                planned(by_head[h], turn, plans[h])
                tile = h // 2 * 128
                q = jnp.where(head_lanes(h), q_land[to, :, tile : tile + 128].astype(F32), 0.0).astype(BF)
                k, v = key_value(kv_land[pl.ds(which * 4, 4)], h)
                s = jnp.where(allowed, dot_t(q, k), -1e30)
                top = jnp.max(s, axis=1, keepdims=True)
                e = jnp.exp(s - top)
                total = jnp.sum(e, axis=1, keepdims=True)
                out = dot(e.astype(BF), v)
                if part == 0:
                    part_out[to, h] = out
                    stats += [top, total]
                else:
                    top_was, total_was = part_stat[to, :, 2 * h : 2 * h + 1], part_stat[to, :, 2 * h + 1 : 2 * h + 2]
                    highest = jnp.maximum(top, top_was)
                    now, was = jnp.exp(top - highest), jnp.exp(top_was - highest)
                    total = total * now + total_was * was
                    outs.append((out * now + part_out[to, h] * was) / total)
                    stats.append(highest + jnp.log(total))
            table_of = jnp.zeros((T, 128), F32)
            for i, v in enumerate(stats):
                table_of = jnp.where(lane == i, v, table_of)
            if part == 0:
                part_stat[to] = table_of
                return carry
            lse_ref[to] = table_of
            o_slab[to, :, 0:128] = jnp.where(first, outs[0], outs[1]).astype(BF)
            o_slab[to, :, 128:256] = jnp.where(first, 0.0, outs[2]).astype(BF)

            @pl.when(turn < 3)
            def _():
                who = ident(to, y, z, core)
                remote(o_slab.at[to], o_land.at[x], o_send.at[d], o_recv.at[d], who).start()

            return carry

        by_head = [[], [], []]
        for n, count in enumerate(events_plan):
            for _ in range(min(count, len(events))):
                by_head[n % 3].append(events.pop(0))
        lax.fori_loop(0, 4, chunk, 0)
        if part:
            o_land[x] = o_slab[x]
            for d in (2, 1, 3):
                to, fro = (x + d) % 4, (x + 4 - d) % 4
                started.append(lambda d=d, to=to: remote(o_slab.at[to], o_land.at[x], o_send.at[d], o_recv.at[d], peers[d - 1]))
                copies.append((o_land.at[fro], o_send.at[d], o_recv.at[d]))

    attend(0, side, mid, (1,) * 12)
    line_onward(1 - side, 5)
    project((1 - side) * 4 + (x + 3) % 4, False)
    project((1 - side) * 4 + (x + 1) % 4, False)
    interleave(mid, 100)
    interleave(late, 8)
    line_finish(1 - side, 5)
    project((1 - side) * 4 + (x + 2) % 4, False)
    keep(kv_land, kv_out)
    keep(words, group_tokens)
    attend(1, 1 - side, late, (1,) * 12)
    keep(o_slab, o_out)
    keep(lse_ref, lse_out)
    puts[1].wait()
    puts[2].wait()

    vecs = land1[:, :, 3840:].reshape(D, 128).astype(F32).T
    out_bias, gain_one, shift_one, down_bias, gain_two, shift_two = (vecs[i : i + 1] for i in range(6))
    i = lax.broadcasted_iota(jnp.int32, (192, D), 0)
    j = lax.broadcasted_iota(jnp.int32, (192, D), 1)
    stretch = jnp.where(i == j // 4, 1.0, 0.0).astype(BF)
    i = lax.broadcasted_iota(jnp.int32, (8, D), 0)
    j = lax.broadcasted_iota(jnp.int32, (8, D), 1)
    four = vecs[8:16].astype(BF)
    up_biases = [columns(jnp.where(i == j % 4, dot(four[:, n * 192 : n * 192 + 192], stretch), 0.0)) for n in range(4)]
    interleave(late, 100)
    for g in range(4):
        part = land1[g * 8 : g * 8 + 8, :, 0:D].reshape(192, D)
        ext[g, 0:128] = part[0:128]
        ext[g, 128:192] = jnp.zeros((64, D), BF)
        ext[g, 192:256] = part[128:192]
    for got, ss, rr in copies:
        remote(got, got, ss, rr, sibling).wait_recv()
    copies.clear()
    branch = dot(o_land[0], ext[0])
    for g in range(1, 4):
        branch += dot(o_land[g], ext[g])
    normed_one, factor_one = normalize(tokens[...].astype(F32) + (branch + out_bias))
    hidden = normed_one * gain_one + shift_one
    low = hidden.astype(BF)
    for n in range(4):
        up = land1[:, :, D + n * D : 2 * D + n * D].reshape(D, D)
        upper = dot(low, up) + up_biases[n]
        square = upper * upper
        t = jnp.tanh(0.7978845608028654 * (upper + 0.044715 * (square * upper)))
        half = 0.5 * (1.0 + t)
        slope[n] = half + 0.5 * upper * (1.0 - t * t) * (0.7978845608028654 * (1.0 + 3.0 * 0.044715 * square))
        act[n] = (upper * half).astype(BF)
    feed = jnp.zeros((T, D), F32)
    for n in range(4):
        feed += dot(act[n], land2[n * 8 : n * 8 + 8].reshape(D, D))
    normed_two, factor_two = normalize(hidden + (feed + down_bias))
    result[...] = (normed_two * gain_two + shift_two).astype(BF)
    keep(result, result_out)

    grad = cotangent[...].astype(F32)
    dz2 = norm_back(grad, normed_two, factor_two, gain_two)
    gain_two_grad, shift_two_grad = columns(grad * normed_two), columns(grad)
    dfeed = dz2.astype(BF)
    down_bias_grad = columns(dfeed.astype(F32))
    dhidden = dz2

    for n in range(4):
        up = land1[:, :, D + n * D : 2 * D + n * D].reshape(D, D)
        down = land2[n * 8 : n * 8 + 8].reshape(D, D)
        dupper = (dot_t(dfeed, down) * slope[n]).astype(BF)
        rows, cols = slice(n * 8, n * 8 + 8), slice(D + n * D, 2 * D + n * D)
        grad2[rows, :, :D] = dot_rows(act[n], dfeed).astype(BF).reshape(8, 96, D)
        grad2[rows, :, D:] = as_columns([columns(dupper.astype(F32))]).reshape(8, 96, 128)
        keep(grad2.at[pl.ds(n * 8, 8)], g2.at[pl.ds(n * 8, 8)])
        grad1[:, :, cols] = dot_rows(low, dupper).astype(BF).reshape(32, 24, D)
        keep(grad1.at[:, :, pl.ds(D + n * D, D)], g1.at[:, :, pl.ds(D + n * D, D)])
        dhidden += dot_t(dupper, up)
    dz1 = norm_back(dhidden, normed_one, factor_one, gain_one)
    dz1_ref[...] = dz1
    keep(dz1_ref, dz1_out)
    dbranch = dz1.astype(BF)
    for d in TURNS:
        to = (x + d) % 4
        do_slab[to] = dot_t(dbranch, ext[to]).astype(BF)
        if d:
            deliver(do_slab.at[to], do_land, x, (x + 4 - d) % 4, d_send.at[d], d_recv.at[d], peers[d - 1])
        else:
            do_land[x] = do_slab[x]
    for g in range(4):
        part = dot_rows(o_land[g], dbranch).astype(BF)
        grad1[g * 8 : g * 8 + 8, :, 0:D] = jnp.concatenate([part[0:128], part[192:256]], axis=0).reshape(8, 24, D)
    grad1[:, :, 3840:] = as_columns(
        [columns(dbranch.astype(F32)), columns(dhidden * normed_one), columns(dhidden),
         down_bias_grad, gain_two_grad, shift_two_grad]
    ).reshape(32, 24, 128)
    keep(grad1.at[:, :, pl.ds(0, D)], g1.at[:, :, pl.ds(0, D)])
    keep(grad1.at[:, :, pl.ds(3840, 128)], g1.at[:, :, pl.ds(3840, 128)])
    for got, ss, rr in copies:
        remote(got, got, ss, rr, sibling).wait_recv()
    keep(do_land, do_out)
    for make in started:
        make().wait_send()
    for c in kept:
        c.wait()


def forward(*args):
    slab = (4, T, 256)
    return pl.pallas_call(
        forward_kernel,
        out_shape=(
            struct((T, D), BF), struct((T, D), F32), struct((32,) + WIDE[0], BF), struct(slab, BF), struct((8, T, 384), BF),
            struct(slab, BF), struct((4, T, 128), F32), struct(slab, BF),
            struct((32,) + SUMS[1], BF), struct((32,) + SUMS[2], BF), struct((8, T, D), BF),
        ),
        in_specs=[SM] * 2 + [VM] * 7,
        out_specs=(ANY,) * 11,
        scratch_shapes=[pltpu.VMEM((T, D), BF), pltpu.VMEM((T, D), F32), pltpu.VMEM(slab, BF), pltpu.VMEM((8, T, 384), BF)]
        + [pltpu.VMEM(slab, BF), pltpu.VMEM((4, T, 128), F32), pltpu.VMEM(slab, BF)]
        + [pltpu.VMEM((4,) + SLAB[0], BF)] + [pltpu.VMEM(t, BF) for t in SLAB[1:]]
        + [pltpu.VMEM((3,) + t, BF) for t in SLAB]
        + [pltpu.VMEM(w, BF) for w in WIDE]
        + [pltpu.VMEM((32,) + w, BF) for w in WIDE]
        + [pltpu.VMEM((8, T, D), BF), pltpu.VMEM(slab, BF), pltpu.VMEM(slab, BF)]
        + [pltpu.VMEM((4, 3, T, 128), F32), pltpu.VMEM((4, T, 128), F32)]
        + [pltpu.VMEM((4, 256, D), BF), pltpu.VMEM((4, T, D), BF), pltpu.VMEM((4, T, D), F32)]
        + [pltpu.VMEM((32,) + w, BF) for w in SUMS[1:]]
        + [DMA((3, 3)), DMA((3, 3)), DMA((3,)), DMA((120,)), DMA((120,)), DMA((64,)), DMA((64,))]
        + [DMA((16,))] * 4
        + [DMA((9,)), DMA((9,)), DMA((4,)), DMA((4,)), DMA((4,)), DMA((4,)), DMA((24,))],
        compiler_params=pltpu.CompilerParams(collective_id=0, has_side_effects=True, vmem_limit_bytes=62 << 20),
        name="forward",
    )(*args)


def scatter_events(routes, grads, acc, fro, buf, where, rings, sibling, sems, started):
    y, z, core = where
    load_sem, core_send, core_recv, send, recv = sems
    moves, waited = {}, set()

    def spot(route, a, b):
        dy, dz = (a, b) if routes[route][0] == "yz" else (b, a)
        return dy, dz, dy * 4 + dz

    def begin():
        for r, a, b in [(r, a, b) for b in TURNS for a in TURNS for r in BOTH]:
            dy, dz, at = spot(r, a, b)
            if at in moves:
                continue
            here = block_of((y + dy) % 4, (z + dz) % 4, core)
            there = block_of((y + dy) % 4, (z + dz) % 4, 1 - core)
            moves[at] = []
            for k in (1, 2):
                n = at * 2 + k - 1
                swap = remote(grads[k].at[there], fro[k].at[at], core_send.at[n], core_recv.at[n], sibling)
                load = pltpu.make_async_copy(grads[k].at[here], acc[k].at[at], load_sem.at[n])
                swap.start()
                load.start()
                started.append(lambda swap=swap: swap)
                moves[at].append((load, swap))

    def folding(r, a, b):
        at = spot(r, a, b)[2]
        fresh = at not in waited
        waited.add(at)
        return fold, r, a, b, fresh

    def fold(r, a, b, fresh):
        _, _, at = spot(r, a, b)
        if fresh:
            for load, swap in moves[at]:
                load.wait()
                swap.wait_recv()
        for k, first, cols in chunks_of(routes[r]):
            view = (at, slice(None), pl.ds(first, cols))
            acc[k][view] = acc[k][view] + fro[k][view]

    def slot(r, group, kind, i):
        return (r * 5 + group) * 9 + kind * 3 + (len(routes[r][1][0]) if i else 0)

    def axis(r, group):
        return rings[routes[r][0][0 if group == 0 else 1]]

    def at_of(r, group, step):
        return spot(r, *((step, 0) if group == 0 else (group - 1, step)))[2]

    def push(r, group, kind, i, step, who):
        for j, (k, first, cols) in enumerate(routes[r][1][i]):
            n, view = slot(r, group, kind, i) + j, pl.ds(first, cols)

            def make(k=k, n=n, view=view):
                src = acc[k].at[at_of(r, group, step), :, view]
                return remote(src, buf[k].at[group * 3 + kind, :, view], send.at[n], recv.at[n], who)

            launch(started, make)

    def add(r, group, kind, i, step):
        for j, (k, first, cols) in enumerate(routes[r][1][i]):
            n, view = slot(r, group, kind, i) + j, pl.ds(first, cols)
            got = buf[k].at[group * 3 + kind, :, view]
            remote(got, got, send.at[n], recv.at[n], sibling).wait_recv()
            at = (at_of(r, group, step), slice(None), view)
            acc[k][at] = acc[k][at] + buf[k][group * 3 + kind, :, view]

    def one(r, group):
        right, left = axis(r, group)
        push(r, group, 0, 0, 2, right)
        push(r, group, 0, 1, 2, left)

    def two(r, group):
        right, left = axis(r, group)
        add(r, group, 0, 0, 1)
        push(r, group, 1, 0, 1, right)
        push(r, group, 1, 1, 1, right)
        add(r, group, 0, 1, 3)
        push(r, group, 2, 0, 3, left)
        push(r, group, 2, 1, 3, left)

    def three(r, group):
        for kind in (1, 2):
            for i in BOTH:
                add(r, group, kind, i, 0)

    events = []

    def event(*steps):
        events.append(lambda: [f(*args) for f, *args in steps])

    for a in TURNS:
        for r in BOTH:
            event(folding(r, a, 2), (one, r, 1 + a))
    for a in TURNS:
        for r in BOTH:
            event(folding(r, a, 1), folding(r, a, 3), (two, r, 1 + a))
    for a in TURNS:
        for r in BOTH:
            more = {2: [(one, r, 0)], 3: [(two, r, 0)]}.get(a, [])
            event(folding(r, a, 0), (three, r, 1 + a), *more)
    for r in BOTH:
        event((three, r, 0))
    return begin, events


def backward_kernel(
    lengths, table, q_in, kv_in, do_in, o_in, lse_in, dz1_in, group_tokens, w0, g1, g2, dx_ref, o0, o1, o2,
    q_ref, kv_ref, do_ref, o_ref, lse_ref, dz1, wa, words, g0, a0, a1, a2, c0, c1, c2, b0, b1, b2, xs0, xs1, xs2, xr0, xr1, xr2, dx_slab, dx_land, kv_slab, kv_land,
    total, q_total, grads_low,
    load_sem, core_send, core_recv, send, recv, e_send, e_recv, e_core_send, e_core_recv, x_send, x_recv, dx_send, dx_recv, kv_send, kv_recv, w_sem,
):
    x, y, z, core = coords()
    side = z % 2
    mine = side * 4 + x
    grads, outs, acc, fro, buf = (g0, g1, g2), (o0, o1, o2), (a0, a1, a2), (c0, c1, c2), (b0, b1, b2)
    out_slabs, in_slabs = (xs0, xs1, xs2), (xr0, xr1, xr2)
    peers, rings, sibling = neighbours(x, y, z, core)
    partner = ident(x, y, z + 1 - 2 * side, core)
    first_in, fetch = [], []
    for src, dst, cuts in (
        (q_in, q_ref, (0, 128, 256)), (kv_in, kv_ref, (0, 128, 256, 384)), (do_in, do_ref, (0, 128, 256)),
        (o_in, o_ref, (0, 128, 256)), (lse_in, lse_ref, (0, 128)),
    ):
        for at, end in zip(cuts, cuts[1:]):
            view = pl.ds(at, end - at)
            first_in.append(pltpu.make_async_copy(src.at[:, :, view], dst.at[:, :, view], w_sem.at[len(first_in)]))
            first_in[-1].start()
    places = plane(x, y, z, core)
    greet(peers + list(places.values()) + [sibling])
    started, copies = [], []
    sems = (load_sem, core_send, core_recv, send, recv)
    begin_late, late = scatter_events(BACK_LATE, grads, acc, fro, buf, (y, z, core), rings, sibling, sems, started)
    begin_late()
    for n, (src, dst) in enumerate(((w0, wa), (group_tokens, words), (dz1_in, dz1))):
        fetch.append(pltpu.make_async_copy(src, dst, w_sem.at[len(first_in) + n]))
        fetch[-1].start()
    for c in first_in:
        c.wait()

    def deliver(src, landing, to_slot, from_slot, ss, rr, who):
        launch(started, lambda: remote(src, landing.at[to_slot], ss, rr, who))
        copies.append((landing.at[from_slot], ss, rr))

    first = head_lanes(0)
    swap = remote(kv_slab, kv_land, kv_send.at[0], kv_recv.at[0], partner)
    for part, which in enumerate((1 - side, side)):
        key_seg = jnp.concatenate([jnp.full((128, 1), seg_of(lengths, table, which * 8 + j), jnp.int32) for j in range(8)], axis=0)
        plan = BACK_PLAN[part * 12 : part * 12 + 12]
        plans = [plan[h::3] for h in range(3)]
        by_head = [[], [], []]
        for n, count in enumerate(plan):
            for _ in range(min(count, len(late))):
                by_head[n % 3].append(late.pop(0))
        total[...] = jnp.zeros_like(total)

        def chunk(turn, carry):
            to = (x + offset_of(turn)) % 4
            block = (side * 4 + to) * 2
            query_seg = jnp.concatenate([jnp.full((1, 128), seg_of(lengths, table, block + i), jnp.int32) for i in BOTH], axis=1)
            allowed = key_seg == query_seg
            logs = lse_ref[to].T
            parts = []
            for h in range(3):
                planned(by_head[h], turn, plans[h])
                tile = h // 2 * 128
                cols = slice(tile, tile + 128)
                lanes = head_lanes(h)
                out_lanes = lanes if h < 2 else jnp.logical_not(lanes)
                q = jnp.where(lanes, q_ref[to, :, cols].astype(F32), 0.0).astype(BF)
                do = jnp.where(out_lanes, do_ref[to, :, cols].astype(F32), 0.0)
                inner = jnp.sum(do * o_ref[to, :, cols].astype(F32), axis=1, keepdims=True)
                inner = jnp.broadcast_to(inner, (T, 128)).T[0:1]
                do = do.astype(BF)
                k, v = key_value(kv_ref[pl.ds(which * 4, 4)], h)
                p = jnp.where(allowed, jnp.exp(dot_t(k, q) - logs[h : h + 1]), 0.0)
                ds = (p * (dot_t(v, do) - inner)).astype(BF)
                dk, dv = dot(ds, q), dot(p.astype(BF), do)
                if h < 2:
                    total[:, 0:128] += dk
                    total[:, 128:256] += dv
                else:
                    total[:, 256:384] += dk + dv
                parts.append(dot_rows(ds, k) * 0.125)
            for at, piece in (
                (slice(0, 128), jnp.where(first, parts[0], parts[1])), (slice(128, 256), jnp.where(first, parts[2], 0.0)),
            ):
                if part == 0:
                    q_total[to, :, at] = piece
                else:
                    grads_low[to, :, at] = (q_total[to, :, at] + piece).astype(BF)
            return carry

        lax.fori_loop(0, 4, chunk, 0)
        if part == 0:
            kv_slab[...] = total[...].astype(BF).reshape(4, T, 384)
            swap.start()
            started.append(lambda: swap)
    for c in fetch:
        c.wait()
    own_part = total[...].astype(BF)
    for at, piece in (
        (slice(0, 256), dot_rows(words[pl.ds(side * 4, 4)].reshape(4 * T, D), grads_low[:, :, 0:256].reshape(4 * T, 256))),
        (slice(256, 640), dot_rows(words[pl.ds(side * 4, 4)].reshape(4 * T, D), own_part)
         + dot_rows(words[pl.ds(4 - side * 4, 4)].reshape(4 * T, D), kv_slab[...].reshape(4 * T, 384))),
    ):
        g0[:, :, at] = piece.astype(BF).reshape(32, 24, at.stop - at.start)
    q_sums = columns(grads_low[:, :, 0:256].reshape(4 * T, 256).astype(F32))
    kv_sums = columns(own_part.astype(F32)) + columns(kv_slab[...].reshape(4 * T, 384).astype(F32))
    bias = (q_sums[:, 0:192], jnp.concatenate([kv_sums[:, 128:256], kv_sums[:, 320:384]], axis=1))
    bias = [jnp.concatenate([jnp.where(x == g, b, 0.0) for g in range(4)], axis=1) for b in bias]
    g0[:, :, 640:] = as_columns(bias).reshape(32, 24, 128)
    folds = {}
    for n in list(places) + [0]:
        there = block_of((y + n // 4) % 4, (z + n % 4) % 4, 1 - core)
        folds[n] = remote(g0.at[there], c0.at[n], e_core_send.at[n], e_core_recv.at[n], sibling)
        folds[n].start()
        started.append(lambda n=n: folds[n])
    interleave(late, 2)
    for n in list(places) + [0]:
        folds[n].wait_recv()
        a0[n] = g0[block_of((y + n // 4) % 4, (z + n % 4) % 4, core)] + c0[n]
        if n:
            launch(started, lambda n=n: remote(a0.at[n], b0.at[n], e_send.at[n], e_recv.at[n], places[n]))
    interleave(late, LATE_BEFORE_SHARE)
    swap.wait_recv()
    for g in range(4):
        grads_low[g, :, 256:] = (total[g * T : g * T + T] + kv_land[g].astype(F32)).astype(BF)
    weight = wa[:, :, 0:640].reshape(D, 640)
    for d in TURNS:
        to = (x + d) % 4
        share = dot_t(grads_low[to], weight)
        if d:
            dx_slab[to] = share.astype(BF)
            deliver(dx_slab.at[to], dx_land, x, (x + 4 - d) % 4, dx_send.at[d], dx_recv.at[d], peers[d - 1])
        else:
            dx_ref[...] = dz1[...] + share

    def line_out(k):
        rows = ROWS[k]
        shape = (SUM_SLAB[k][0], 4 * rows)

        def slab(at):
            if k != 1:
                return dot(picker(shape, rows, at, True), acc[k][0])
            upper, lower = picker(shape, rows, at, True), picker(shape, rows, at, True, 8)
            rest = jnp.concatenate([acc[1][0, :, 2048:NB], jnp.zeros((24, 128), BF)], axis=1)
            return dot(upper, acc[1][0, :, 0:2048]) + dot(lower, rest)

        for d in (2, 1, 3):
            out_slabs[k][d - 1] = slab((x + d) % 4).astype(BF)
            c = remote(out_slabs[k].at[d - 1], in_slabs[k].at[d - 1], x_send.at[d - 1, k], x_recv.at[d - 1, k], peers[d - 1])
            c.start()
            started.append(lambda c=c: c)
            x_copies[k].append(c)
        in_slabs[k][3] = slab(x).astype(BF)

    def gathered(k):
        for c in x_copies[k]:
            c.wait_recv()
        return [in_slabs[k][i].astype(F32) for i in range(4)]

    x_copies = {0: [], 1: [], 2: []}
    interleave(late, 100)
    line_out(1)
    line_out(2)
    first_sum = a0[0].astype(F32)
    for n in places:
        remote(b0.at[n], b0.at[n], e_send.at[n], e_recv.at[n], sibling).wait_recv()
        first_sum += b0[n].astype(F32)
    a0[0] = first_sum.astype(BF)
    line_out(0)
    one, two, three, four = gathered(1)
    both = one + two + three + four
    o1[:, 0:2048] = both[0:8]
    o1[:, 2048:NB] = both[8:16, 0:1920]
    one, two, three, four = gathered(2)
    o2[...] = (one + two + three + four)[0:24]
    for got, ss, rr in copies:
        remote(got, got, ss, rr, sibling).wait_recv()
    dx = dx_ref[...]
    for d in (1, 2, 3):
        dx += dx_land[(x + d) % 4].astype(F32)
    dx_ref[...] = dx
    gathered(0)
    groups = []
    for g in range(4):
        groups.append(xr0[(x - g + 3) % 4].astype(F32))
    groups = [v[0:8] for v in groups]
    o0[:, 0 : 3 * D] = jnp.concatenate(
        [v[:, 0:192] for v in groups]
        + [p for v in groups for p in (v[:, 256:384], v[:, 512:576])]
        + [p for v in groups for p in (v[:, 384:512], v[:, 576:640])], axis=1
    )
    o0[:, 3 * D :] = groups[0][:, 640:] + groups[1][:, 640:] + groups[2][:, 640:] + groups[3][:, 640:]
    for make in started:
        make().wait_send()


BACK_PLAN = (2, 2, 2, 2, 0, 1, 1, 1, 1, 1, 1, 1, 1, 0, 0, 0, 0, 1, 0, 1, 0, 1, 0, 1)
LATE_BEFORE_SHARE = 2


def backward(*args):
    return pl.pallas_call(
        backward_kernel,
        out_shape=(struct((T, D), F32), struct((8, 2432), F32), struct((8, NB), F32), struct((24, NC), F32)),
        in_specs=[SM] * 2 + [ANY] * 10,
        out_specs=(VM,) * 4,
        scratch_shapes=[pltpu.VMEM((4, T, 256), BF), pltpu.VMEM((8, T, 384), BF), pltpu.VMEM((4, T, 256), BF)]
        + [pltpu.VMEM((4, T, 256), BF), pltpu.VMEM((4, T, 128), F32), pltpu.VMEM((T, D), F32)]
        + [pltpu.VMEM((32,) + WIDE[0], BF), pltpu.VMEM((8, T, D), BF), pltpu.VMEM((32,) + WIDE[0], BF)]
        + [pltpu.VMEM((16,) + w, BF) for w in SUMS] * 2
        + [pltpu.VMEM((16,) + SUMS[0], BF)] + [pltpu.VMEM((15,) + w, BF) for w in SUMS[1:]]
        + [pltpu.VMEM((3,) + t, BF) for t in SUM_SLAB] + [pltpu.VMEM((4,) + t, BF) for t in SUM_SLAB]
        + [pltpu.VMEM((4, T, D), BF)] * 2 + [pltpu.VMEM((4, T, 384), BF)] * 2
        + [pltpu.VMEM((4 * T, 384), F32), pltpu.VMEM((4, T, 256), F32), pltpu.VMEM((4, T, 640), BF)]
        + [DMA((32,)), DMA((32,)), DMA((32,)), DMA((90,)), DMA((90,))] + [DMA((16,))] * 4 + [DMA((3, 3)), DMA((3, 3))]
        + [DMA((4,)), DMA((4,)), DMA((1,)), DMA((1,)), DMA((16,))],
        compiler_params=pltpu.CompilerParams(collective_id=1, has_side_effects=True, vmem_limit_bytes=62 << 20),
        name="backward",
    )(*args)


def unpack_kernel(o0, o1, o2, dx_in, low_in, low, dx, qkv, query, value, out, out_bias, gain_one, shift_one, up, up_bias,
                  down, down_bias, gain_two, shift_two):
    dx[...] = dx_in[...]
    low[...] = low_in[...]
    qkv[...] = o0[0:6, 0 : 3 * D]
    out[...] = o1[0:6, 0:D]
    up[...] = o1[0:6, D:3840]
    down[...] = o2[:, 0:D]
    first, second = o0[:, 3 * D :].T, o1[:, 3840:].T
    third = jnp.concatenate([o2[:, D:], jnp.zeros((104, 128), F32)], axis=0).T
    query[...], value[...] = first[0, 0:6], first[1, 0:6]
    for i, ref in enumerate((out_bias, gain_one, shift_one, down_bias, gain_two, shift_two)):
        ref[...] = second[i, 0:6]
    up_bias[...] = third[0, 0:24]


def unpack(*args):
    six = struct((6,), F32)
    return pl.pallas_call(
        unpack_kernel,
        out_shape=(
            struct((T, D), BF), struct((T, D), F32), struct((6, 3 * D), F32), six, six, struct((6, D), F32), six, six, six,
            struct((6, FF), F32), struct((24,), F32), struct((24, D), F32), six, six, six,
        ),
        in_specs=[VM] * 5,
        out_specs=(VM,) * 15,
        name="unpack",
    )(*args)


def shards(
    tokens, lengths, block_table, qkv_weight, query_bias, value_bias, out_weight, out_bias, first_gain, first_shift,
    up_weight, up_bias, down_weight, down_bias, second_gain, second_shift, cotangent,
):
    vectors = jnp.zeros((128,), BF)
    at = 0
    for v in (query_bias, value_bias, out_bias, first_gain, first_shift, down_bias, second_gain, second_shift, up_bias):
        vectors += jnp.pad(v, (at, 128 - at - v.shape[0]))
        at += v.shape[0]
    vectors = vectors[None, :]
    result, dz1, w0, q, kv, o, lse, do, g1, g2, words = forward(
        lengths, block_table, qkv_weight, out_weight, up_weight, down_weight, vectors, tokens, cotangent
    )
    dx, ga, gb, gc = backward(lengths, block_table, q, kv, do, o, lse, dz1, words, w0, g1, g2)
    return unpack(ga, gb, gc, dx, result)


def solution(mesh):
    both = ("fsdp", "seq")
    whole, flat, group = P(both, None), P(both), P("fsdp", None)
    return jax.shard_map(
        shards,
        mesh=mesh,
        in_specs=(whole, group, group, whole, flat, flat, whole, flat, flat, flat, whole, flat, whole, flat, flat, flat, whole),
        out_specs=(whole, whole, whole, flat, flat, whole, flat, flat, flat, whole, flat, whole, flat, flat, flat),
        check_vma=False,
    )
```
